32 devices in a mesh: groups: 2 (over y), dp: 4 (over z), layer: 4 (over x, core).
Axes of the slice: x: 2, y: 2, z: 4, core: 2. Of those that a mesh axis runs over, the one named last changes fastest.
Arguments:
- acts_in: bfloat16 [8, 2, 64, 4, 4096], P(('groups', 'dp'), None, None, 'layer'), parts along dimension 0, may hold values from -6 to 6
- grads_out: bfloat16 [8, 2, 64, 4, 4096], P(('groups', 'dp'), None, None, 'layer'), parts along dimension 0, may hold values from -6 to 6
- proj_in: bfloat16 [4, 4096, 64], P('layer'), may hold values from -0.09375 to 0.09375
- proj_out: bfloat16 [4, 4096, 64], P('layer'), may hold values from -0.09375 to 0.09375
- query_grads: bfloat16 [256, 4, 4096], P('dp', 'layer'), may hold values from -6 to 6
- margin: float32 [8], P(('groups', 'dp')), parts along dimension 0, may hold values from -8 to 8
- labels: int32 [8], P(('groups', 'dp')), parts along dimension 0, may hold values from 0 to 1
- lengths: int32 [8, 2], P(('groups', 'dp')), parts along dimension 0, may hold values from 16 to 64
Outputs:
- scores: float32 [8, 256], P(('groups', 'dp'), 'layer'), parts along dimension 0
The draws below stay inside these ranges and needn't reach their ends.
There are 2 independent parts, one for each index of `groups`. The reference program is written for one: setup_inputs(seed, part) draws one part's arguments, and reference() takes and returns one part's arrays. A program takes and returns all parts, laid end to end along the dimension named above; an argument that names none is the same for every part. Nothing has to cross between parts.
All inputs are finite; a program needn't handle non-finite values.
Results may differ from the reference program's by a relative error of at most 0.011.
Values may be sent and summed in bfloat16 or wider, within the bound.
No kernel may reach another device: no remote copies, remote signals or barrier semaphores. Data moves between devices by JAX's collectives and lax.ppermute only.
A program may use at most 64 MiB of HBM per device.

```python
import math
import jax
import jax.numpy as jnp

D = 4096
R = 64
SEQ = 64
QUERIES = 256
TRAIN = 4
LAYERS = 4


def place_ends(drawn, stream_key, smallest, largest):
    dims = drawn.shape
    index_at = [jax.random.randint(jax.random.fold_in(stream_key, axis), (), 0, dims[axis]) for axis in range(len(dims))]
    drawn = drawn.at[tuple(index_at)].set(smallest)
    longest = dims.index(max(dims))
    index_at[longest] = (index_at[longest] + 1) % dims[longest]
    return drawn.at[tuple(index_at)].set(largest)


def block_scale(own_key, extent, cuts, low, top_value):
    def one(dim, parts):
        steps = jax.random.uniform(jax.random.fold_in(jax.random.fold_in(own_key, 6), dim), (parts,), jnp.float32, low / len(cuts), top_value / len(cuts))
        return jnp.repeat(jnp.exp(steps), extent[dim] // parts).reshape((-1,) + (1,) * (len(extent) - dim - 1))

    level = one(*cuts[0])
    for cut in cuts[1:]:
        level = level * one(*cut)
    return level


def normal_values(own_key, shape, deviation, reach, pieces=(), held_as=jnp.bfloat16):
    values = jax.random.normal(own_key, shape, jnp.float32) * deviation
    if len(pieces) > 0:
        values = block_scale(own_key, shape, pieces, -0.22, 0.18) * values
    return jnp.clip(values, min=-reach, max=reach).astype(held_as)


def setup_inputs(seed: int = 0, part: int = 0) -> dict:
    key_of = jax.random.split(jax.random.key(seed), 9)
    own_keys = jax.random.split(jax.random.fold_in(key_of[8], part), 9)
    acts_in = normal_values(own_keys[0], (TRAIN, 2, SEQ, LAYERS, D), 1.0, 6.0, ((0, 4), (3, 4)))
    grads_out = normal_values(own_keys[1], (TRAIN, 2, SEQ, LAYERS, D), 1.0, 6.0, ((0, 4), (3, 4)))
    proj_in = normal_values(key_of[2], (LAYERS, D, R), D ** -0.5, 0.09375, ((0, 4),))
    proj_out = normal_values(key_of[3], (LAYERS, D, R), D ** -0.5, 0.09375, ((0, 4),))
    query_grads = normal_values(key_of[4], (QUERIES, LAYERS, R * R), 1.0, 6.0, ((0, 4), (1, 4)))
    margin = normal_values(own_keys[5], (TRAIN,), 2.0, 8.0, ((0, 4),), jnp.float32)
    labels = place_ends(jax.random.randint(own_keys[6], (TRAIN,), 0, 2), jax.random.fold_in(own_keys[6], 1), 0, 1).astype(jnp.int32)
    lengths = place_ends(jax.random.randint(own_keys[7], (TRAIN, 2), SEQ // 4, SEQ + 1), jax.random.fold_in(own_keys[7], 1), SEQ // 4, SEQ).astype(jnp.int32)
    return dict(acts_in=acts_in, grads_out=grads_out, proj_in=proj_in, proj_out=proj_out, query_grads=query_grads, margin=margin, labels=labels, lengths=lengths)


def reference(acts_in, grads_out, proj_in, proj_out, query_grads, margin, labels, lengths):
    in_coords = jnp.einsum('pstld,ldr->pstlr', acts_in.astype(jnp.float32), proj_in.astype(jnp.float32))
    out_coords = jnp.einsum('pstld,ldr->pstlr', grads_out.astype(jnp.float32), proj_out.astype(jnp.float32))
    position = jnp.arange(SEQ, dtype=jnp.int32)
    live = (position[None, None, :] < lengths[:, :, None]).astype(jnp.float32)
    side = jnp.arange(2, dtype=jnp.int32)
    signs = jnp.where(side[None, :] == labels[:, None], 1.0, -1.0).astype(jnp.float32)
    pair_weight = jax.nn.sigmoid(-margin)
    tok_weight = live * signs[:, :, None] * pair_weight[:, None, None] / math.sqrt(SEQ)
    kron_grads = jnp.einsum('pst,pstlr,pstlk->plrk', tok_weight, out_coords, in_coords)
    kron_grads = kron_grads.reshape(TRAIN, LAYERS, R * R).astype(jnp.bfloat16)
    total = jnp.einsum('plk,qlk->pq', kron_grads.astype(jnp.float32), query_grads.astype(jnp.float32))
    return total / (R * math.sqrt(LAYERS))
```

```python
import math

import jax
import jax.numpy as jnp
from jax import lax
from jax.sharding import PartitionSpec as P

FEW = 8


def gather_pairs(rows, count):
    got = [rows]
    for step in range(1, count):
        pairs = [(i, (i + step) % count) for i in range(count)]
        got.append(lax.ppermute(rows, "dp", pairs))
    return got


def send_home(scores, dp_count, layer_count):
    share = dp_count // layer_count
    mine, layer = lax.axis_index("dp"), lax.axis_index("layer")
    total = []
    lane = (mine % share) * layer_count + layer
    for turn in range(dp_count):
        pair = (lane + turn) % dp_count
        row = lax.dynamic_index_in_dim(scores, (mine - pair) % dp_count, 0, keepdims=False)
        moves = []
        for d in range(dp_count):
            for l in range(layer_count):
                target = ((d % share) * layer_count + l + turn) % dp_count
                moves.append((d * layer_count + l, target * layer_count + d // share))
        total.append(lax.ppermute(row, ("dp", "layer"), moves))
    return total


def local(acts_in, grads_out, proj_in, proj_out, query_grads, margin, labels, lengths):
    pair_count, side_count, seq_len, layer_count, model_width = acts_in.shape
    rank = proj_in.shape[2]
    dp_size, layer_size = lax.axis_size("dp"), lax.axis_size("layer")
    in_coords = jnp.einsum("pstld,ldr->pstlr", acts_in, proj_in, preferred_element_type=jnp.float32)
    out_coords = jnp.einsum(
        "pstld,ldr->pstlr", grads_out, proj_out, preferred_element_type=jnp.float32
    )
    position = jnp.arange(seq_len, dtype=jnp.int32)
    live = (position[None, None, :] < lengths[:, :, None]).astype(jnp.float32)
    side = jnp.arange(side_count, dtype=jnp.int32)
    signs = jnp.where(side[None, :] == labels[:, None], 1.0, -1.0).astype(jnp.float32)
    pair_weight = jax.nn.sigmoid(-margin)
    tok_weight = live * signs[:, :, None] * pair_weight[:, None, None] / math.sqrt(seq_len)
    kron_grads = jnp.einsum("pst,pstlr,pstlk->plrk", tok_weight, out_coords, in_coords)
    grad_rows = kron_grads.reshape(pair_count, layer_count * rank * rank).astype(jnp.bfloat16)
    block = query_grads.reshape(query_grads.shape[0], -1)
    scale = rank * math.sqrt(layer_count * layer_size)
    if dp_size <= FEW and pair_count == 1 and dp_size % layer_size == 0:
        rows = jnp.concatenate(gather_pairs(grad_rows, dp_size), axis=0)
        scores = jnp.einsum("pk,qk->pq", rows, block, preferred_element_type=jnp.float32)
        parts = send_home(scores, dp_size, layer_size)
        return sum(parts[1:], parts[0])[None] / scale
    rows = lax.all_gather(grad_rows, "dp", axis=0, tiled=True)
    scores = jnp.einsum("pk,qk->pq", rows, block, preferred_element_type=jnp.float32)
    scores = lax.all_to_all(scores, "dp", split_axis=0, concat_axis=1, tiled=True)
    summed = lax.psum_scatter(scores, "layer", scatter_dimension=1, tiled=True)
    return summed / scale


def solution(mesh):
    placed = (
        P(("groups", "dp"), None, None, "layer", None),
        P(("groups", "dp"), None, None, "layer", None),
        P("layer", None, None),
        P("layer", None, None),
        P("dp", "layer", None),
        P(("groups", "dp")),
        P(("groups", "dp")),
        P(("groups", "dp"), None),
    )
    return jax.shard_map(
        local, mesh=mesh, in_specs=placed, out_specs=P(("groups", "dp"), "layer"), check_vma=False
    )
```

```python
import math

import jax
import jax.numpy as jnp
from jax import lax
from jax.sharding import PartitionSpec as P

FEW = 8


def gather_pairs(rows, count):
    return lax.all_to_all(jnp.broadcast_to(rows, (count, rows.shape[1])), "dp", 0, 0, tiled=True)


def send_home(scores, dp_count, layer_count):
    share = dp_count // layer_count
    mine = lax.axis_index("dp")
    here = jnp.arange(layer_count)[None, :, None] == mine // share
    out = jnp.where(here, scores[:, None, :], 0.0).reshape(dp_count * layer_count, -1)
    got = lax.all_to_all(out, ("dp", "layer"), 0, 0, tiled=True)
    got = got.reshape(layer_count, share, layer_count, -1)
    return got.sum(axis=(0, 2)).reshape(1, -1)


def local(acts_in, grads_out, proj_in, proj_out, query_grads, margin, labels, lengths):
    pair_count, side_count, seq_len, layer_count, model_width = acts_in.shape
    rank = proj_in.shape[2]
    dp_size, layer_size = lax.axis_size("dp"), lax.axis_size("layer")
    in_coords = jnp.einsum("pstld,ldr->pstlr", acts_in, proj_in, preferred_element_type=jnp.float32)
    out_coords = jnp.einsum(
        "pstld,ldr->pstlr", grads_out, proj_out, preferred_element_type=jnp.float32
    )
    position = jnp.arange(seq_len, dtype=jnp.int32)
    live = (position[None, None, :] < lengths[:, :, None]).astype(jnp.float32)
    side = jnp.arange(side_count, dtype=jnp.int32)
    signs = jnp.where(side[None, :] == labels[:, None], 1.0, -1.0).astype(jnp.float32)
    pair_weight = jax.nn.sigmoid(-margin)
    tok_weight = live * signs[:, :, None] * pair_weight[:, None, None] / math.sqrt(seq_len)
    kron_grads = jnp.einsum("pst,pstlr,pstlk->plrk", tok_weight, out_coords, in_coords)
    grad_rows = kron_grads.reshape(pair_count, layer_count * rank * rank).astype(jnp.bfloat16)
    block = query_grads.reshape(query_grads.shape[0], -1)
    scale = rank * math.sqrt(layer_count * layer_size)
    if dp_size <= FEW and pair_count == 1 and dp_size % layer_size == 0:
        rows = gather_pairs(grad_rows, dp_size)
        scores = jnp.einsum("pk,qk->pq", rows, block, preferred_element_type=jnp.float32)
        return send_home(scores, dp_size, layer_size) / scale
    rows = lax.all_gather(grad_rows, "dp", axis=0, tiled=True)
    scores = jnp.einsum("pk,qk->pq", rows, block, preferred_element_type=jnp.float32)
    scores = lax.all_to_all(scores, "dp", split_axis=0, concat_axis=1, tiled=True)
    summed = lax.psum_scatter(scores, "layer", scatter_dimension=1, tiled=True)
    return summed / scale


def solution(mesh):
    placed = (
        P(("groups", "dp"), None, None, "layer", None),
        P(("groups", "dp"), None, None, "layer", None),
        P("layer", None, None),
        P("layer", None, None),
        P("dp", "layer", None),
        P(("groups", "dp")),
        P(("groups", "dp")),
        P(("groups", "dp"), None),
    )
    return jax.shard_map(
        local, mesh=mesh, in_specs=placed, out_specs=P(("groups", "dp"), "layer"), check_vma=False
    )
```

```python
import math

import jax
import jax.numpy as jnp
from jax import lax
from jax.sharding import PartitionSpec as P

FIRST = (3, 2, 1, 0)
SECOND = (0, 1, 2, 3)


def swap(x):
    return lax.ppermute(x, "layer", [(i, i ^ 1) for i in range(lax.axis_size("layer"))])


def along_dp(x, steps):
    count = len(steps)
    moves = [(d * count + i, (d ^ steps[i]) * count + i) for d in range(count) for i in range(count)]
    return lax.ppermute(x, ("dp", "layer"), moves)


def to_owner(x, steps):
    count = len(steps)
    moves = [(d * count + i, (d ^ steps[i]) * count + d) for d in range(count) for i in range(count)]
    return lax.ppermute(x, ("dp", "layer"), moves)


def shared_scores(own_row, own_block):
    other_block = swap(own_block)
    rows = jnp.concatenate([own_row, swap(own_row)], axis=0)
    first, second = along_dp(rows, FIRST), along_dp(rows, SECOND)

    def score(got):
        one = jnp.einsum("k,qk->q", got[0], own_block, preferred_element_type=jnp.float32)
        two = jnp.einsum("k,qk->q", got[1], other_block, preferred_element_type=jnp.float32)
        return one + two

    return (to_owner(score(first), FIRST) + to_owner(score(second), SECOND))[None]


def local(acts_in, grads_out, proj_in, proj_out, query_grads, margin, labels, lengths):
    pair_count, side_count, seq_len, layer_count, model_width = acts_in.shape
    rank = proj_in.shape[2]
    dp_size, layer_size = lax.axis_size("dp"), lax.axis_size("layer")
    in_coords = jnp.einsum("pstld,ldr->pstlr", acts_in, proj_in, preferred_element_type=jnp.float32)
    out_coords = jnp.einsum(
        "pstld,ldr->pstlr", grads_out, proj_out, preferred_element_type=jnp.float32
    )
    position = jnp.arange(seq_len, dtype=jnp.int32)
    live = (position[None, None, :] < lengths[:, :, None]).astype(jnp.float32)
    side = jnp.arange(side_count, dtype=jnp.int32)
    signs = jnp.where(side[None, :] == labels[:, None], 1.0, -1.0).astype(jnp.float32)
    pair_weight = jax.nn.sigmoid(-margin)
    tok_weight = live * signs[:, :, None] * pair_weight[:, None, None] / math.sqrt(seq_len)
    kron_grads = jnp.einsum("pst,pstlr,pstlk->plrk", tok_weight, out_coords, in_coords)
    grad_rows = kron_grads.reshape(pair_count, layer_count * rank * rank).astype(jnp.bfloat16)
    block = query_grads.reshape(query_grads.shape[0], -1)
    scale = rank * math.sqrt(layer_count * layer_size)
    if pair_count == layer_count == 1 and dp_size == layer_size == len(FIRST):
        return shared_scores(grad_rows, block) / scale
    rows = lax.all_gather(grad_rows, "dp", axis=0, tiled=True)
    scores = jnp.einsum("pk,qk->pq", rows, block, preferred_element_type=jnp.float32)
    scores = lax.all_to_all(scores, "dp", split_axis=0, concat_axis=1, tiled=True)
    summed = lax.psum_scatter(scores, "layer", scatter_dimension=1, tiled=True)
    return summed / scale


def solution(mesh):
    placed = (
        P(("groups", "dp"), None, None, "layer", None),
        P(("groups", "dp"), None, None, "layer", None),
        P("layer", None, None),
        P("layer", None, None),
        P("dp", "layer", None),
        P(("groups", "dp")),
        P(("groups", "dp")),
        P(("groups", "dp"), None),
    )
    return jax.shard_map(
        local, mesh=mesh, in_specs=placed, out_specs=P(("groups", "dp"), "layer"), check_vma=False
    )
```

```python
import functools
import math

import jax
import jax.numpy as jnp
from jax import lax
from jax.sharding import PartitionSpec as P

FIRST = ((1, 3, 2, 0), (0, 2, 1, 3), (3, 1, 0, 2), (2, 0, 3, 1))
SECOND = ((2, 0, 3, 1), (1, 3, 2, 0), (0, 2, 1, 3), (3, 1, 0, 2))


def swap(x):
    return lax.ppermute(x, "layer", [(i, i ^ 1) for i in range(lax.axis_size("layer"))])


def fetch_pair(x, slot):
    count = len(slot)
    moves, own = [], []
    for d in range(count):
        for i in range(count):
            if slot[d][i] == d:
                own.append(d * count + i)
            else:
                moves.append((slot[d][i] * count + i, d * count + i))
    fill = zip(own, own[1::-1] + own[:1:-1])
    here = lax.axis_index("dp") * count + lax.axis_index("layer")
    is_own = functools.reduce(jnp.logical_or, [here == i for i in own])
    return lax.ppermute(x, ("dp", "layer"), moves + list(fill)), is_own


def to_owner(x, slot):
    count = len(slot)
    moves = [(d * count + i, slot[d][i] * count + d) for d in range(count) for i in range(count)]
    return lax.ppermute(x, ("dp", "layer"), moves)


def shared_scores(own_row, own_block):
    other_block = swap(own_block)
    rows = jnp.concatenate([own_row, swap(own_row)], axis=0)
    (first, first_own), (second, second_own) = fetch_pair(rows, FIRST), fetch_pair(rows, SECOND)

    def score(got):
        one = jnp.einsum("k,qk->q", got[0], own_block, preferred_element_type=jnp.float32)
        two = jnp.einsum("k,qk->q", got[1], other_block, preferred_element_type=jnp.float32)
        return one + two

    own = score(rows)
    first, second = jnp.where(first_own, own, score(first)), jnp.where(second_own, own, score(second))
    return (to_owner(first, FIRST) + to_owner(second, SECOND))[None]


def local(acts_in, grads_out, proj_in, proj_out, query_grads, margin, labels, lengths):
    pair_count, side_count, seq_len, layer_count, model_width = acts_in.shape
    rank = proj_in.shape[2]
    dp_size, layer_size = lax.axis_size("dp"), lax.axis_size("layer")
    in_coords = jnp.einsum("pstld,ldr->pstlr", acts_in, proj_in, preferred_element_type=jnp.float32)
    out_coords = jnp.einsum(
        "pstld,ldr->pstlr", grads_out, proj_out, preferred_element_type=jnp.float32
    )
    position = jnp.arange(seq_len, dtype=jnp.int32)
    live = (position[None, None, :] < lengths[:, :, None]).astype(jnp.float32)
    side = jnp.arange(side_count, dtype=jnp.int32)
    signs = jnp.where(side[None, :] == labels[:, None], 1.0, -1.0).astype(jnp.float32)
    pair_weight = jax.nn.sigmoid(-margin)
    tok_weight = live * signs[:, :, None] * pair_weight[:, None, None] / math.sqrt(seq_len)
    kron_grads = jnp.einsum("pst,pstlr,pstlk->plrk", tok_weight, out_coords, in_coords)
    grad_rows = kron_grads.reshape(pair_count, layer_count * rank * rank).astype(jnp.bfloat16)
    block = query_grads.reshape(query_grads.shape[0], -1)
    scale = rank * math.sqrt(layer_count * layer_size)
    if pair_count == layer_count == 1 and dp_size == layer_size == len(FIRST):
        return shared_scores(grad_rows, block) / scale
    rows = lax.all_gather(grad_rows, "dp", axis=0, tiled=True)
    scores = jnp.einsum("pk,qk->pq", rows, block, preferred_element_type=jnp.float32)
    scores = lax.all_to_all(scores, "dp", split_axis=0, concat_axis=1, tiled=True)
    summed = lax.psum_scatter(scores, "layer", scatter_dimension=1, tiled=True)
    return summed / scale


def solution(mesh):
    placed = (
        P(("groups", "dp"), None, None, "layer", None),
        P(("groups", "dp"), None, None, "layer", None),
        P("layer", None, None),
        P("layer", None, None),
        P("dp", "layer", None),
        P(("groups", "dp")),
        P(("groups", "dp")),
        P(("groups", "dp"), None),
    )
    return jax.shard_map(
        local, mesh=mesh, in_specs=placed, out_specs=P(("groups", "dp"), "layer"), check_vma=False
    )
```

```python
import functools
import math

import jax
import jax.numpy as jnp
from jax import lax
from jax.experimental import pallas as pl
from jax.experimental.pallas import tpu as pltpu
from jax.sharding import PartitionSpec as P

FIRST = ((2, 0, 3, 1), (1, 3, 2, 0), (0, 2, 1, 3), (3, 1, 0, 2))
SECOND = ((1, 3, 2, 0), (0, 2, 1, 3), (3, 1, 0, 2), (2, 0, 3, 1))


CHUNKS = 2


def pair_kernel(seq_len, acts, proj_in, grads, proj_out, lengths, out, *scratch):
    acts_v, pin_v, grads_v, pout_v, kron_v, lengths_s, sems = scratch
    width = acts.shape[1] // CHUNKS
    limits = pltpu.make_async_copy(lengths, lengths_s, sems.at[4 * CHUNKS])
    loads = []
    for pair in (((acts, acts_v), (proj_in, pin_v)), ((grads, grads_v), (proj_out, pout_v))):
        for c in range(CHUNKS):
            part = pl.ds(c * width, width)
            loads.append([
                pltpu.make_async_copy(src.at[:, part], dst.at[:, part], sems.at[2 * len(loads) + i])
                for i, (src, dst) in enumerate(pair)
            ])
    for copies in loads:
        for copy in copies:
            copy.start()
    limits.start()

    def project(left, right, steps):
        total = None
        for c, copies in enumerate(steps):
            for copy in copies:
                copy.wait()
            part = pl.ds(c * width, width)
            term = lax.dot_general(
                left[:, part], right[:, part], (((1,), (1,)), ((), ())), preferred_element_type=jnp.float32
            )
            total = term if total is None else total + term
        return total

    in_coords = project(acts_v, pin_v, loads[:CHUNKS])
    limits.wait()
    token = lax.broadcasted_iota(jnp.int32, in_coords.shape, 0)
    side = token // seq_len
    live = token - side * seq_len < jnp.where(side == 0, lengths_s[0, 0], lengths_s[0, 1])
    weight = jnp.where(live, jnp.where(side == 0, 1.0, -1.0), 0.0)
    in_coords = (in_coords * weight).astype(jnp.bfloat16)
    out_coords = project(pout_v, grads_v, loads[CHUNKS:]).astype(jnp.bfloat16)
    kron_v[...] = jnp.dot(out_coords, in_coords, preferred_element_type=jnp.float32)
    half = kron_v.shape[0] // 2
    rows = jnp.concatenate([kron_v[pl.ds(i, half, stride=2), :] for i in range(2)], axis=1)
    for i in range(half):
        out[:, pl.ds(i * rows.shape[1], rows.shape[1])] = rows[i : i + 1].astype(out.dtype)


def pair_gradient(acts_in, grads_out, proj_in, proj_out, lengths):
    _, sides, seq_len, _, model_width = acts_in.shape
    rank = proj_in.shape[2]
    tokens = sides * seq_len
    anywhere = pl.BlockSpec(memory_space=pl.ANY)
    return pl.pallas_call(
        functools.partial(pair_kernel, seq_len),
        out_shape=jax.ShapeDtypeStruct((1, rank * rank), jnp.bfloat16),
        in_specs=[anywhere] * 5,
        out_specs=pl.BlockSpec(memory_space=pltpu.VMEM),
        scratch_shapes=[
            pltpu.VMEM((tokens, model_width), jnp.bfloat16),
            pltpu.VMEM((rank, model_width), jnp.bfloat16),
            pltpu.VMEM((tokens, model_width), jnp.bfloat16),
            pltpu.VMEM((rank, model_width), jnp.bfloat16),
            pltpu.VMEM((rank, rank), jnp.float32),
            pltpu.SMEM((1, 2), jnp.int32),
            pltpu.SemaphoreType.DMA((4 * CHUNKS + 1,)),
        ],
        compiler_params=pltpu.CompilerParams(vmem_limit_bytes=32 * 1024 * 1024),
        cost_estimate=pl.CostEstimate(
            flops=4 * tokens * model_width * rank,
            bytes_accessed=4 * (tokens + rank) * model_width,
            transcendentals=0,
        ),
    )(
        *(
            pltpu.with_memory_space_constraint(x, pltpu.HBM)
            for x in (
                acts_in.reshape(tokens, model_width),
                jnp.swapaxes(proj_in, 1, 2).reshape(rank, model_width),
                grads_out.reshape(tokens, model_width),
                jnp.swapaxes(proj_out, 1, 2).reshape(rank, model_width),
                lengths,
            )
        )
    )


def swap(x):
    return lax.ppermute(x, "layer", [(i, i ^ 1) for i in range(lax.axis_size("layer"))])


def fetch_pair(x, slot):
    count = len(slot)
    moves, own = [], []
    for d in range(count):
        for i in range(count):
            if slot[d][i] == d:
                own.append(d * count + i)
            else:
                moves.append((slot[d][i] * count + i, d * count + i))
    fill = zip(own, own[1::-1] + own[:1:-1])
    here = lax.axis_index("dp") * count + lax.axis_index("layer")
    is_own = functools.reduce(jnp.logical_or, [here == i for i in own])
    return lax.ppermute(x, ("dp", "layer"), moves + list(fill)), is_own


def to_owner(x, slot):
    count = len(slot)
    moves = [(d * count + i, slot[d][i] * count + d) for d in range(count) for i in range(count)]
    return lax.ppermute(x, ("dp", "layer"), moves)


def shared_scores(own_row, own_block):
    other_block = swap(own_block)
    rows = jnp.concatenate([own_row, swap(own_row)], axis=0)
    (first, first_own), (second, second_own) = fetch_pair(rows, FIRST), fetch_pair(rows, SECOND)

    def score(got):
        one = jnp.einsum("k,qk->q", got[0], own_block, preferred_element_type=jnp.float32)
        two = jnp.einsum("k,qk->q", got[1], other_block, preferred_element_type=jnp.float32)
        return one + two

    own = score(rows)
    first, second = jnp.where(first_own, own, score(first)), jnp.where(second_own, own, score(second))
    return (to_owner(first, FIRST) + to_owner(second, SECOND))[None]


def pair_gradients(acts_in, grads_out, proj_in, proj_out, lengths):
    pair_count, side_count, seq_len, layer_count, _ = acts_in.shape
    in_coords = jnp.einsum("pstld,ldr->pstlr", acts_in, proj_in, preferred_element_type=jnp.float32)
    out_coords = jnp.einsum(
        "pstld,ldr->pstlr", grads_out, proj_out, preferred_element_type=jnp.float32
    )
    position = jnp.arange(seq_len, dtype=jnp.int32)
    live = (position[None, None, :] < lengths[:, :, None]).astype(jnp.float32)
    signs = 1.0 - 2.0 * jnp.arange(side_count, dtype=jnp.float32)
    kron_grads = jnp.einsum("pst,pstlr,pstlk->plrk", live * signs[:, None], out_coords, in_coords)
    return kron_grads.reshape(pair_count, -1).astype(jnp.bfloat16)


def local(acts_in, grads_out, proj_in, proj_out, query_grads, margin, labels, lengths):
    pair_count, side_count, _, layer_count, _ = acts_in.shape
    rank = proj_in.shape[2]
    dp_size, layer_size = lax.axis_size("dp"), lax.axis_size("layer")
    block = query_grads.reshape(query_grads.shape[0], -1)
    one_each = pair_count == layer_count == 1 and side_count == 2
    form = pair_gradient if one_each else pair_gradients
    grad_rows = form(acts_in, grads_out, proj_in, proj_out, lengths)
    margin, labels, grad_rows = lax.optimization_barrier((margin, labels, grad_rows))
    scale = rank * math.sqrt(layer_count * layer_size) * math.sqrt(acts_in.shape[2])
    factor = jax.nn.sigmoid(-margin) * jnp.where(labels == 0, 1.0, -1.0) / scale
    if one_each and dp_size == layer_size == len(FIRST):
        return shared_scores(grad_rows, block) * factor[:, None]
    rows = lax.all_gather(grad_rows, "dp", axis=0, tiled=True)
    scores = jnp.einsum("pk,qk->pq", rows, block, preferred_element_type=jnp.float32)
    scores = lax.all_to_all(scores, "dp", split_axis=0, concat_axis=1, tiled=True)
    summed = lax.psum_scatter(scores, "layer", scatter_dimension=1, tiled=True)
    return summed * factor[:, None]


def solution(mesh):
    placed = (
        P(("groups", "dp"), None, None, "layer", None),
        P(("groups", "dp"), None, None, "layer", None),
        P("layer", None, None),
        P("layer", None, None),
        P("dp", "layer", None),
        P(("groups", "dp")),
        P(("groups", "dp")),
        P(("groups", "dp"), None),
    )
    return jax.shard_map(
        local, mesh=mesh, in_specs=placed, out_specs=P(("groups", "dp"), "layer"), check_vma=False
    )
```

```python
import functools
import math

import jax
import jax.numpy as jnp
from jax import lax
from jax.experimental import pallas as pl
from jax.experimental.pallas import tpu as pltpu
from jax.sharding import PartitionSpec as P

FIRST = ((3, 1, 2, 0), (1, 2, 0, 3), (0, 3, 1, 2), (2, 0, 3, 1))
SECOND = ((2, 0, 1, 3), (0, 3, 2, 1), (1, 2, 3, 0), (3, 1, 0, 2))
CHUNKS = 2


def pair_kernel(seq_len, acts, proj_in, grads, proj_out, lengths, out, *scratch):
    acts_v, pin_v, grads_v, pout_v, kron_v, lengths_s, sems = scratch
    width = acts.shape[1] // CHUNKS
    limits = pltpu.make_async_copy(lengths, lengths_s, sems.at[4 * CHUNKS])
    loads = []
    for pair in (((acts, acts_v), (proj_in, pin_v)), ((grads, grads_v), (proj_out, pout_v))):
        for c in range(CHUNKS):
            part = pl.ds(c * width, width)
            loads.append([
                pltpu.make_async_copy(src.at[:, part], dst.at[:, part], sems.at[2 * len(loads) + i])
                for i, (src, dst) in enumerate(pair)
            ])
    for copies in loads:
        for copy in copies:
            copy.start()
    limits.start()

    def project(left, right, steps):
        total = None
        for c, copies in enumerate(steps):
            for copy in copies:
                copy.wait()
            part = pl.ds(c * width, width)
            term = lax.dot_general(
                left[:, part], right[:, part], (((1,), (1,)), ((), ())), preferred_element_type=jnp.float32
            )
            total = term if total is None else total + term
        return total

    in_coords = project(acts_v, pin_v, loads[:CHUNKS])
    limits.wait()
    token = lax.broadcasted_iota(jnp.int32, in_coords.shape, 0)
    side = token // seq_len
    live = token - side * seq_len < jnp.where(side == 0, lengths_s[0, 0], lengths_s[0, 1])
    weight = jnp.where(live, jnp.where(side == 0, 1.0, -1.0), 0.0)
    in_coords = (in_coords * weight).astype(jnp.bfloat16)
    out_coords = project(pout_v, grads_v, loads[CHUNKS:]).astype(jnp.bfloat16)
    kron_v[...] = jnp.dot(out_coords, in_coords, preferred_element_type=jnp.float32)
    half = kron_v.shape[0] // 2
    rows = jnp.concatenate([kron_v[pl.ds(i, half, stride=2), :] for i in range(2)], axis=1)
    for i in range(half):
        out[:, pl.ds(i * rows.shape[1], rows.shape[1])] = rows[i : i + 1].astype(out.dtype)


def pair_gradient(acts_in, grads_out, proj_in, proj_out, lengths):
    _, sides, seq_len, _, model_width = acts_in.shape
    rank = proj_in.shape[2]
    tokens = sides * seq_len
    anywhere = pl.BlockSpec(memory_space=pl.ANY)
    return pl.pallas_call(
        functools.partial(pair_kernel, seq_len),
        out_shape=jax.ShapeDtypeStruct((1, rank * rank), jnp.bfloat16),
        in_specs=[anywhere] * 5,
        out_specs=pl.BlockSpec(memory_space=pltpu.VMEM),
        scratch_shapes=[
            pltpu.VMEM((tokens, model_width), jnp.bfloat16),
            pltpu.VMEM((rank, model_width), jnp.bfloat16),
            pltpu.VMEM((tokens, model_width), jnp.bfloat16),
            pltpu.VMEM((rank, model_width), jnp.bfloat16),
            pltpu.VMEM((rank, rank), jnp.float32),
            pltpu.SMEM((1, 2), jnp.int32),
            pltpu.SemaphoreType.DMA((4 * CHUNKS + 1,)),
        ],
        compiler_params=pltpu.CompilerParams(vmem_limit_bytes=32 * 1024 * 1024),
        cost_estimate=pl.CostEstimate(
            flops=4 * tokens * model_width * rank,
            bytes_accessed=4 * (tokens + rank) * model_width,
            transcendentals=0,
        ),
    )(
        *(
            pltpu.with_memory_space_constraint(x, pltpu.HBM)
            for x in (
                acts_in.reshape(tokens, model_width),
                jnp.swapaxes(proj_in, 1, 2).reshape(rank, model_width),
                grads_out.reshape(tokens, model_width),
                jnp.swapaxes(proj_out, 1, 2).reshape(rank, model_width),
                lengths,
            )
        )
    )


def swap(x):
    return lax.ppermute(x, "layer", [(i, i ^ 1) for i in range(lax.axis_size("layer"))])


def own_places(slot):
    return [(d, i) for d, row in enumerate(slot) for i, pair in enumerate(row) if pair == d]


def fetch_pair(x, slot):
    count = len(slot)
    moves = [
        (slot[d][i] * count + i, d * count + i) for d in range(count) for i in range(count) if slot[d][i] != d
    ]
    own = [d * count + i for d, i in own_places(slot)]
    fill = zip(own, own[1::-1] + own[:1:-1])
    return lax.ppermute(x, ("dp", "layer"), moves + list(fill))


def to_owner(x, slot):
    count = len(slot)
    moves = [(d * count + i, slot[d][i] * count + d) for d in range(count) for i in range(count)]
    return lax.ppermute(x, ("dp", "layer"), moves)


def row_scores(rows, own_block, other_block):
    one, two = (
        lax.dot_general(rows, block[...], (((1,), (1,)), ((), ())), preferred_element_type=jnp.float32)
        for block in (own_block, other_block)
    )
    return one[:1] + two[1:]


def own_kernel(scale, margin, label, rows, own_block, other_block, out, factor):
    out[...] = row_scores(rows[...], own_block, other_block)
    sign = jnp.where(label[0] == 0, 1.0, -1.0)
    factor[...] = sign / ((1.0 + jnp.exp(jnp.full(factor.shape, margin[0], jnp.float32))) * scale)


def slot_kernel(slot, rows, own, own_block, other_block, out):
    here = lax.axis_index("dp") * len(slot) + lax.axis_index("layer")
    is_own = functools.reduce(jnp.logical_or, [here == d * len(slot) + i for d, i in own_places(slot)])
    out[...] = jnp.where(is_own, own[...], row_scores(rows[...], own_block, other_block))


def shared_scores(own_row, own_block, margin, labels, scale):
    blocks = [pltpu.with_memory_space_constraint(x, pltpu.VMEM) for x in (own_block, swap(own_block))]
    rows = jnp.concatenate([own_row, swap(own_row)], axis=0)
    first, second = fetch_pair(rows, FIRST), fetch_pair(rows, SECOND)
    scalar, vector = pl.BlockSpec(memory_space=pltpu.SMEM), pl.BlockSpec(memory_space=pltpu.VMEM)
    line = jax.ShapeDtypeStruct((1, own_block.shape[0]), jnp.float32)
    cost = pl.CostEstimate(flops=8 * own_block.size, bytes_accessed=4 * own_block.size, transcendentals=0)
    own, factor = pl.pallas_call(
        functools.partial(own_kernel, scale),
        out_shape=(line, line),
        in_specs=[scalar] * 2 + [vector] * 3,
        out_specs=(vector, vector),
        cost_estimate=cost,
    )(margin, labels, rows, *blocks)

    def score(got, slot):
        return pl.pallas_call(
            functools.partial(slot_kernel, slot),
            out_shape=line,
            in_specs=[vector] * 4,
            out_specs=vector,
            cost_estimate=cost,
        )(got, own, *blocks)

    first, second = to_owner(score(first, FIRST), FIRST), to_owner(score(second, SECOND), SECOND)
    return (first + second) * factor


def pair_gradients(acts_in, grads_out, proj_in, proj_out, lengths):
    pair_count, side_count, seq_len, layer_count, _ = acts_in.shape
    in_coords = jnp.einsum("pstld,ldr->pstlr", acts_in, proj_in, preferred_element_type=jnp.float32)
    out_coords = jnp.einsum(
        "pstld,ldr->pstlr", grads_out, proj_out, preferred_element_type=jnp.float32
    )
    position = jnp.arange(seq_len, dtype=jnp.int32)
    live = (position[None, None, :] < lengths[:, :, None]).astype(jnp.float32)
    signs = 1.0 - 2.0 * jnp.arange(side_count, dtype=jnp.float32)
    kron_grads = jnp.einsum("pst,pstlr,pstlk->plrk", live * signs[:, None], out_coords, in_coords)
    return kron_grads.reshape(pair_count, -1).astype(jnp.bfloat16)


def local(acts_in, grads_out, proj_in, proj_out, query_grads, margin, labels, lengths):
    pair_count, side_count, _, layer_count, _ = acts_in.shape
    rank = proj_in.shape[2]
    dp_size, layer_size = lax.axis_size("dp"), lax.axis_size("layer")
    block = query_grads.reshape(query_grads.shape[0], -1)
    one_each = pair_count == layer_count == 1 and side_count == 2
    form = pair_gradient if one_each else pair_gradients
    grad_rows = form(acts_in, grads_out, proj_in, proj_out, lengths)
    scale = rank * math.sqrt(layer_count * layer_size) * math.sqrt(acts_in.shape[2])
    if one_each and dp_size == layer_size == len(FIRST):
        return shared_scores(grad_rows, block, margin, labels, scale)
    factor = jax.nn.sigmoid(-margin) * jnp.where(labels == 0, 1.0, -1.0) / scale
    rows = lax.all_gather(grad_rows, "dp", axis=0, tiled=True)
    scores = jnp.einsum("pk,qk->pq", rows, block, preferred_element_type=jnp.float32)
    scores = lax.all_to_all(scores, "dp", split_axis=0, concat_axis=1, tiled=True)
    summed = lax.psum_scatter(scores, "layer", scatter_dimension=1, tiled=True)
    return summed * factor[:, None]


def solution(mesh):
    placed = (
        P(("groups", "dp"), None, None, "layer", None),
        P(("groups", "dp"), None, None, "layer", None),
        P("layer", None, None),
        P("layer", None, None),
        P("dp", "layer", None),
        P(("groups", "dp")),
        P(("groups", "dp")),
        P(("groups", "dp"), None),
    )
    return jax.shard_map(
        local, mesh=mesh, in_specs=placed, out_specs=P(("groups", "dp"), "layer"), check_vma=False
    )
```

```python
import functools
import math

import jax
import jax.numpy as jnp
from jax import lax
from jax.experimental import pallas as pl
from jax.experimental.pallas import tpu as pltpu
from jax.sharding import PartitionSpec as P

FIRST = ((2, 0, 1, 3), (0, 3, 2, 1), (1, 2, 3, 0), (3, 1, 0, 2))
SECOND = ((3, 1, 2, 0), (1, 2, 0, 3), (0, 3, 1, 2), (2, 0, 3, 1))
CHUNKS = 2


def pair_kernel(seq_len, acts, proj_in, grads, proj_out, lengths, out, *scratch):
    acts_v, pin_v, grads_v, pout_v, kron_v, lengths_s, sems = scratch
    width = acts.shape[1] // CHUNKS
    limits = pltpu.make_async_copy(lengths, lengths_s, sems.at[4 * CHUNKS])
    loads = []
    for pair in (((acts, acts_v), (proj_in, pin_v)), ((grads, grads_v), (proj_out, pout_v))):
        for c in range(CHUNKS):
            part = pl.ds(c * width, width)
            loads.append([
                pltpu.make_async_copy(src.at[:, part], dst.at[:, part], sems.at[2 * len(loads) + i])
                for i, (src, dst) in enumerate(pair)
            ])
    for copies in loads:
        for copy in copies:
            copy.start()
    limits.start()

    def project(left, right, steps):
        total = None
        for c, copies in enumerate(steps):
            for copy in copies:
                copy.wait()
            part = pl.ds(c * width, width)
            term = lax.dot_general(
                left[:, part], right[:, part], (((1,), (1,)), ((), ())), preferred_element_type=jnp.float32
            )
            total = term if total is None else total + term
        return total

    in_coords = project(acts_v, pin_v, loads[:CHUNKS])
    limits.wait()
    token = lax.broadcasted_iota(jnp.int32, in_coords.shape, 0)
    side = token // seq_len
    live = token - side * seq_len < jnp.where(side == 0, lengths_s[0, 0], lengths_s[0, 1])
    weight = jnp.where(live, jnp.where(side == 0, 1.0, -1.0), 0.0)
    in_coords = (in_coords * weight).astype(jnp.bfloat16)
    out_coords = project(pout_v, grads_v, loads[CHUNKS:]).astype(jnp.bfloat16)
    kron_v[...] = jnp.dot(out_coords, in_coords, preferred_element_type=jnp.float32)
    half = kron_v.shape[0] // 2
    rows = jnp.concatenate([kron_v[pl.ds(i, half, stride=2), :] for i in range(2)], axis=1)
    for i in range(half):
        out[:, pl.ds(i * rows.shape[1], rows.shape[1])] = rows[i : i + 1].astype(out.dtype)


def pair_gradient(acts_in, grads_out, proj_in, proj_out, lengths):
    _, sides, seq_len, _, model_width = acts_in.shape
    rank = proj_in.shape[2]
    tokens = sides * seq_len
    anywhere = pl.BlockSpec(memory_space=pl.ANY)
    return pl.pallas_call(
        functools.partial(pair_kernel, seq_len),
        out_shape=jax.ShapeDtypeStruct((1, rank * rank), jnp.bfloat16),
        in_specs=[anywhere] * 5,
        out_specs=pl.BlockSpec(memory_space=pltpu.VMEM),
        scratch_shapes=[
            pltpu.VMEM((tokens, model_width), jnp.bfloat16),
            pltpu.VMEM((rank, model_width), jnp.bfloat16),
            pltpu.VMEM((tokens, model_width), jnp.bfloat16),
            pltpu.VMEM((rank, model_width), jnp.bfloat16),
            pltpu.VMEM((rank, rank), jnp.float32),
            pltpu.SMEM((1, 2), jnp.int32),
            pltpu.SemaphoreType.DMA((4 * CHUNKS + 1,)),
        ],
        compiler_params=pltpu.CompilerParams(vmem_limit_bytes=32 * 1024 * 1024),
        cost_estimate=pl.CostEstimate(
            flops=4 * tokens * model_width * rank,
            bytes_accessed=4 * (tokens + rank) * model_width,
            transcendentals=0,
        ),
    )(
        *(
            pltpu.with_memory_space_constraint(x, pltpu.HBM)
            for x in (
                acts_in.reshape(tokens, model_width),
                jnp.swapaxes(proj_in, 1, 2).reshape(rank, model_width),
                grads_out.reshape(tokens, model_width),
                jnp.swapaxes(proj_out, 1, 2).reshape(rank, model_width),
                lengths,
            )
        )
    )


def swap(x):
    return lax.ppermute(x, "layer", [(i, i ^ 1) for i in range(lax.axis_size("layer"))])


def own_places(slot):
    return [(d, i) for d, row in enumerate(slot) for i, pair in enumerate(row) if pair == d]


def fetch_pair(x, slot):
    count = len(slot)
    moves = [
        (slot[d][i] * count + i, d * count + i) for d in range(count) for i in range(count) if slot[d][i] != d
    ]
    own = [d * count + i for d, i in own_places(slot)]
    fill = zip(own, own[1::-1] + own[:1:-1])
    return lax.ppermute(x, ("dp", "layer"), moves + list(fill))


def to_owner(x, slot):
    count = len(slot)
    moves = [(d * count + i, slot[d][i] * count + d) for d in range(count) for i in range(count)]
    return lax.ppermute(x, ("dp", "layer"), moves)


def factor_kernel(scale, margin, label, rows, factor):
    sign = jnp.where(label[0] == 0, 1.0, -1.0)
    factor[...] = sign / ((1.0 + jnp.exp(jnp.full(factor.shape, margin[0], jnp.float32))) * scale)


def shared_scores(own_row, own_block, margin, labels, scale):
    blocks = own_block, swap(own_block)
    rows = jnp.concatenate([own_row, swap(own_row)], axis=0)
    first, second = fetch_pair(rows, FIRST), fetch_pair(rows, SECOND)
    factor = pl.pallas_call(
        functools.partial(factor_kernel, scale),
        out_shape=jax.ShapeDtypeStruct(own_block.shape[:1], jnp.float32),
        in_specs=[pl.BlockSpec(memory_space=pltpu.SMEM)] * 2 + [pl.BlockSpec(memory_space=pl.ANY)],
        out_specs=pl.BlockSpec(memory_space=pltpu.VMEM),
        cost_estimate=pl.CostEstimate(flops=0, bytes_accessed=4 * own_block.shape[0], transcendentals=0),
    )(margin, labels, rows)
    here = lax.axis_index("dp") * len(FIRST) + lax.axis_index("layer")

    def score(got, slot):
        is_own = functools.reduce(jnp.logical_or, [here == d * len(slot) + i for d, i in own_places(slot)])
        return sum(
            jnp.einsum("k,qk->q", jnp.where(is_own, mine, row), block, preferred_element_type=jnp.float32)
            for mine, row, block in zip(rows, got, blocks)
        )

    first, second = to_owner(score(first, FIRST), FIRST), to_owner(score(second, SECOND), SECOND)
    return ((first + second) * factor)[None]


def pair_gradients(acts_in, grads_out, proj_in, proj_out, lengths):
    pair_count, side_count, seq_len, layer_count, _ = acts_in.shape
    in_coords = jnp.einsum("pstld,ldr->pstlr", acts_in, proj_in, preferred_element_type=jnp.float32)
    out_coords = jnp.einsum(
        "pstld,ldr->pstlr", grads_out, proj_out, preferred_element_type=jnp.float32
    )
    position = jnp.arange(seq_len, dtype=jnp.int32)
    live = (position[None, None, :] < lengths[:, :, None]).astype(jnp.float32)
    signs = 1.0 - 2.0 * jnp.arange(side_count, dtype=jnp.float32)
    kron_grads = jnp.einsum("pst,pstlr,pstlk->plrk", live * signs[:, None], out_coords, in_coords)
    return kron_grads.reshape(pair_count, -1).astype(jnp.bfloat16)


def local(acts_in, grads_out, proj_in, proj_out, query_grads, margin, labels, lengths):
    pair_count, side_count, _, layer_count, _ = acts_in.shape
    rank = proj_in.shape[2]
    dp_size, layer_size = lax.axis_size("dp"), lax.axis_size("layer")
    block = query_grads.reshape(query_grads.shape[0], -1)
    one_each = pair_count == layer_count == 1 and side_count == 2
    form = pair_gradient if one_each else pair_gradients
    grad_rows = form(acts_in, grads_out, proj_in, proj_out, lengths)
    scale = rank * math.sqrt(layer_count * layer_size) * math.sqrt(acts_in.shape[2])
    if one_each and dp_size == layer_size == len(FIRST):
        return shared_scores(grad_rows, block, margin, labels, scale)
    factor = jax.nn.sigmoid(-margin) * jnp.where(labels == 0, 1.0, -1.0) / scale
    rows = lax.all_gather(grad_rows, "dp", axis=0, tiled=True)
    scores = jnp.einsum("pk,qk->pq", rows, block, preferred_element_type=jnp.float32)
    scores = lax.all_to_all(scores, "dp", split_axis=0, concat_axis=1, tiled=True)
    summed = lax.psum_scatter(scores, "layer", scatter_dimension=1, tiled=True)
    return summed * factor[:, None]


def solution(mesh):
    placed = (
        P(("groups", "dp"), None, None, "layer", None),
        P(("groups", "dp"), None, None, "layer", None),
        P("layer", None, None),
        P("layer", None, None),
        P("dp", "layer", None),
        P(("groups", "dp")),
        P(("groups", "dp")),
        P(("groups", "dp"), None),
    )
    return jax.shard_map(
        local, mesh=mesh, in_specs=placed, out_specs=P(("groups", "dp"), "layer"), check_vma=False
    )
```

```python
import functools
import math

import jax
import jax.numpy as jnp
from jax import lax
from jax.experimental import pallas as pl
from jax.experimental.pallas import tpu as pltpu
from jax.sharding import PartitionSpec as P

FIRST = ((2, 0, 1, 3), (0, 3, 2, 1), (1, 2, 3, 0), (3, 1, 0, 2))
SECOND = ((3, 1, 2, 0), (1, 2, 0, 3), (0, 3, 1, 2), (2, 0, 3, 1))
CHUNKS = 2


def pair_kernel(seq_len, acts, proj_in, grads, proj_out, lengths, out, *scratch):
    acts_v, pin_v, grads_v, pout_v, kron_v, lengths_s, sems = scratch
    width = acts.shape[1] // CHUNKS
    limits = pltpu.make_async_copy(lengths, lengths_s, sems.at[4 * CHUNKS])
    loads = []
    for pair in (((acts, acts_v), (proj_in, pin_v)), ((grads, grads_v), (proj_out, pout_v))):
        for c in range(CHUNKS):
            part = pl.ds(c * width, width)
            loads.append([
                pltpu.make_async_copy(src.at[:, part], dst.at[:, part], sems.at[2 * len(loads) + i])
                for i, (src, dst) in enumerate(pair)
            ])
    for copies in loads:
        for copy in copies:
            copy.start()
    limits.start()

    def project(left, right, steps):
        total = None
        for c, copies in enumerate(steps):
            for copy in copies:
                copy.wait()
            part = pl.ds(c * width, width)
            term = lax.dot_general(
                left[:, part], right[:, part], (((1,), (1,)), ((), ())), preferred_element_type=jnp.float32
            )
            total = term if total is None else total + term
        return total

    in_coords = project(acts_v, pin_v, loads[:CHUNKS])
    limits.wait()
    token = lax.broadcasted_iota(jnp.int32, in_coords.shape, 0)
    side = token // seq_len
    live = token - side * seq_len < jnp.where(side == 0, lengths_s[0, 0], lengths_s[0, 1])
    weight = jnp.where(live, jnp.where(side == 0, 1.0, -1.0), 0.0)
    in_coords = (in_coords * weight).astype(jnp.bfloat16)
    out_coords = project(pout_v, grads_v, loads[CHUNKS:]).astype(jnp.bfloat16)
    kron_v[...] = jnp.dot(out_coords, in_coords, preferred_element_type=jnp.float32)
    half = kron_v.shape[0] // 2
    rows = jnp.concatenate([kron_v[pl.ds(i, half, stride=2), :] for i in range(2)], axis=1)
    for i in range(half):
        out[:, pl.ds(i * rows.shape[1], rows.shape[1])] = rows[i : i + 1].astype(out.dtype)


def pair_gradient(acts_in, grads_out, proj_in, proj_out, lengths):
    _, sides, seq_len, _, model_width = acts_in.shape
    rank = proj_in.shape[2]
    tokens = sides * seq_len
    anywhere = pl.BlockSpec(memory_space=pl.ANY)
    return pl.pallas_call(
        functools.partial(pair_kernel, seq_len),
        out_shape=jax.ShapeDtypeStruct((1, rank * rank), jnp.bfloat16),
        in_specs=[anywhere] * 5,
        out_specs=pl.BlockSpec(memory_space=pltpu.VMEM),
        scratch_shapes=[
            pltpu.VMEM((tokens, model_width), jnp.bfloat16),
            pltpu.VMEM((rank, model_width), jnp.bfloat16),
            pltpu.VMEM((tokens, model_width), jnp.bfloat16),
            pltpu.VMEM((rank, model_width), jnp.bfloat16),
            pltpu.VMEM((rank, rank), jnp.float32),
            pltpu.SMEM((1, 2), jnp.int32),
            pltpu.SemaphoreType.DMA((4 * CHUNKS + 1,)),
        ],
        compiler_params=pltpu.CompilerParams(vmem_limit_bytes=32 * 1024 * 1024),
        cost_estimate=pl.CostEstimate(
            flops=4 * tokens * model_width * rank,
            bytes_accessed=4 * (tokens + rank) * model_width,
            transcendentals=0,
        ),
    )(
        *(
            pltpu.with_memory_space_constraint(x, pltpu.HBM)
            for x in (
                acts_in.reshape(tokens, model_width),
                jnp.swapaxes(proj_in, 1, 2).reshape(rank, model_width),
                grads_out.reshape(tokens, model_width),
                jnp.swapaxes(proj_out, 1, 2).reshape(rank, model_width),
                lengths,
            )
        )
    )


def swap(x):
    return lax.ppermute(x, "layer", [(i, i ^ 1) for i in range(lax.axis_size("layer"))])


def own_places(slot):
    return [(d, i) for d, row in enumerate(slot) for i, pair in enumerate(row) if pair == d]


def fetch_pair(x, slot):
    count = len(slot)
    moves = [
        (slot[d][i] * count + i, d * count + i) for d in range(count) for i in range(count) if slot[d][i] != d
    ]
    own = [d * count + i for d, i in own_places(slot)]
    fill = zip(own, own[1::-1] + own[:1:-1])
    return lax.ppermute(x, ("dp", "layer"), moves + list(fill))


def to_owner(x, slot):
    count = len(slot)
    moves = [(d * count + i, slot[d][i] * count + d) for d in range(count) for i in range(count)]
    return lax.ppermute(x, ("dp", "layer"), moves)


def factor_kernel(scale, margin, label, rows, factor):
    sign = jnp.where(label[0] == 0, 1.0, -1.0)
    factor[...] = sign / ((1.0 + jnp.exp(jnp.full(factor.shape, margin[0], jnp.float32))) * scale)


def shared_scores(own_row, own_block, margin, labels, scale):
    blocks = own_block, swap(own_block)
    rows = jnp.concatenate([own_row, swap(own_row)], axis=0)
    first, second = fetch_pair(rows, FIRST), fetch_pair(rows, SECOND)
    factor = pl.pallas_call(
        functools.partial(factor_kernel, scale),
        out_shape=jax.ShapeDtypeStruct(own_block.shape[:1], jnp.float32),
        in_specs=[pl.BlockSpec(memory_space=pltpu.SMEM)] * 2 + [pl.BlockSpec(memory_space=pl.ANY)],
        out_specs=pl.BlockSpec(memory_space=pltpu.VMEM),
        compiler_params=pltpu.CompilerParams(vmem_limit_bytes=1024 * 1024),
        cost_estimate=pl.CostEstimate(flops=0, bytes_accessed=4 * own_block.shape[0], transcendentals=0),
    )(margin, labels, rows)
    here = lax.axis_index("dp") * len(FIRST) + lax.axis_index("layer")

    def score(got, slot):
        is_own = functools.reduce(jnp.logical_or, [here == d * len(slot) + i for d, i in own_places(slot)])
        return sum(
            jnp.einsum("k,qk->q", jnp.where(is_own, mine, row), block, preferred_element_type=jnp.float32)
            for mine, row, block in zip(rows, got, blocks)
        )

    first, second = to_owner(score(first, FIRST), FIRST), to_owner(score(second, SECOND), SECOND)
    return ((first + second) * factor)[None]


def pair_gradients(acts_in, grads_out, proj_in, proj_out, lengths):
    pair_count, side_count, seq_len, layer_count, _ = acts_in.shape
    in_coords = jnp.einsum("pstld,ldr->pstlr", acts_in, proj_in, preferred_element_type=jnp.float32)
    out_coords = jnp.einsum(
        "pstld,ldr->pstlr", grads_out, proj_out, preferred_element_type=jnp.float32
    )
    position = jnp.arange(seq_len, dtype=jnp.int32)
    live = (position[None, None, :] < lengths[:, :, None]).astype(jnp.float32)
    signs = 1.0 - 2.0 * jnp.arange(side_count, dtype=jnp.float32)
    kron_grads = jnp.einsum("pst,pstlr,pstlk->plrk", live * signs[:, None], out_coords, in_coords)
    return kron_grads.reshape(pair_count, -1).astype(jnp.bfloat16)


def local(acts_in, grads_out, proj_in, proj_out, query_grads, margin, labels, lengths):
    pair_count, side_count, _, layer_count, _ = acts_in.shape
    rank = proj_in.shape[2]
    dp_size, layer_size = lax.axis_size("dp"), lax.axis_size("layer")
    block = query_grads.reshape(query_grads.shape[0], -1)
    one_each = pair_count == layer_count == 1 and side_count == 2
    form = pair_gradient if one_each else pair_gradients
    grad_rows = form(acts_in, grads_out, proj_in, proj_out, lengths)
    scale = rank * math.sqrt(layer_count * layer_size) * math.sqrt(acts_in.shape[2])
    if one_each and dp_size == layer_size == len(FIRST):
        return shared_scores(grad_rows, block, margin, labels, scale)
    factor = jax.nn.sigmoid(-margin) * jnp.where(labels == 0, 1.0, -1.0) / scale
    rows = lax.all_gather(grad_rows, "dp", axis=0, tiled=True)
    scores = jnp.einsum("pk,qk->pq", rows, block, preferred_element_type=jnp.float32)
    scores = lax.all_to_all(scores, "dp", split_axis=0, concat_axis=1, tiled=True)
    summed = lax.psum_scatter(scores, "layer", scatter_dimension=1, tiled=True)
    return summed * factor[:, None]


def solution(mesh):
    placed = (
        P(("groups", "dp"), None, None, "layer", None),
        P(("groups", "dp"), None, None, "layer", None),
        P("layer", None, None),
        P("layer", None, None),
        P("dp", "layer", None),
        P(("groups", "dp")),
        P(("groups", "dp")),
        P(("groups", "dp"), None),
    )
    return jax.shard_map(
        local, mesh=mesh, in_specs=placed, out_specs=P(("groups", "dp"), "layer"), check_vma=False
    )
```

```python
import functools
import math

import jax
import jax.numpy as jnp
from jax import lax
from jax.experimental import pallas as pl
from jax.experimental.pallas import tpu as pltpu
from jax.sharding import PartitionSpec as P

FIRST = ((2, 0, 1, 3), (0, 3, 2, 1), (1, 2, 3, 0), (3, 1, 0, 2))
SECOND = ((3, 1, 2, 0), (1, 2, 0, 3), (0, 3, 1, 2), (2, 0, 3, 1))
CHUNKS = 4


def pair_kernel(seq_len, acts, grads, proj_in, proj_out, lengths, out, *scratch):
    tokens_v, proj_v, kron_v, lengths_s, sems, lengths_sem = scratch
    tokens, model_width = acts.shape
    rank = proj_in.shape[0]
    width = model_width // CHUNKS
    limits = pltpu.make_async_copy(lengths, lengths_s, lengths_sem)
    loads = [
        [
            pltpu.make_async_copy(
                src.at[:, pl.ds(c * width, width)],
                dst.at[pl.ds(half * src.shape[0], src.shape[0]), pl.ds(c * width, width)],
                sems.at[c, 2 * half + i],
            )
            for half, pair in enumerate(((acts, proj_in), (grads, proj_out)))
            for i, (src, dst) in enumerate(zip(pair, (tokens_v, proj_v)))
        ]
        for c in range(CHUNKS)
    ]
    for copies in loads:
        for copy in copies:
            copy.start()
    limits.start()
    coords = None
    for c, copies in enumerate(loads):
        for copy in copies:
            copy.wait()
        part = pl.ds(c * width, width)
        term = lax.dot_general(
            proj_v[:, part], tokens_v[:, part], (((1,), (1,)), ((), ())), preferred_element_type=jnp.float32
        )
        coords = term if coords is None else coords + term
    limits.wait()
    token = lax.broadcasted_iota(jnp.int32, (1, tokens), 1)
    side = token // seq_len
    live = token - side * seq_len < jnp.where(side == 0, lengths_s[0, 0], lengths_s[0, 1])
    weight = jnp.where(live, jnp.where(side == 0, 1.0, -1.0), 0.0)
    in_coords = (coords[:rank, :tokens] * weight).astype(jnp.bfloat16)
    out_coords = coords[rank:, tokens:].astype(jnp.bfloat16)
    kron_v[...] = lax.dot_general(
        out_coords, in_coords, (((1,), (1,)), ((), ())), preferred_element_type=jnp.float32
    )
    half = rank // 2
    rows = jnp.concatenate([kron_v[pl.ds(i, half, stride=2), :] for i in range(2)], axis=1)
    for i in range(half):
        out[:, pl.ds(i * rows.shape[1], rows.shape[1])] = rows[i : i + 1].astype(out.dtype)


def pair_gradient(acts_in, grads_out, proj_in, proj_out, lengths):
    _, sides, seq_len, _, model_width = acts_in.shape
    rank = proj_in.shape[2]
    tokens = sides * seq_len
    return pl.pallas_call(
        functools.partial(pair_kernel, seq_len),
        out_shape=jax.ShapeDtypeStruct((1, rank * rank), jnp.bfloat16),
        in_specs=[pl.BlockSpec(memory_space=pl.ANY)] * 5,
        out_specs=pl.BlockSpec(memory_space=pltpu.VMEM),
        scratch_shapes=[
            pltpu.VMEM((2 * tokens, model_width), jnp.bfloat16),
            pltpu.VMEM((2 * rank, model_width), jnp.bfloat16),
            pltpu.VMEM((rank, rank), jnp.float32),
            pltpu.SMEM((1, 2), jnp.int32),
            pltpu.SemaphoreType.DMA((CHUNKS, 4)),
            pltpu.SemaphoreType.DMA,
        ],
        compiler_params=pltpu.CompilerParams(vmem_limit_bytes=32 * 1024 * 1024),
        cost_estimate=pl.CostEstimate(
            flops=4 * tokens * model_width * rank,
            bytes_accessed=4 * (tokens + rank) * model_width,
            transcendentals=0,
        ),
    )(
        *(
            pltpu.with_memory_space_constraint(x, pltpu.HBM)
            for x in (
                acts_in.reshape(tokens, model_width),
                grads_out.reshape(tokens, model_width),
                jnp.swapaxes(proj_in, 1, 2).reshape(rank, model_width),
                jnp.swapaxes(proj_out, 1, 2).reshape(rank, model_width),
                lengths,
            )
        )
    )


def swap(x):
    return lax.ppermute(x, "layer", [(i, i ^ 1) for i in range(lax.axis_size("layer"))])


def own_places(slot):
    return [(d, i) for d, row in enumerate(slot) for i, pair in enumerate(row) if pair == d]


def fetch_pair(x, slot):
    count = len(slot)
    moves = [
        (slot[d][i] * count + i, d * count + i) for d in range(count) for i in range(count) if slot[d][i] != d
    ]
    own = [d * count + i for d, i in own_places(slot)]
    fill = zip(own, own[1::-1] + own[:1:-1])
    return lax.ppermute(x, ("dp", "layer"), moves + list(fill))


def to_owner(x, slot):
    count = len(slot)
    moves = [(d * count + i, slot[d][i] * count + d) for d in range(count) for i in range(count)]
    return lax.ppermute(x, ("dp", "layer"), moves)


def factor_kernel(scale, margin, label, rows, factor):
    sign = jnp.where(label[0] == 0, 1.0, -1.0)
    factor[...] = sign / ((1.0 + jnp.exp(jnp.full(factor.shape, margin[0], jnp.float32))) * scale)


def shared_scores(own_row, own_block, margin, labels, scale):
    blocks = own_block, swap(own_block)
    rows = jnp.concatenate([own_row, swap(own_row)], axis=0)
    first, second = fetch_pair(rows, FIRST), fetch_pair(rows, SECOND)
    factor = pl.pallas_call(
        functools.partial(factor_kernel, scale),
        out_shape=jax.ShapeDtypeStruct(own_block.shape[:1], jnp.float32),
        in_specs=[pl.BlockSpec(memory_space=pltpu.SMEM)] * 2 + [pl.BlockSpec(memory_space=pl.ANY)],
        out_specs=pl.BlockSpec(memory_space=pltpu.VMEM),
        compiler_params=pltpu.CompilerParams(vmem_limit_bytes=1024 * 1024),
        cost_estimate=pl.CostEstimate(flops=0, bytes_accessed=4 * own_block.shape[0], transcendentals=0),
    )(margin, labels, rows)
    here = lax.axis_index("dp") * len(FIRST) + lax.axis_index("layer")

    def score(got, slot):
        is_own = functools.reduce(jnp.logical_or, [here == d * len(slot) + i for d, i in own_places(slot)])
        return sum(
            jnp.einsum("k,qk->q", jnp.where(is_own, mine, row), block, preferred_element_type=jnp.float32)
            for mine, row, block in zip(rows, got, blocks)
        )

    first, second = to_owner(score(first, FIRST), FIRST), to_owner(score(second, SECOND), SECOND)
    return ((first + second) * factor)[None]


def pair_gradients(acts_in, grads_out, proj_in, proj_out, lengths):
    pair_count, side_count, seq_len, layer_count, _ = acts_in.shape
    in_coords = jnp.einsum("pstld,ldr->pstlr", acts_in, proj_in, preferred_element_type=jnp.float32)
    out_coords = jnp.einsum(
        "pstld,ldr->pstlr", grads_out, proj_out, preferred_element_type=jnp.float32
    )
    position = jnp.arange(seq_len, dtype=jnp.int32)
    live = (position[None, None, :] < lengths[:, :, None]).astype(jnp.float32)
    signs = 1.0 - 2.0 * jnp.arange(side_count, dtype=jnp.float32)
    kron_grads = jnp.einsum("pst,pstlr,pstlk->plrk", live * signs[:, None], out_coords, in_coords)
    return kron_grads.reshape(pair_count, -1).astype(jnp.bfloat16)


def local(acts_in, grads_out, proj_in, proj_out, query_grads, margin, labels, lengths):
    pair_count, side_count, _, layer_count, _ = acts_in.shape
    rank = proj_in.shape[2]
    dp_size, layer_size = lax.axis_size("dp"), lax.axis_size("layer")
    block = query_grads.reshape(query_grads.shape[0], -1)
    one_each = pair_count == layer_count == 1 and side_count == 2
    form = pair_gradient if one_each else pair_gradients
    grad_rows = form(acts_in, grads_out, proj_in, proj_out, lengths)
    scale = rank * math.sqrt(layer_count * layer_size) * math.sqrt(acts_in.shape[2])
    if one_each and dp_size == layer_size == len(FIRST):
        return shared_scores(grad_rows, block, margin, labels, scale)
    factor = jax.nn.sigmoid(-margin) * jnp.where(labels == 0, 1.0, -1.0) / scale
    rows = lax.all_gather(grad_rows, "dp", axis=0, tiled=True)
    scores = jnp.einsum("pk,qk->pq", rows, block, preferred_element_type=jnp.float32)
    scores = lax.all_to_all(scores, "dp", split_axis=0, concat_axis=1, tiled=True)
    summed = lax.psum_scatter(scores, "layer", scatter_dimension=1, tiled=True)
    return summed * factor[:, None]


def solution(mesh):
    placed = (
        P(("groups", "dp"), None, None, "layer", None),
        P(("groups", "dp"), None, None, "layer", None),
        P("layer", None, None),
        P("layer", None, None),
        P("dp", "layer", None),
        P(("groups", "dp")),
        P(("groups", "dp")),
        P(("groups", "dp"), None),
    )
    return jax.shard_map(
        local, mesh=mesh, in_specs=placed, out_specs=P(("groups", "dp"), "layer"), check_vma=False
    )
```

```python
import functools
import math

import jax
import jax.numpy as jnp
from jax import lax
from jax.experimental import pallas as pl
from jax.experimental.pallas import tpu as pltpu
from jax.sharding import PartitionSpec as P

FIRST = ((2, 0, 1, 3), (0, 3, 2, 1), (1, 2, 3, 0), (3, 1, 0, 2))
SECOND = ((3, 1, 2, 0), (1, 2, 0, 3), (0, 3, 1, 2), (2, 0, 3, 1))
CHUNKS = 2


def pair_kernel(seq_len, acts, grads, proj_in, proj_out, lengths, out, *scratch):
    tokens_v, proj_v, kron_v, lengths_s, sems, lengths_sem = scratch
    tokens, model_width = acts.shape
    rank = proj_in.shape[0]
    width = model_width // CHUNKS
    limits = pltpu.make_async_copy(lengths, lengths_s, lengths_sem)
    loads = [
        [
            pltpu.make_async_copy(
                src.at[:, pl.ds(c * width, width)],
                dst.at[pl.ds(half * src.shape[0], src.shape[0]), pl.ds(c * width, width)],
                sems.at[c, 2 * half + i],
            )
            for half, pair in enumerate(((acts, proj_in), (grads, proj_out)))
            for i, (src, dst) in enumerate(zip(pair, (tokens_v, proj_v)))
        ]
        for c in range(CHUNKS)
    ]
    for copies in loads:
        for copy in copies:
            copy.start()
    limits.start()
    coords = None
    for c, copies in enumerate(loads):
        for copy in copies:
            copy.wait()
        part = pl.ds(c * width, width)
        term = lax.dot_general(
            tokens_v[:, part], proj_v[:, part], (((1,), (1,)), ((), ())), preferred_element_type=jnp.float32
        )
        coords = term if coords is None else coords + term
    limits.wait()
    token = lax.broadcasted_iota(jnp.int32, (tokens, 1), 0)
    side = token // seq_len
    live = token - side * seq_len < jnp.where(side == 0, lengths_s[0, 0], lengths_s[0, 1])
    weight = jnp.where(live, jnp.where(side == 0, 1.0, -1.0), 0.0)
    in_coords = (coords[:tokens, :rank] * weight).astype(jnp.bfloat16)
    out_coords = coords[tokens:, rank:].astype(jnp.bfloat16)
    kron_v[...] = lax.dot_general(
        out_coords, in_coords, (((0,), (0,)), ((), ())), preferred_element_type=jnp.float32
    )
    half = rank // 2
    rows = jnp.concatenate([kron_v[pl.ds(i, half, stride=2), :] for i in range(2)], axis=1)
    for i in range(half):
        out[:, pl.ds(i * rows.shape[1], rows.shape[1])] = rows[i : i + 1].astype(out.dtype)


def pair_gradient(acts_in, grads_out, proj_in, proj_out, lengths):
    _, sides, seq_len, _, model_width = acts_in.shape
    rank = proj_in.shape[2]
    tokens = sides * seq_len
    return pl.pallas_call(
        functools.partial(pair_kernel, seq_len),
        out_shape=jax.ShapeDtypeStruct((1, rank * rank), jnp.bfloat16),
        in_specs=[pl.BlockSpec(memory_space=pl.ANY)] * 5,
        out_specs=pl.BlockSpec(memory_space=pltpu.VMEM),
        scratch_shapes=[
            pltpu.VMEM((2 * tokens, model_width), jnp.bfloat16),
            pltpu.VMEM((2 * rank, model_width), jnp.bfloat16),
            pltpu.VMEM((rank, rank), jnp.float32),
            pltpu.SMEM((1, 2), jnp.int32),
            pltpu.SemaphoreType.DMA((CHUNKS, 4)),
            pltpu.SemaphoreType.DMA,
        ],
        compiler_params=pltpu.CompilerParams(vmem_limit_bytes=32 * 1024 * 1024),
        cost_estimate=pl.CostEstimate(
            flops=4 * tokens * model_width * rank,
            bytes_accessed=4 * (tokens + rank) * model_width,
            transcendentals=0,
        ),
    )(
        *(
            pltpu.with_memory_space_constraint(x, pltpu.HBM)
            for x in (
                acts_in.reshape(tokens, model_width),
                grads_out.reshape(tokens, model_width),
                jnp.swapaxes(proj_in, 1, 2).reshape(rank, model_width),
                jnp.swapaxes(proj_out, 1, 2).reshape(rank, model_width),
                lengths,
            )
        )
    )


def swap(x):
    return lax.ppermute(x, "layer", [(i, i ^ 1) for i in range(lax.axis_size("layer"))])


def own_places(slot):
    return [(d, i) for d, row in enumerate(slot) for i, pair in enumerate(row) if pair == d]


def fetch_pair(x, slot):
    count = len(slot)
    moves = [
        (slot[d][i] * count + i, d * count + i) for d in range(count) for i in range(count) if slot[d][i] != d
    ]
    own = [d * count + i for d, i in own_places(slot)]
    fill = zip(own, own[1::-1] + own[:1:-1])
    return lax.ppermute(x, ("dp", "layer"), moves + list(fill))


def to_owner(x, slot):
    count = len(slot)
    moves = [(d * count + i, slot[d][i] * count + d) for d in range(count) for i in range(count)]
    return lax.ppermute(x, ("dp", "layer"), moves)


def factor_kernel(scale, margin, label, rows, factor):
    sign = jnp.where(label[0] == 0, 1.0, -1.0)
    factor[...] = sign / ((1.0 + jnp.exp(jnp.full(factor.shape, margin[0], jnp.float32))) * scale)


def shared_scores(own_row, own_block, margin, labels, scale):
    blocks = own_block, swap(own_block)
    rows = jnp.concatenate([own_row, swap(own_row)], axis=0)
    first, second = fetch_pair(rows, FIRST), fetch_pair(rows, SECOND)
    factor = pl.pallas_call(
        functools.partial(factor_kernel, scale),
        out_shape=jax.ShapeDtypeStruct(own_block.shape[:1], jnp.float32),
        in_specs=[pl.BlockSpec(memory_space=pltpu.SMEM)] * 2 + [pl.BlockSpec(memory_space=pl.ANY)],
        out_specs=pl.BlockSpec(memory_space=pltpu.VMEM),
        compiler_params=pltpu.CompilerParams(vmem_limit_bytes=1024 * 1024),
        cost_estimate=pl.CostEstimate(flops=0, bytes_accessed=4 * own_block.shape[0], transcendentals=0),
    )(margin, labels, rows)
    here = lax.axis_index("dp") * len(FIRST) + lax.axis_index("layer")

    def score(got, slot):
        is_own = functools.reduce(jnp.logical_or, [here == d * len(slot) + i for d, i in own_places(slot)])
        return sum(
            jnp.einsum("k,qk->q", jnp.where(is_own, mine, row), block, preferred_element_type=jnp.float32)
            for mine, row, block in zip(rows, got, blocks)
        )

    first, second = to_owner(score(first, FIRST), FIRST), to_owner(score(second, SECOND), SECOND)
    return ((first + second) * factor)[None]


def pair_gradients(acts_in, grads_out, proj_in, proj_out, lengths):
    pair_count, side_count, seq_len, layer_count, _ = acts_in.shape
    in_coords = jnp.einsum("pstld,ldr->pstlr", acts_in, proj_in, preferred_element_type=jnp.float32)
    out_coords = jnp.einsum(
        "pstld,ldr->pstlr", grads_out, proj_out, preferred_element_type=jnp.float32
    )
    position = jnp.arange(seq_len, dtype=jnp.int32)
    live = (position[None, None, :] < lengths[:, :, None]).astype(jnp.float32)
    signs = 1.0 - 2.0 * jnp.arange(side_count, dtype=jnp.float32)
    kron_grads = jnp.einsum("pst,pstlr,pstlk->plrk", live * signs[:, None], out_coords, in_coords)
    return kron_grads.reshape(pair_count, -1).astype(jnp.bfloat16)


def local(acts_in, grads_out, proj_in, proj_out, query_grads, margin, labels, lengths):
    pair_count, side_count, _, layer_count, _ = acts_in.shape
    rank = proj_in.shape[2]
    dp_size, layer_size = lax.axis_size("dp"), lax.axis_size("layer")
    block = query_grads.reshape(query_grads.shape[0], -1)
    one_each = pair_count == layer_count == 1 and side_count == 2
    form = pair_gradient if one_each else pair_gradients
    grad_rows = form(acts_in, grads_out, proj_in, proj_out, lengths)
    scale = rank * math.sqrt(layer_count * layer_size) * math.sqrt(acts_in.shape[2])
    if one_each and dp_size == layer_size == len(FIRST):
        return shared_scores(grad_rows, block, margin, labels, scale)
    factor = jax.nn.sigmoid(-margin) * jnp.where(labels == 0, 1.0, -1.0) / scale
    rows = lax.all_gather(grad_rows, "dp", axis=0, tiled=True)
    scores = jnp.einsum("pk,qk->pq", rows, block, preferred_element_type=jnp.float32)
    scores = lax.all_to_all(scores, "dp", split_axis=0, concat_axis=1, tiled=True)
    summed = lax.psum_scatter(scores, "layer", scatter_dimension=1, tiled=True)
    return summed * factor[:, None]


def solution(mesh):
    placed = (
        P(("groups", "dp"), None, None, "layer", None),
        P(("groups", "dp"), None, None, "layer", None),
        P("layer", None, None),
        P("layer", None, None),
        P("dp", "layer", None),
        P(("groups", "dp")),
        P(("groups", "dp")),
        P(("groups", "dp"), None),
    )
    return jax.shard_map(
        local, mesh=mesh, in_specs=placed, out_specs=P(("groups", "dp"), "layer"), check_vma=False
    )
```

```python
import functools
import math

import jax
import jax.numpy as jnp
from jax import lax
from jax.experimental import pallas as pl
from jax.experimental.pallas import tpu as pltpu
from jax.sharding import PartitionSpec as P

FIRST = ((3, 0, 2, 1), (1, 2, 0, 3), (0, 3, 1, 2), (2, 1, 3, 0))
SECOND = ((2, 1, 0, 3), (0, 3, 2, 1), (1, 2, 3, 0), (3, 0, 1, 2))
CHUNKS = 2


def pair_kernel(seq_len, acts, grads, proj_in, proj_out, lengths, out, *scratch):
    tokens_v, proj_v, kron_v, lengths_s, sems, lengths_sem = scratch
    tokens, model_width = acts.shape
    rank = proj_in.shape[0]
    width = model_width // CHUNKS
    limits = pltpu.make_async_copy(lengths, lengths_s, lengths_sem)
    loads = [
        [
            pltpu.make_async_copy(
                src.at[:, pl.ds(c * width, width)],
                dst.at[pl.ds(half * src.shape[0], src.shape[0]), pl.ds(c * width, width)],
                sems.at[c, 2 * half + i],
            )
            for half, pair in enumerate(((acts, proj_in), (grads, proj_out)))
            for i, (src, dst) in enumerate(zip(pair, (tokens_v, proj_v)))
        ]
        for c in range(CHUNKS)
    ]
    for copies in loads:
        for copy in copies:
            copy.start()
    limits.start()
    coords = None
    for c, copies in enumerate(loads):
        for copy in copies:
            copy.wait()
        part = pl.ds(c * width, width)
        term = lax.dot_general(
            tokens_v[:, part], proj_v[:, part], (((1,), (1,)), ((), ())), preferred_element_type=jnp.float32
        )
        coords = term if coords is None else coords + term
    limits.wait()
    token = lax.broadcasted_iota(jnp.int32, (tokens, 1), 0)
    side = token // seq_len
    live = token - side * seq_len < jnp.where(side == 0, lengths_s[0, 0], lengths_s[0, 1])
    weight = jnp.where(live, jnp.where(side == 0, 1.0, -1.0), 0.0)
    in_coords = (coords[:tokens, :rank] * weight).astype(jnp.bfloat16)
    out_coords = coords[tokens:, rank:].astype(jnp.bfloat16)
    kron_v[...] = lax.dot_general(
        out_coords, in_coords, (((0,), (0,)), ((), ())), preferred_element_type=jnp.float32
    )
    half = rank // 2
    rows = jnp.concatenate([kron_v[pl.ds(i, half, stride=2), :] for i in range(2)], axis=1)
    for i in range(half):
        out[:, pl.ds(i * rows.shape[1], rows.shape[1])] = rows[i : i + 1].astype(out.dtype)


def pair_gradient(acts_in, grads_out, proj_in, proj_out, lengths):
    _, sides, seq_len, _, model_width = acts_in.shape
    rank = proj_in.shape[2]
    tokens = sides * seq_len
    return pl.pallas_call(
        functools.partial(pair_kernel, seq_len),
        out_shape=jax.ShapeDtypeStruct((1, rank * rank), jnp.bfloat16),
        in_specs=[pl.BlockSpec(memory_space=pl.ANY)] * 5,
        out_specs=pl.BlockSpec(memory_space=pltpu.VMEM),
        scratch_shapes=[
            pltpu.VMEM((2 * tokens, model_width), jnp.bfloat16),
            pltpu.VMEM((2 * rank, model_width), jnp.bfloat16),
            pltpu.VMEM((rank, rank), jnp.float32),
            pltpu.SMEM((1, 2), jnp.int32),
            pltpu.SemaphoreType.DMA((CHUNKS, 4)),
            pltpu.SemaphoreType.DMA,
        ],
        compiler_params=pltpu.CompilerParams(vmem_limit_bytes=32 * 1024 * 1024),
        cost_estimate=pl.CostEstimate(
            flops=4 * tokens * model_width * rank,
            bytes_accessed=4 * (tokens + rank) * model_width,
            transcendentals=0,
        ),
    )(
        *(
            pltpu.with_memory_space_constraint(x, pltpu.HBM)
            for x in (
                acts_in.reshape(tokens, model_width),
                grads_out.reshape(tokens, model_width),
                jnp.swapaxes(proj_in, 1, 2).reshape(rank, model_width),
                jnp.swapaxes(proj_out, 1, 2).reshape(rank, model_width),
                lengths,
            )
        )
    )


def swap(x):
    return lax.ppermute(x, "layer", [(i, i ^ 1) for i in range(lax.axis_size("layer"))])


def own_places(slot):
    return [(d, i) for d, row in enumerate(slot) for i, pair in enumerate(row) if pair == d]


def fetch_pair(x, slot):
    count = len(slot)
    moves = [
        (slot[d][i] * count + i, d * count + i) for d in range(count) for i in range(count) if slot[d][i] != d
    ]
    return lax.ppermute(x, ("dp", "layer"), moves)


def to_owner(x, slot):
    count = len(slot)
    moves = [(d * count + i, slot[d][i] * count + d) for d in range(count) for i in range(count)]
    return lax.ppermute(x, ("dp", "layer"), moves)


def factor_kernel(scale, margin, label, rows, factor):
    sign = jnp.where(label[0] == 0, 1.0, -1.0)
    factor[...] = sign / ((1.0 + jnp.exp(jnp.full(factor.shape, margin[0], jnp.float32))) * scale)


def shared_scores(own_row, own_block, margin, labels, scale):
    blocks = own_block, swap(own_block)
    rows = jnp.concatenate([own_row, swap(own_row)], axis=0)
    first, second = fetch_pair(rows, FIRST), fetch_pair(rows, SECOND)
    factor = pl.pallas_call(
        functools.partial(factor_kernel, scale),
        out_shape=jax.ShapeDtypeStruct(own_block.shape[:1], jnp.float32),
        in_specs=[pl.BlockSpec(memory_space=pltpu.SMEM)] * 2 + [pl.BlockSpec(memory_space=pl.ANY)],
        out_specs=pl.BlockSpec(memory_space=pltpu.VMEM),
        compiler_params=pltpu.CompilerParams(vmem_limit_bytes=1024 * 1024),
        cost_estimate=pl.CostEstimate(flops=0, bytes_accessed=4 * own_block.shape[0], transcendentals=0),
    )(margin, labels, rows)
    here = lax.axis_index("dp") * len(FIRST) + lax.axis_index("layer")

    def score(got, slot):
        is_own = functools.reduce(jnp.logical_or, [here == d * len(slot) + i for d, i in own_places(slot)])
        return sum(
            jnp.einsum("k,qk->q", jnp.where(is_own, mine, row), block, preferred_element_type=jnp.float32)
            for mine, row, block in zip(rows, got, blocks)
        )

    first, second = to_owner(score(first, FIRST), FIRST), to_owner(score(second, SECOND), SECOND)
    return ((first + second) * factor)[None]


def pair_gradients(acts_in, grads_out, proj_in, proj_out, lengths):
    pair_count, side_count, seq_len, layer_count, _ = acts_in.shape
    in_coords = jnp.einsum("pstld,ldr->pstlr", acts_in, proj_in, preferred_element_type=jnp.float32)
    out_coords = jnp.einsum(
        "pstld,ldr->pstlr", grads_out, proj_out, preferred_element_type=jnp.float32
    )
    position = jnp.arange(seq_len, dtype=jnp.int32)
    live = (position[None, None, :] < lengths[:, :, None]).astype(jnp.float32)
    signs = 1.0 - 2.0 * jnp.arange(side_count, dtype=jnp.float32)
    kron_grads = jnp.einsum("pst,pstlr,pstlk->plrk", live * signs[:, None], out_coords, in_coords)
    return kron_grads.reshape(pair_count, -1).astype(jnp.bfloat16)


def local(acts_in, grads_out, proj_in, proj_out, query_grads, margin, labels, lengths):
    pair_count, side_count, _, layer_count, _ = acts_in.shape
    rank = proj_in.shape[2]
    dp_size, layer_size = lax.axis_size("dp"), lax.axis_size("layer")
    block = query_grads.reshape(query_grads.shape[0], -1)
    one_each = pair_count == layer_count == 1 and side_count == 2
    form = pair_gradient if one_each else pair_gradients
    grad_rows = form(acts_in, grads_out, proj_in, proj_out, lengths)
    scale = rank * math.sqrt(layer_count * layer_size) * math.sqrt(acts_in.shape[2])
    if one_each and dp_size == layer_size == len(FIRST):
        return shared_scores(grad_rows, block, margin, labels, scale)
    factor = jax.nn.sigmoid(-margin) * jnp.where(labels == 0, 1.0, -1.0) / scale
    rows = lax.all_gather(grad_rows, "dp", axis=0, tiled=True)
    scores = jnp.einsum("pk,qk->pq", rows, block, preferred_element_type=jnp.float32)
    scores = lax.all_to_all(scores, "dp", split_axis=0, concat_axis=1, tiled=True)
    summed = lax.psum_scatter(scores, "layer", scatter_dimension=1, tiled=True)
    return summed * factor[:, None]


def solution(mesh):
    placed = (
        P(("groups", "dp"), None, None, "layer", None),
        P(("groups", "dp"), None, None, "layer", None),
        P("layer", None, None),
        P("layer", None, None),
        P("dp", "layer", None),
        P(("groups", "dp")),
        P(("groups", "dp")),
        P(("groups", "dp"), None),
    )
    return jax.shard_map(
        local, mesh=mesh, in_specs=placed, out_specs=P(("groups", "dp"), "layer"), check_vma=False
    )
```

```python
import functools
import math

import jax
import jax.numpy as jnp
from jax import lax
from jax.experimental import pallas as pl
from jax.experimental.pallas import tpu as pltpu
from jax.sharding import PartitionSpec as P

FIRST = ((2, 0, 1, 3), (0, 3, 2, 1), (1, 2, 3, 0), (3, 1, 0, 2))
SECOND = ((3, 1, 2, 0), (1, 2, 0, 3), (0, 3, 1, 2), (2, 0, 3, 1))
CHUNKS = 4


def pair_kernel(seq_len, acts, grads, proj_in, proj_out, lengths, out, *scratch):
    tokens_v, proj_v, kron_v, lengths_s, sems, lengths_sem = scratch
    tokens, model_width = acts.shape
    rank = proj_in.shape[0]
    width = model_width // CHUNKS
    limits = pltpu.make_async_copy(lengths, lengths_s, lengths_sem)
    loads = [
        [
            pltpu.make_async_copy(
                src.at[:, pl.ds(c * width, width)],
                dst.at[pl.ds(half * src.shape[0], src.shape[0]), pl.ds(c * width, width)],
                sems.at[c, 2 * half + i],
            )
            for half, pair in enumerate(((acts, proj_in), (grads, proj_out)))
            for i, (src, dst) in enumerate(zip(pair, (tokens_v, proj_v)))
        ]
        for c in range(CHUNKS)
    ]
    limits.start()
    for copies in loads:
        for copy in copies:
            copy.start()
    limits.wait()
    token = lax.broadcasted_iota(jnp.int32, (tokens, 1), 0)
    side = token // seq_len
    live = token - side * seq_len < jnp.where(side == 0, lengths_s[0, 0], lengths_s[0, 1])
    weight = jnp.where(live, jnp.where(side == 0, 1.0, -1.0), 0.0)
    coords = None
    for c, copies in enumerate(loads):
        for copy in copies:
            copy.wait()
        part = pl.ds(c * width, width)
        term = lax.dot_general(
            tokens_v[:, part], proj_v[:, part], (((1,), (1,)), ((), ())), preferred_element_type=jnp.float32
        )
        coords = term if coords is None else coords + term
    in_coords = (coords[:tokens, :rank] * weight).astype(jnp.bfloat16)
    out_coords = coords[tokens:, rank:].astype(jnp.bfloat16)
    kron_v[...] = lax.dot_general(
        out_coords, in_coords, (((0,), (0,)), ((), ())), preferred_element_type=jnp.float32
    )
    half = rank // 2
    rows = jnp.concatenate([kron_v[pl.ds(i, half, stride=2), :] for i in range(2)], axis=1)
    for i in range(half):
        out[:, pl.ds(i * rows.shape[1], rows.shape[1])] = rows[i : i + 1].astype(out.dtype)


def pair_gradient(acts_in, grads_out, proj_in, proj_out, lengths):
    _, sides, seq_len, _, model_width = acts_in.shape
    rank = proj_in.shape[2]
    tokens = sides * seq_len
    return pl.pallas_call(
        functools.partial(pair_kernel, seq_len),
        out_shape=jax.ShapeDtypeStruct((1, rank * rank), jnp.bfloat16),
        in_specs=[pl.BlockSpec(memory_space=pl.ANY)] * 5,
        out_specs=pl.BlockSpec(memory_space=pltpu.VMEM),
        scratch_shapes=[
            pltpu.VMEM((2 * tokens, model_width), jnp.bfloat16),
            pltpu.VMEM((2 * rank, model_width), jnp.bfloat16),
            pltpu.VMEM((rank, rank), jnp.float32),
            pltpu.SMEM((1, 2), jnp.int32),
            pltpu.SemaphoreType.DMA((CHUNKS, 4)),
            pltpu.SemaphoreType.DMA,
        ],
        compiler_params=pltpu.CompilerParams(vmem_limit_bytes=32 * 1024 * 1024),
        cost_estimate=pl.CostEstimate(
            flops=4 * tokens * model_width * rank,
            bytes_accessed=4 * (tokens + rank) * model_width,
            transcendentals=0,
        ),
    )(
        *(
            pltpu.with_memory_space_constraint(x, pltpu.HBM)
            for x in (
                acts_in.reshape(tokens, model_width),
                grads_out.reshape(tokens, model_width),
                jnp.swapaxes(proj_in, 1, 2).reshape(rank, model_width),
                jnp.swapaxes(proj_out, 1, 2).reshape(rank, model_width),
                lengths,
            )
        )
    )


def swap(x):
    return lax.ppermute(x, "layer", [(i, i ^ 1) for i in range(lax.axis_size("layer"))])


def own_places(slot):
    return [(d, i) for d, row in enumerate(slot) for i, pair in enumerate(row) if pair == d]


def fetch_pair(x, slot):
    count = len(slot)
    moves = [
        (slot[d][i] * count + i, d * count + i) for d in range(count) for i in range(count) if slot[d][i] != d
    ]
    own = [d * count + i for d, i in own_places(slot)]
    fill = zip(own, own[1::-1] + own[:1:-1])
    return lax.ppermute(x, ("dp", "layer"), moves + list(fill))


def to_owner(x, slot):
    count = len(slot)
    moves = [(d * count + i, slot[d][i] * count + d) for d in range(count) for i in range(count)]
    return lax.ppermute(x, ("dp", "layer"), moves)


def factor_kernel(scale, margin, label, rows, factor):
    sign = jnp.where(label[0] == 0, 1.0, -1.0)
    factor[...] = sign / ((1.0 + jnp.exp(jnp.full(factor.shape, margin[0], jnp.float32))) * scale)


def shared_scores(own_row, own_block, margin, labels, scale):
    blocks = own_block, swap(own_block)
    rows = jnp.concatenate([own_row, swap(own_row)], axis=0)
    first, second = fetch_pair(rows, FIRST), fetch_pair(rows, SECOND)
    factor = pl.pallas_call(
        functools.partial(factor_kernel, scale),
        out_shape=jax.ShapeDtypeStruct(own_block.shape[:1], jnp.float32),
        in_specs=[pl.BlockSpec(memory_space=pltpu.SMEM)] * 2 + [pl.BlockSpec(memory_space=pl.ANY)],
        out_specs=pl.BlockSpec(memory_space=pltpu.VMEM),
        compiler_params=pltpu.CompilerParams(vmem_limit_bytes=1024 * 1024),
        cost_estimate=pl.CostEstimate(flops=0, bytes_accessed=4 * own_block.shape[0], transcendentals=0),
    )(margin, labels, rows)
    here = lax.axis_index("dp") * len(FIRST) + lax.axis_index("layer")

    def score(got, slot):
        is_own = functools.reduce(jnp.logical_or, [here == d * len(slot) + i for d, i in own_places(slot)])
        return sum(
            jnp.einsum("k,qk->q", jnp.where(is_own, mine, row), block, preferred_element_type=jnp.float32)
            for mine, row, block in zip(rows, got, blocks)
        )

    first, second = to_owner(score(first, FIRST), FIRST), to_owner(score(second, SECOND), SECOND)
    return ((first + second) * factor)[None]


def pair_gradients(acts_in, grads_out, proj_in, proj_out, lengths):
    pair_count, side_count, seq_len, layer_count, _ = acts_in.shape
    in_coords = jnp.einsum("pstld,ldr->pstlr", acts_in, proj_in, preferred_element_type=jnp.float32)
    out_coords = jnp.einsum(
        "pstld,ldr->pstlr", grads_out, proj_out, preferred_element_type=jnp.float32
    )
    position = jnp.arange(seq_len, dtype=jnp.int32)
    live = (position[None, None, :] < lengths[:, :, None]).astype(jnp.float32)
    signs = 1.0 - 2.0 * jnp.arange(side_count, dtype=jnp.float32)
    kron_grads = jnp.einsum("pst,pstlr,pstlk->plrk", live * signs[:, None], out_coords, in_coords)
    return kron_grads.reshape(pair_count, -1).astype(jnp.bfloat16)


def local(acts_in, grads_out, proj_in, proj_out, query_grads, margin, labels, lengths):
    pair_count, side_count, _, layer_count, _ = acts_in.shape
    rank = proj_in.shape[2]
    dp_size, layer_size = lax.axis_size("dp"), lax.axis_size("layer")
    block = query_grads.reshape(query_grads.shape[0], -1)
    one_each = pair_count == layer_count == 1 and side_count == 2
    form = pair_gradient if one_each else pair_gradients
    grad_rows = form(acts_in, grads_out, proj_in, proj_out, lengths)
    scale = rank * math.sqrt(layer_count * layer_size) * math.sqrt(acts_in.shape[2])
    if one_each and dp_size == layer_size == len(FIRST):
        return shared_scores(grad_rows, block, margin, labels, scale)
    factor = jax.nn.sigmoid(-margin) * jnp.where(labels == 0, 1.0, -1.0) / scale
    rows = lax.all_gather(grad_rows, "dp", axis=0, tiled=True)
    scores = jnp.einsum("pk,qk->pq", rows, block, preferred_element_type=jnp.float32)
    scores = lax.all_to_all(scores, "dp", split_axis=0, concat_axis=1, tiled=True)
    summed = lax.psum_scatter(scores, "layer", scatter_dimension=1, tiled=True)
    return summed * factor[:, None]


def solution(mesh):
    placed = (
        P(("groups", "dp"), None, None, "layer", None),
        P(("groups", "dp"), None, None, "layer", None),
        P("layer", None, None),
        P("layer", None, None),
        P("dp", "layer", None),
        P(("groups", "dp")),
        P(("groups", "dp")),
        P(("groups", "dp"), None),
    )
    return jax.shard_map(
        local, mesh=mesh, in_specs=placed, out_specs=P(("groups", "dp"), "layer"), check_vma=False
    )
```

```python
import functools
import math

import jax
import jax.numpy as jnp
from jax import lax
from jax.experimental import pallas as pl
from jax.experimental.pallas import tpu as pltpu
from jax.sharding import PartitionSpec as P

FIRST = ((2, 0, 1, 3), (0, 3, 2, 1), (1, 2, 3, 0), (3, 1, 0, 2))
SECOND = ((3, 1, 2, 0), (1, 2, 0, 3), (0, 3, 1, 2), (2, 0, 3, 1))
CHUNKS = 2


def pair_kernel(seq_len, acts, grads, proj_in, proj_out, lengths, out, *scratch):
    tokens_v, proj_v, kron_v, lengths_s, sems, lengths_sem = scratch
    tokens, model_width = acts.shape
    rank = proj_in.shape[0]
    width = model_width // CHUNKS
    limits = pltpu.make_async_copy(lengths, lengths_s, lengths_sem)
    loads = [
        [
            pltpu.make_async_copy(
                src.at[:, pl.ds(c * width, width)],
                dst.at[pl.ds(half * src.shape[0], src.shape[0]), pl.ds(c * width, width)],
                sems.at[c, 2 * half + i],
            )
            for half, pair in enumerate(((acts, proj_in), (grads, proj_out)))
            for i, (src, dst) in enumerate(zip(pair, (tokens_v, proj_v)))
        ]
        for c in range(CHUNKS)
    ]
    limits.start()
    for copies in loads:
        for i, copy in enumerate(copies):
            copy.start(priority=i // 2)
    coords = None
    for c, copies in enumerate(loads):
        for copy in copies:
            copy.wait()
        part = pl.ds(c * width, width)
        term = lax.dot_general(
            tokens_v[:, part], proj_v[:, part], (((1,), (1,)), ((), ())), preferred_element_type=jnp.float32
        )
        coords = term if coords is None else coords + term
    limits.wait()
    token = lax.broadcasted_iota(jnp.int32, (tokens, 1), 0)
    side = token // seq_len
    live = token - side * seq_len < jnp.where(side == 0, lengths_s[0, 0], lengths_s[0, 1])
    weight = jnp.where(live, jnp.where(side == 0, 1.0, -1.0), 0.0)
    in_coords = (coords[:tokens, :rank] * weight).astype(jnp.bfloat16)
    out_coords = coords[tokens:, rank:].astype(jnp.bfloat16)
    kron_v[...] = lax.dot_general(
        out_coords, in_coords, (((0,), (0,)), ((), ())), preferred_element_type=jnp.float32
    )
    half = rank // 2
    rows = jnp.concatenate([kron_v[pl.ds(i, half, stride=2), :] for i in range(2)], axis=1)
    for i in range(half):
        out[:, pl.ds(i * rows.shape[1], rows.shape[1])] = rows[i : i + 1].astype(out.dtype)


def pair_gradient(acts_in, grads_out, proj_in, proj_out, lengths):
    _, sides, seq_len, _, model_width = acts_in.shape
    rank = proj_in.shape[2]
    tokens = sides * seq_len
    return pl.pallas_call(
        functools.partial(pair_kernel, seq_len),
        out_shape=jax.ShapeDtypeStruct((1, rank * rank), jnp.bfloat16),
        in_specs=[pl.BlockSpec(memory_space=pl.ANY)] * 5,
        out_specs=pl.BlockSpec(memory_space=pltpu.VMEM),
        scratch_shapes=[
            pltpu.VMEM((2 * tokens, model_width), jnp.bfloat16),
            pltpu.VMEM((2 * rank, model_width), jnp.bfloat16),
            pltpu.VMEM((rank, rank), jnp.float32),
            pltpu.SMEM((1, 2), jnp.int32),
            pltpu.SemaphoreType.DMA((CHUNKS, 4)),
            pltpu.SemaphoreType.DMA,
        ],
        compiler_params=pltpu.CompilerParams(vmem_limit_bytes=32 * 1024 * 1024),
        cost_estimate=pl.CostEstimate(
            flops=4 * tokens * model_width * rank,
            bytes_accessed=4 * (tokens + rank) * model_width,
            transcendentals=0,
        ),
    )(
        *(
            pltpu.with_memory_space_constraint(x, pltpu.HBM)
            for x in (
                acts_in.reshape(tokens, model_width),
                grads_out.reshape(tokens, model_width),
                jnp.swapaxes(proj_in, 1, 2).reshape(rank, model_width),
                jnp.swapaxes(proj_out, 1, 2).reshape(rank, model_width),
                lengths,
            )
        )
    )


def swap(x):
    return lax.ppermute(x, "layer", [(i, i ^ 1) for i in range(lax.axis_size("layer"))])


def own_places(slot):
    return [(d, i) for d, row in enumerate(slot) for i, pair in enumerate(row) if pair == d]


def fetch_pair(x, slot):
    count = len(slot)
    moves = [
        (slot[d][i] * count + i, d * count + i) for d in range(count) for i in range(count) if slot[d][i] != d
    ]
    own = [d * count + i for d, i in own_places(slot)]
    fill = zip(own, own[1::-1] + own[:1:-1])
    return lax.ppermute(x, ("dp", "layer"), moves + list(fill))


def to_owner(x, slot):
    count = len(slot)
    moves = [(d * count + i, slot[d][i] * count + d) for d in range(count) for i in range(count)]
    return lax.ppermute(x, ("dp", "layer"), moves)


def factor_kernel(scale, margin, label, rows, factor):
    sign = jnp.where(label[0] == 0, 1.0, -1.0)
    factor[...] = sign / ((1.0 + jnp.exp(jnp.full(factor.shape, margin[0], jnp.float32))) * scale)


def shared_scores(own_row, own_block, margin, labels, scale):
    blocks = own_block, swap(own_block)
    rows = jnp.concatenate([own_row, swap(own_row)], axis=0)
    first, second = fetch_pair(rows, FIRST), fetch_pair(rows, SECOND)
    factor = pl.pallas_call(
        functools.partial(factor_kernel, scale),
        out_shape=jax.ShapeDtypeStruct(own_block.shape[:1], jnp.float32),
        in_specs=[pl.BlockSpec(memory_space=pltpu.SMEM)] * 2 + [pl.BlockSpec(memory_space=pl.ANY)],
        out_specs=pl.BlockSpec(memory_space=pltpu.VMEM),
        compiler_params=pltpu.CompilerParams(vmem_limit_bytes=1024 * 1024),
        cost_estimate=pl.CostEstimate(flops=0, bytes_accessed=4 * own_block.shape[0], transcendentals=0),
    )(margin, labels, rows)
    here = lax.axis_index("dp") * len(FIRST) + lax.axis_index("layer")

    def score(got, slot):
        is_own = functools.reduce(jnp.logical_or, [here == d * len(slot) + i for d, i in own_places(slot)])
        return sum(
            jnp.einsum("k,qk->q", jnp.where(is_own, mine, row), block, preferred_element_type=jnp.float32)
            for mine, row, block in zip(rows, got, blocks)
        )

    first, second = to_owner(score(first, FIRST), FIRST), to_owner(score(second, SECOND), SECOND)
    return ((first + second) * factor)[None]


def pair_gradients(acts_in, grads_out, proj_in, proj_out, lengths):
    pair_count, side_count, seq_len, layer_count, _ = acts_in.shape
    in_coords = jnp.einsum("pstld,ldr->pstlr", acts_in, proj_in, preferred_element_type=jnp.float32)
    out_coords = jnp.einsum(
        "pstld,ldr->pstlr", grads_out, proj_out, preferred_element_type=jnp.float32
    )
    position = jnp.arange(seq_len, dtype=jnp.int32)
    live = (position[None, None, :] < lengths[:, :, None]).astype(jnp.float32)
    signs = 1.0 - 2.0 * jnp.arange(side_count, dtype=jnp.float32)
    kron_grads = jnp.einsum("pst,pstlr,pstlk->plrk", live * signs[:, None], out_coords, in_coords)
    return kron_grads.reshape(pair_count, -1).astype(jnp.bfloat16)


def local(acts_in, grads_out, proj_in, proj_out, query_grads, margin, labels, lengths):
    pair_count, side_count, _, layer_count, _ = acts_in.shape
    rank = proj_in.shape[2]
    dp_size, layer_size = lax.axis_size("dp"), lax.axis_size("layer")
    block = query_grads.reshape(query_grads.shape[0], -1)
    one_each = pair_count == layer_count == 1 and side_count == 2
    form = pair_gradient if one_each else pair_gradients
    grad_rows = form(acts_in, grads_out, proj_in, proj_out, lengths)
    scale = rank * math.sqrt(layer_count * layer_size) * math.sqrt(acts_in.shape[2])
    if one_each and dp_size == layer_size == len(FIRST):
        return shared_scores(grad_rows, block, margin, labels, scale)
    factor = jax.nn.sigmoid(-margin) * jnp.where(labels == 0, 1.0, -1.0) / scale
    rows = lax.all_gather(grad_rows, "dp", axis=0, tiled=True)
    scores = jnp.einsum("pk,qk->pq", rows, block, preferred_element_type=jnp.float32)
    scores = lax.all_to_all(scores, "dp", split_axis=0, concat_axis=1, tiled=True)
    summed = lax.psum_scatter(scores, "layer", scatter_dimension=1, tiled=True)
    return summed * factor[:, None]


def solution(mesh):
    placed = (
        P(("groups", "dp"), None, None, "layer", None),
        P(("groups", "dp"), None, None, "layer", None),
        P("layer", None, None),
        P("layer", None, None),
        P("dp", "layer", None),
        P(("groups", "dp")),
        P(("groups", "dp")),
        P(("groups", "dp"), None),
    )
    return jax.shard_map(
        local, mesh=mesh, in_specs=placed, out_specs=P(("groups", "dp"), "layer"), check_vma=False
    )
```

```python
import functools
import math

import jax
import jax.numpy as jnp
from jax import lax
from jax.experimental import pallas as pl
from jax.experimental.pallas import tpu as pltpu
from jax.sharding import PartitionSpec as P

FIRST = ((2, 0, 1, 3), (0, 3, 2, 1), (1, 2, 3, 0), (3, 1, 0, 2))
SECOND = ((3, 1, 2, 0), (1, 2, 0, 3), (0, 3, 1, 2), (2, 0, 3, 1))
def pair_kernel(seq_len, acts, grads, proj_in, proj_out, lengths, out, *scratch):
    *held, kron_v, lengths_s, sems = scratch
    limits = pltpu.make_async_copy(lengths, lengths_s, sems.at[len(held)])
    loads = [
        pltpu.make_async_copy(src, dst, sems.at[i])
        for i, (src, dst) in enumerate(zip((acts, proj_in, grads, proj_out), held))
    ]
    limits.start()
    for i, copy in enumerate(loads):
        copy.start(priority=i % 2)

    def project(first):
        for copy in loads[first : first + 2]:
            copy.wait()
        tokens, proj = held[first : first + 2]
        return lax.dot_general(
            tokens[...], proj[...], (((1,), (1,)), ((), ())), preferred_element_type=jnp.float32
        )

    coords = project(0)
    limits.wait()
    token = lax.broadcasted_iota(jnp.int32, (coords.shape[0], 1), 0)
    side = token // seq_len
    live = token - side * seq_len < jnp.where(side == 0, lengths_s[0, 0], lengths_s[0, 1])
    weight = jnp.where(live, jnp.where(side == 0, 1.0, -1.0), 0.0)
    in_coords = (coords * weight).astype(jnp.bfloat16)
    out_coords = project(2).astype(jnp.bfloat16)
    kron_v[...] = lax.dot_general(
        out_coords, in_coords, (((0,), (0,)), ((), ())), preferred_element_type=jnp.float32
    )
    half = kron_v.shape[0] // 2
    rows = jnp.concatenate([kron_v[pl.ds(i, half, stride=2), :] for i in range(2)], axis=1)
    for i in range(half):
        out[:, pl.ds(i * rows.shape[1], rows.shape[1])] = rows[i : i + 1].astype(out.dtype)


def pair_gradient(acts_in, grads_out, proj_in, proj_out, lengths):
    _, sides, seq_len, _, model_width = acts_in.shape
    rank = proj_in.shape[2]
    tokens = sides * seq_len
    return pl.pallas_call(
        functools.partial(pair_kernel, seq_len),
        out_shape=jax.ShapeDtypeStruct((1, rank * rank), jnp.bfloat16),
        in_specs=[pl.BlockSpec(memory_space=pl.ANY)] * 5,
        out_specs=pl.BlockSpec(memory_space=pltpu.VMEM),
        scratch_shapes=[
            *(pltpu.VMEM((rows, model_width), jnp.bfloat16) for rows in (tokens, rank, tokens, rank)),
            pltpu.VMEM((rank, rank), jnp.float32),
            pltpu.SMEM((1, 2), jnp.int32),
            pltpu.SemaphoreType.DMA((5,)),
        ],
        compiler_params=pltpu.CompilerParams(vmem_limit_bytes=32 * 1024 * 1024),
        cost_estimate=pl.CostEstimate(
            flops=4 * tokens * model_width * rank,
            bytes_accessed=4 * (tokens + rank) * model_width,
            transcendentals=0,
        ),
    )(
        *(
            pltpu.with_memory_space_constraint(x, pltpu.HBM)
            for x in (
                acts_in.reshape(tokens, model_width),
                grads_out.reshape(tokens, model_width),
                jnp.swapaxes(proj_in, 1, 2).reshape(rank, model_width),
                jnp.swapaxes(proj_out, 1, 2).reshape(rank, model_width),
                lengths,
            )
        )
    )


def swap(x):
    return lax.ppermute(x, "layer", [(i, i ^ 1) for i in range(lax.axis_size("layer"))])


def own_places(slot):
    return [(d, i) for d, row in enumerate(slot) for i, pair in enumerate(row) if pair == d]


def fetch_pair(x, slot):
    count = len(slot)
    moves = [
        (slot[d][i] * count + i, d * count + i) for d in range(count) for i in range(count) if slot[d][i] != d
    ]
    own = [d * count + i for d, i in own_places(slot)]
    fill = zip(own, own[1::-1] + own[:1:-1])
    return lax.ppermute(x, ("dp", "layer"), moves + list(fill))


def to_owner(x, slot):
    count = len(slot)
    moves = [(d * count + i, slot[d][i] * count + d) for d in range(count) for i in range(count)]
    return lax.ppermute(x, ("dp", "layer"), moves)


def factor_kernel(scale, margin, label, rows, factor):
    sign = jnp.where(label[0] == 0, 1.0, -1.0)
    factor[...] = sign / ((1.0 + jnp.exp(jnp.full(factor.shape, margin[0], jnp.float32))) * scale)


def shared_scores(own_row, own_block, margin, labels, scale):
    blocks = own_block, swap(own_block)
    rows = jnp.concatenate([own_row, swap(own_row)], axis=0)
    first, second = fetch_pair(rows, FIRST), fetch_pair(rows, SECOND)
    factor = pl.pallas_call(
        functools.partial(factor_kernel, scale),
        out_shape=jax.ShapeDtypeStruct(own_block.shape[:1], jnp.float32),
        in_specs=[pl.BlockSpec(memory_space=pltpu.SMEM)] * 2 + [pl.BlockSpec(memory_space=pl.ANY)],
        out_specs=pl.BlockSpec(memory_space=pltpu.VMEM),
        compiler_params=pltpu.CompilerParams(vmem_limit_bytes=1024 * 1024),
        cost_estimate=pl.CostEstimate(flops=0, bytes_accessed=4 * own_block.shape[0], transcendentals=0),
    )(margin, labels, rows)
    here = lax.axis_index("dp") * len(FIRST) + lax.axis_index("layer")

    def score(got, slot):
        is_own = functools.reduce(jnp.logical_or, [here == d * len(slot) + i for d, i in own_places(slot)])
        return sum(
            jnp.einsum("k,qk->q", jnp.where(is_own, mine, row), block, preferred_element_type=jnp.float32)
            for mine, row, block in zip(rows, got, blocks)
        )

    first, second = to_owner(score(first, FIRST), FIRST), to_owner(score(second, SECOND), SECOND)
    return ((first + second) * factor)[None]


def pair_gradients(acts_in, grads_out, proj_in, proj_out, lengths):
    pair_count, side_count, seq_len, layer_count, _ = acts_in.shape
    in_coords = jnp.einsum("pstld,ldr->pstlr", acts_in, proj_in, preferred_element_type=jnp.float32)
    out_coords = jnp.einsum(
        "pstld,ldr->pstlr", grads_out, proj_out, preferred_element_type=jnp.float32
    )
    position = jnp.arange(seq_len, dtype=jnp.int32)
    live = (position[None, None, :] < lengths[:, :, None]).astype(jnp.float32)
    signs = 1.0 - 2.0 * jnp.arange(side_count, dtype=jnp.float32)
    kron_grads = jnp.einsum("pst,pstlr,pstlk->plrk", live * signs[:, None], out_coords, in_coords)
    return kron_grads.reshape(pair_count, -1).astype(jnp.bfloat16)


def local(acts_in, grads_out, proj_in, proj_out, query_grads, margin, labels, lengths):
    pair_count, side_count, _, layer_count, _ = acts_in.shape
    rank = proj_in.shape[2]
    dp_size, layer_size = lax.axis_size("dp"), lax.axis_size("layer")
    block = query_grads.reshape(query_grads.shape[0], -1)
    one_each = pair_count == layer_count == 1 and side_count == 2
    form = pair_gradient if one_each else pair_gradients
    grad_rows = form(acts_in, grads_out, proj_in, proj_out, lengths)
    scale = rank * math.sqrt(layer_count * layer_size) * math.sqrt(acts_in.shape[2])
    if one_each and dp_size == layer_size == len(FIRST):
        return shared_scores(grad_rows, block, margin, labels, scale)
    factor = jax.nn.sigmoid(-margin) * jnp.where(labels == 0, 1.0, -1.0) / scale
    rows = lax.all_gather(grad_rows, "dp", axis=0, tiled=True)
    scores = jnp.einsum("pk,qk->pq", rows, block, preferred_element_type=jnp.float32)
    scores = lax.all_to_all(scores, "dp", split_axis=0, concat_axis=1, tiled=True)
    summed = lax.psum_scatter(scores, "layer", scatter_dimension=1, tiled=True)
    return summed * factor[:, None]


def solution(mesh):
    placed = (
        P(("groups", "dp"), None, None, "layer", None),
        P(("groups", "dp"), None, None, "layer", None),
        P("layer", None, None),
        P("layer", None, None),
        P("dp", "layer", None),
        P(("groups", "dp")),
        P(("groups", "dp")),
        P(("groups", "dp"), None),
    )
    return jax.shard_map(
        local, mesh=mesh, in_specs=placed, out_specs=P(("groups", "dp"), "layer"), check_vma=False
    )
```

```python
import functools
import math

import jax
import jax.numpy as jnp
from jax import lax
from jax.experimental import pallas as pl
from jax.experimental.pallas import tpu as pltpu
from jax.sharding import PartitionSpec as P

FIRST = ((2, 0, 1, 3), (0, 3, 2, 1), (1, 2, 3, 0), (3, 1, 0, 2))
SECOND = ((3, 1, 2, 0), (1, 2, 0, 3), (0, 3, 1, 2), (2, 0, 3, 1))
CHUNKS = 1


def pair_kernel(seq_len, acts, grads, proj_in, proj_out, lengths, out, *scratch):
    tokens_v, proj_v, kron_v, lengths_s, sems, lengths_sem = scratch
    tokens, model_width = acts.shape
    rank = proj_in.shape[0]
    width = model_width // CHUNKS
    limits = pltpu.make_async_copy(lengths, lengths_s, lengths_sem)
    loads = [
        [
            pltpu.make_async_copy(
                src.at[:, pl.ds(c * width, width)],
                dst.at[pl.ds(half * src.shape[0], src.shape[0]), pl.ds(c * width, width)],
                sems.at[c, 2 * half + i],
            )
            for half, pair in enumerate(((acts, proj_in), (grads, proj_out)))
            for i, (src, dst) in enumerate(zip(pair, (tokens_v, proj_v)))
        ]
        for c in range(CHUNKS)
    ]
    limits.start()
    for copies in loads:
        for i, copy in enumerate(copies):
            copy.start(priority=i // 2)
    coords = None
    for c, copies in enumerate(loads):
        for copy in copies:
            copy.wait()
        part = pl.ds(c * width, width)
        term = lax.dot_general(
            tokens_v[:, part], proj_v[:, part], (((1,), (1,)), ((), ())), preferred_element_type=jnp.float32
        )
        coords = term if coords is None else coords + term
    limits.wait()
    token = lax.broadcasted_iota(jnp.int32, (tokens, 1), 0)
    side = token // seq_len
    live = token - side * seq_len < jnp.where(side == 0, lengths_s[0, 0], lengths_s[0, 1])
    weight = jnp.where(live, jnp.where(side == 0, 1.0, -1.0), 0.0)
    in_coords = (coords[:tokens, :rank] * weight).astype(jnp.bfloat16)
    out_coords = coords[tokens:, rank:].astype(jnp.bfloat16)
    kron_v[...] = lax.dot_general(
        out_coords, in_coords, (((0,), (0,)), ((), ())), preferred_element_type=jnp.float32
    )
    half = rank // 2
    rows = jnp.concatenate([kron_v[pl.ds(i, half, stride=2), :] for i in range(2)], axis=1)
    for i in range(half):
        out[:, pl.ds(i * rows.shape[1], rows.shape[1])] = rows[i : i + 1].astype(out.dtype)


def pair_gradient(acts_in, grads_out, proj_in, proj_out, lengths):
    _, sides, seq_len, _, model_width = acts_in.shape
    rank = proj_in.shape[2]
    tokens = sides * seq_len
    return pl.pallas_call(
        functools.partial(pair_kernel, seq_len),
        out_shape=jax.ShapeDtypeStruct((1, rank * rank), jnp.bfloat16),
        in_specs=[pl.BlockSpec(memory_space=pl.ANY)] * 5,
        out_specs=pl.BlockSpec(memory_space=pltpu.VMEM),
        scratch_shapes=[
            pltpu.VMEM((2 * tokens, model_width), jnp.bfloat16),
            pltpu.VMEM((2 * rank, model_width), jnp.bfloat16),
            pltpu.VMEM((rank, rank), jnp.float32),
            pltpu.SMEM((1, 2), jnp.int32),
            pltpu.SemaphoreType.DMA((CHUNKS, 4)),
            pltpu.SemaphoreType.DMA,
        ],
        compiler_params=pltpu.CompilerParams(vmem_limit_bytes=32 * 1024 * 1024),
        cost_estimate=pl.CostEstimate(
            flops=4 * tokens * model_width * rank,
            bytes_accessed=4 * (tokens + rank) * model_width,
            transcendentals=0,
        ),
    )(
        *(
            pltpu.with_memory_space_constraint(x, pltpu.HBM)
            for x in (
                acts_in.reshape(tokens, model_width),
                grads_out.reshape(tokens, model_width),
                jnp.swapaxes(proj_in, 1, 2).reshape(rank, model_width),
                jnp.swapaxes(proj_out, 1, 2).reshape(rank, model_width),
                lengths,
            )
        )
    )


def swap(x):
    return lax.ppermute(x, "layer", [(i, i ^ 1) for i in range(lax.axis_size("layer"))])


def own_places(slot):
    return [(d, i) for d, row in enumerate(slot) for i, pair in enumerate(row) if pair == d]


def fetch_pair(x, slot):
    count = len(slot)
    moves = [
        (slot[d][i] * count + i, d * count + i) for d in range(count) for i in range(count) if slot[d][i] != d
    ]
    own = [d * count + i for d, i in own_places(slot)]
    fill = zip(own, own[1::-1] + own[:1:-1])
    return lax.ppermute(x, ("dp", "layer"), moves + list(fill))


def to_owner(x, slot):
    count = len(slot)
    moves = [(d * count + i, slot[d][i] * count + d) for d in range(count) for i in range(count)]
    return lax.ppermute(x, ("dp", "layer"), moves)


def factor_kernel(scale, margin, label, rows, factor):
    sign = jnp.where(label[0] == 0, 1.0, -1.0)
    factor[...] = sign / ((1.0 + jnp.exp(jnp.full(factor.shape, margin[0], jnp.float32))) * scale)


def shared_scores(own_row, own_block, margin, labels, scale):
    blocks = own_block, swap(own_block)
    rows = jnp.concatenate([own_row, swap(own_row)], axis=0)
    first, second = fetch_pair(rows, FIRST), fetch_pair(rows, SECOND)
    factor = pl.pallas_call(
        functools.partial(factor_kernel, scale),
        out_shape=jax.ShapeDtypeStruct(own_block.shape[:1], jnp.float32),
        in_specs=[pl.BlockSpec(memory_space=pltpu.SMEM)] * 2 + [pl.BlockSpec(memory_space=pl.ANY)],
        out_specs=pl.BlockSpec(memory_space=pltpu.VMEM),
        compiler_params=pltpu.CompilerParams(vmem_limit_bytes=1024 * 1024),
        cost_estimate=pl.CostEstimate(flops=0, bytes_accessed=4 * own_block.shape[0], transcendentals=0),
    )(margin, labels, rows)
    here = lax.axis_index("dp") * len(FIRST) + lax.axis_index("layer")

    def score(got, slot):
        is_own = functools.reduce(jnp.logical_or, [here == d * len(slot) + i for d, i in own_places(slot)])
        return sum(
            jnp.einsum("k,qk->q", jnp.where(is_own, mine, row), block, preferred_element_type=jnp.float32)
            for mine, row, block in zip(rows, got, blocks)
        )

    first, second = to_owner(score(first, FIRST), FIRST), to_owner(score(second, SECOND), SECOND)
    return ((first + second) * factor)[None]


def pair_gradients(acts_in, grads_out, proj_in, proj_out, lengths):
    pair_count, side_count, seq_len, layer_count, _ = acts_in.shape
    in_coords = jnp.einsum("pstld,ldr->pstlr", acts_in, proj_in, preferred_element_type=jnp.float32)
    out_coords = jnp.einsum(
        "pstld,ldr->pstlr", grads_out, proj_out, preferred_element_type=jnp.float32
    )
    position = jnp.arange(seq_len, dtype=jnp.int32)
    live = (position[None, None, :] < lengths[:, :, None]).astype(jnp.float32)
    signs = 1.0 - 2.0 * jnp.arange(side_count, dtype=jnp.float32)
    kron_grads = jnp.einsum("pst,pstlr,pstlk->plrk", live * signs[:, None], out_coords, in_coords)
    return kron_grads.reshape(pair_count, -1).astype(jnp.bfloat16)


def local(acts_in, grads_out, proj_in, proj_out, query_grads, margin, labels, lengths):
    pair_count, side_count, _, layer_count, _ = acts_in.shape
    rank = proj_in.shape[2]
    dp_size, layer_size = lax.axis_size("dp"), lax.axis_size("layer")
    block = query_grads.reshape(query_grads.shape[0], -1)
    one_each = pair_count == layer_count == 1 and side_count == 2
    form = pair_gradient if one_each else pair_gradients
    grad_rows = form(acts_in, grads_out, proj_in, proj_out, lengths)
    scale = rank * math.sqrt(layer_count * layer_size) * math.sqrt(acts_in.shape[2])
    if one_each and dp_size == layer_size == len(FIRST):
        return shared_scores(grad_rows, block, margin, labels, scale)
    factor = jax.nn.sigmoid(-margin) * jnp.where(labels == 0, 1.0, -1.0) / scale
    rows = lax.all_gather(grad_rows, "dp", axis=0, tiled=True)
    scores = jnp.einsum("pk,qk->pq", rows, block, preferred_element_type=jnp.float32)
    scores = lax.all_to_all(scores, "dp", split_axis=0, concat_axis=1, tiled=True)
    summed = lax.psum_scatter(scores, "layer", scatter_dimension=1, tiled=True)
    return summed * factor[:, None]


def solution(mesh):
    placed = (
        P(("groups", "dp"), None, None, "layer", None),
        P(("groups", "dp"), None, None, "layer", None),
        P("layer", None, None),
        P("layer", None, None),
        P("dp", "layer", None),
        P(("groups", "dp")),
        P(("groups", "dp")),
        P(("groups", "dp"), None),
    )
    return jax.shard_map(
        local, mesh=mesh, in_specs=placed, out_specs=P(("groups", "dp"), "layer"), check_vma=False
    )
```

```python
import functools
import math

import jax
import jax.numpy as jnp
from jax import lax
from jax.experimental import pallas as pl
from jax.experimental.pallas import tpu as pltpu
from jax.sharding import PartitionSpec as P

FIRST = ((2, 0, 1, 3), (0, 3, 2, 1), (1, 2, 3, 0), (3, 1, 0, 2))
SECOND = ((3, 1, 2, 0), (1, 2, 0, 3), (0, 3, 1, 2), (2, 0, 3, 1))
PARTS = 4


def pair_kernel(seq_len, acts, grads, proj_in, proj_out, lengths, out, *scratch):
    tokens_v, proj_v, turned_v, kron_v, lengths_s, sems = scratch
    tokens = acts.shape[0]
    rank, model_width = proj_in.shape
    limits = pltpu.make_async_copy(lengths, lengths_s, sems.at[4])
    loads = [
        pltpu.make_async_copy(src, dst.at[pl.ds(half * src.shape[0], src.shape[0])], sems.at[2 * i + half])
        for i, (pair, dst) in enumerate((((proj_in, proj_out), proj_v), ((acts, grads), tokens_v)))
        for half, src in enumerate(pair)
    ]
    limits.start()
    for i, copy in enumerate(loads):
        copy.start(priority=i % 2)
    limits.wait()
    token = lax.broadcasted_iota(jnp.int32, (tokens, 1), 0)
    side = token // seq_len
    live = token - side * seq_len < jnp.where(side == 0, lengths_s[0, 0], lengths_s[0, 1])
    weight = jnp.where(live, jnp.where(side == 0, 1.0, -1.0), 0.0)
    for copy in loads[:2]:
        copy.wait()
    width = model_width // PARTS
    for c in range(PARTS):
        turned_v[pl.ds(c * width, width), :] = proj_v[:, pl.ds(c * width, width)].T
    for copy in loads[2:]:
        copy.wait()
    coords = jnp.dot(tokens_v[...], turned_v[...], preferred_element_type=jnp.float32)
    in_coords = (coords[:tokens, :rank] * weight).astype(jnp.bfloat16)
    out_coords = coords[tokens:, rank:].astype(jnp.bfloat16)
    kron_v[...] = lax.dot_general(
        out_coords, in_coords, (((0,), (0,)), ((), ())), preferred_element_type=jnp.float32
    )
    half = rank // 2
    rows = jnp.concatenate([kron_v[pl.ds(i, half, stride=2), :] for i in range(2)], axis=1)
    for i in range(half):
        out[:, pl.ds(i * rows.shape[1], rows.shape[1])] = rows[i : i + 1].astype(out.dtype)


def pair_gradient(acts_in, grads_out, proj_in, proj_out, lengths):
    _, sides, seq_len, _, model_width = acts_in.shape
    rank = proj_in.shape[2]
    tokens = sides * seq_len
    return pl.pallas_call(
        functools.partial(pair_kernel, seq_len),
        out_shape=jax.ShapeDtypeStruct((1, rank * rank), jnp.bfloat16),
        in_specs=[pl.BlockSpec(memory_space=pl.ANY)] * 5,
        out_specs=pl.BlockSpec(memory_space=pltpu.VMEM),
        scratch_shapes=[
            pltpu.VMEM((2 * tokens, model_width), jnp.bfloat16),
            pltpu.VMEM((2 * rank, model_width), jnp.bfloat16),
            pltpu.VMEM((model_width, 2 * rank), jnp.bfloat16),
            pltpu.VMEM((rank, rank), jnp.float32),
            pltpu.SMEM((1, 2), jnp.int32),
            pltpu.SemaphoreType.DMA((5,)),
        ],
        compiler_params=pltpu.CompilerParams(vmem_limit_bytes=32 * 1024 * 1024),
        cost_estimate=pl.CostEstimate(
            flops=4 * tokens * model_width * rank,
            bytes_accessed=4 * (tokens + rank) * model_width,
            transcendentals=0,
        ),
    )(
        *(
            pltpu.with_memory_space_constraint(x, pltpu.HBM)
            for x in (
                acts_in.reshape(tokens, model_width),
                grads_out.reshape(tokens, model_width),
                jnp.swapaxes(proj_in, 1, 2).reshape(rank, model_width),
                jnp.swapaxes(proj_out, 1, 2).reshape(rank, model_width),
                lengths,
            )
        )
    )


def swap(x):
    return lax.ppermute(x, "layer", [(i, i ^ 1) for i in range(lax.axis_size("layer"))])


def own_places(slot):
    return [(d, i) for d, row in enumerate(slot) for i, pair in enumerate(row) if pair == d]


def fetch_pair(x, slot):
    count = len(slot)
    moves = [
        (slot[d][i] * count + i, d * count + i) for d in range(count) for i in range(count) if slot[d][i] != d
    ]
    own = [d * count + i for d, i in own_places(slot)]
    fill = zip(own, own[1::-1] + own[:1:-1])
    return lax.ppermute(x, ("dp", "layer"), moves + list(fill))


def to_owner(x, slot):
    count = len(slot)
    moves = [(d * count + i, slot[d][i] * count + d) for d in range(count) for i in range(count)]
    return lax.ppermute(x, ("dp", "layer"), moves)


def factor_kernel(scale, margin, label, rows, factor):
    sign = jnp.where(label[0] == 0, 1.0, -1.0)
    factor[...] = sign / ((1.0 + jnp.exp(jnp.full(factor.shape, margin[0], jnp.float32))) * scale)


def shared_scores(own_row, own_block, margin, labels, scale):
    blocks = own_block, swap(own_block)
    rows = jnp.concatenate([own_row, swap(own_row)], axis=0)
    first, second = fetch_pair(rows, FIRST), fetch_pair(rows, SECOND)
    factor = pl.pallas_call(
        functools.partial(factor_kernel, scale),
        out_shape=jax.ShapeDtypeStruct(own_block.shape[:1], jnp.float32),
        in_specs=[pl.BlockSpec(memory_space=pltpu.SMEM)] * 2 + [pl.BlockSpec(memory_space=pl.ANY)],
        out_specs=pl.BlockSpec(memory_space=pltpu.VMEM),
        compiler_params=pltpu.CompilerParams(vmem_limit_bytes=1024 * 1024),
        cost_estimate=pl.CostEstimate(flops=0, bytes_accessed=4 * own_block.shape[0], transcendentals=0),
    )(margin, labels, rows)
    here = lax.axis_index("dp") * len(FIRST) + lax.axis_index("layer")

    def score(got, slot):
        is_own = functools.reduce(jnp.logical_or, [here == d * len(slot) + i for d, i in own_places(slot)])
        return sum(
            jnp.einsum("k,qk->q", jnp.where(is_own, mine, row), block, preferred_element_type=jnp.float32)
            for mine, row, block in zip(rows, got, blocks)
        )

    first, second = to_owner(score(first, FIRST), FIRST), to_owner(score(second, SECOND), SECOND)
    return ((first + second) * factor)[None]


def pair_gradients(acts_in, grads_out, proj_in, proj_out, lengths):
    pair_count, side_count, seq_len, layer_count, _ = acts_in.shape
    in_coords = jnp.einsum("pstld,ldr->pstlr", acts_in, proj_in, preferred_element_type=jnp.float32)
    out_coords = jnp.einsum(
        "pstld,ldr->pstlr", grads_out, proj_out, preferred_element_type=jnp.float32
    )
    position = jnp.arange(seq_len, dtype=jnp.int32)
    live = (position[None, None, :] < lengths[:, :, None]).astype(jnp.float32)
    signs = 1.0 - 2.0 * jnp.arange(side_count, dtype=jnp.float32)
    kron_grads = jnp.einsum("pst,pstlr,pstlk->plrk", live * signs[:, None], out_coords, in_coords)
    return kron_grads.reshape(pair_count, -1).astype(jnp.bfloat16)


def local(acts_in, grads_out, proj_in, proj_out, query_grads, margin, labels, lengths):
    pair_count, side_count, _, layer_count, _ = acts_in.shape
    rank = proj_in.shape[2]
    dp_size, layer_size = lax.axis_size("dp"), lax.axis_size("layer")
    block = query_grads.reshape(query_grads.shape[0], -1)
    one_each = pair_count == layer_count == 1 and side_count == 2
    form = pair_gradient if one_each else pair_gradients
    grad_rows = form(acts_in, grads_out, proj_in, proj_out, lengths)
    scale = rank * math.sqrt(layer_count * layer_size) * math.sqrt(acts_in.shape[2])
    if one_each and dp_size == layer_size == len(FIRST):
        return shared_scores(grad_rows, block, margin, labels, scale)
    factor = jax.nn.sigmoid(-margin) * jnp.where(labels == 0, 1.0, -1.0) / scale
    rows = lax.all_gather(grad_rows, "dp", axis=0, tiled=True)
    scores = jnp.einsum("pk,qk->pq", rows, block, preferred_element_type=jnp.float32)
    scores = lax.all_to_all(scores, "dp", split_axis=0, concat_axis=1, tiled=True)
    summed = lax.psum_scatter(scores, "layer", scatter_dimension=1, tiled=True)
    return summed * factor[:, None]


def solution(mesh):
    placed = (
        P(("groups", "dp"), None, None, "layer", None),
        P(("groups", "dp"), None, None, "layer", None),
        P("layer", None, None),
        P("layer", None, None),
        P("dp", "layer", None),
        P(("groups", "dp")),
        P(("groups", "dp")),
        P(("groups", "dp"), None),
    )
    return jax.shard_map(
        local, mesh=mesh, in_specs=placed, out_specs=P(("groups", "dp"), "layer"), check_vma=False
    )
```

```python
import functools
import math

import jax
import jax.numpy as jnp
from jax import lax
from jax.experimental import pallas as pl
from jax.experimental.pallas import tpu as pltpu
from jax.sharding import PartitionSpec as P

FIRST = ((2, 0, 1, 3), (0, 3, 2, 1), (1, 2, 3, 0), (3, 1, 0, 2))
SECOND = ((3, 1, 2, 0), (1, 2, 0, 3), (0, 3, 1, 2), (2, 0, 3, 1))
PIECE = 32


def pair_kernel(seq_len, acts, grads, proj_in, proj_out, lengths, out, *scratch):
    tokens_v, proj_v, kron_v, lengths_s, sems, lengths_sem = scratch
    tokens = acts.shape[0]
    rank = proj_in.shape[0]
    limits = pltpu.make_async_copy(lengths, lengths_s, lengths_sem)
    limits.start()
    loads = []
    for pair, dst in (((proj_in, proj_out), proj_v), ((acts, grads), tokens_v)):
        for half, src in enumerate(pair):
            for row in range(0, src.shape[0], PIECE):
                to = dst.at[pl.ds(half * src.shape[0] + row, PIECE)]
                loads.append(pltpu.make_async_copy(src.at[pl.ds(row, PIECE)], to, sems.at[len(loads)]))
                loads[-1].start(priority=half)
    for copy in loads:
        copy.wait()
    coords = lax.dot_general(
        tokens_v[...], proj_v[...], (((1,), (1,)), ((), ())), preferred_element_type=jnp.float32
    )
    limits.wait()
    token = lax.broadcasted_iota(jnp.int32, (tokens, 1), 0)
    side = token // seq_len
    live = token - side * seq_len < jnp.where(side == 0, lengths_s[0, 0], lengths_s[0, 1])
    weight = jnp.where(live, jnp.where(side == 0, 1.0, -1.0), 0.0)
    in_coords = (coords[:tokens, :rank] * weight).astype(jnp.bfloat16)
    out_coords = coords[tokens:, rank:].astype(jnp.bfloat16)
    kron_v[...] = lax.dot_general(
        out_coords, in_coords, (((0,), (0,)), ((), ())), preferred_element_type=jnp.float32
    )
    half = rank // 2
    rows = jnp.concatenate([kron_v[pl.ds(i, half, stride=2), :] for i in range(2)], axis=1)
    for i in range(half):
        out[:, pl.ds(i * rows.shape[1], rows.shape[1])] = rows[i : i + 1].astype(out.dtype)


def pair_gradient(acts_in, grads_out, proj_in, proj_out, lengths):
    _, sides, seq_len, _, model_width = acts_in.shape
    rank = proj_in.shape[2]
    tokens = sides * seq_len
    return pl.pallas_call(
        functools.partial(pair_kernel, seq_len),
        out_shape=jax.ShapeDtypeStruct((1, rank * rank), jnp.bfloat16),
        in_specs=[pl.BlockSpec(memory_space=pl.ANY)] * 5,
        out_specs=pl.BlockSpec(memory_space=pltpu.VMEM),
        scratch_shapes=[
            pltpu.VMEM((2 * tokens, model_width), jnp.bfloat16),
            pltpu.VMEM((2 * rank, model_width), jnp.bfloat16),
            pltpu.VMEM((rank, rank), jnp.float32),
            pltpu.SMEM((1, 2), jnp.int32),
            pltpu.SemaphoreType.DMA((2 * (tokens + rank) // PIECE,)),
            pltpu.SemaphoreType.DMA,
        ],
        compiler_params=pltpu.CompilerParams(vmem_limit_bytes=32 * 1024 * 1024),
        cost_estimate=pl.CostEstimate(
            flops=4 * tokens * model_width * rank,
            bytes_accessed=4 * (tokens + rank) * model_width,
            transcendentals=0,
        ),
    )(
        *(
            pltpu.with_memory_space_constraint(x, pltpu.HBM)
            for x in (
                acts_in.reshape(tokens, model_width),
                grads_out.reshape(tokens, model_width),
                jnp.swapaxes(proj_in, 1, 2).reshape(rank, model_width),
                jnp.swapaxes(proj_out, 1, 2).reshape(rank, model_width),
                lengths,
            )
        )
    )


def swap(x):
    return lax.ppermute(x, "layer", [(i, i ^ 1) for i in range(lax.axis_size("layer"))])


def own_places(slot):
    return [(d, i) for d, row in enumerate(slot) for i, pair in enumerate(row) if pair == d]


def fetch_pair(x, slot):
    count = len(slot)
    moves = [
        (slot[d][i] * count + i, d * count + i) for d in range(count) for i in range(count) if slot[d][i] != d
    ]
    own = [d * count + i for d, i in own_places(slot)]
    fill = zip(own, own[1::-1] + own[:1:-1])
    return lax.ppermute(x, ("dp", "layer"), moves + list(fill))


def to_owner(x, slot):
    count = len(slot)
    moves = [(d * count + i, slot[d][i] * count + d) for d in range(count) for i in range(count)]
    return lax.ppermute(x, ("dp", "layer"), moves)


def factor_kernel(scale, margin, label, rows, factor):
    sign = jnp.where(label[0] == 0, 1.0, -1.0)
    factor[...] = sign / ((1.0 + jnp.exp(jnp.full(factor.shape, margin[0], jnp.float32))) * scale)


def shared_scores(own_row, own_block, margin, labels, scale):
    blocks = own_block, swap(own_block)
    rows = jnp.concatenate([own_row, swap(own_row)], axis=0)
    first, second = fetch_pair(rows, FIRST), fetch_pair(rows, SECOND)
    factor = pl.pallas_call(
        functools.partial(factor_kernel, scale),
        out_shape=jax.ShapeDtypeStruct(own_block.shape[:1], jnp.float32),
        in_specs=[pl.BlockSpec(memory_space=pltpu.SMEM)] * 2 + [pl.BlockSpec(memory_space=pl.ANY)],
        out_specs=pl.BlockSpec(memory_space=pltpu.VMEM),
        compiler_params=pltpu.CompilerParams(vmem_limit_bytes=1024 * 1024),
        cost_estimate=pl.CostEstimate(flops=0, bytes_accessed=4 * own_block.shape[0], transcendentals=0),
    )(margin, labels, rows)
    here = lax.axis_index("dp") * len(FIRST) + lax.axis_index("layer")

    def score(got, slot):
        is_own = functools.reduce(jnp.logical_or, [here == d * len(slot) + i for d, i in own_places(slot)])
        return sum(
            jnp.einsum("k,qk->q", jnp.where(is_own, mine, row), block, preferred_element_type=jnp.float32)
            for mine, row, block in zip(rows, got, blocks)
        )

    first, second = to_owner(score(first, FIRST), FIRST), to_owner(score(second, SECOND), SECOND)
    return ((first + second) * factor)[None]


def pair_gradients(acts_in, grads_out, proj_in, proj_out, lengths):
    pair_count, side_count, seq_len, layer_count, _ = acts_in.shape
    in_coords = jnp.einsum("pstld,ldr->pstlr", acts_in, proj_in, preferred_element_type=jnp.float32)
    out_coords = jnp.einsum(
        "pstld,ldr->pstlr", grads_out, proj_out, preferred_element_type=jnp.float32
    )
    position = jnp.arange(seq_len, dtype=jnp.int32)
    live = (position[None, None, :] < lengths[:, :, None]).astype(jnp.float32)
    signs = 1.0 - 2.0 * jnp.arange(side_count, dtype=jnp.float32)
    kron_grads = jnp.einsum("pst,pstlr,pstlk->plrk", live * signs[:, None], out_coords, in_coords)
    return kron_grads.reshape(pair_count, -1).astype(jnp.bfloat16)


def local(acts_in, grads_out, proj_in, proj_out, query_grads, margin, labels, lengths):
    pair_count, side_count, _, layer_count, _ = acts_in.shape
    rank = proj_in.shape[2]
    dp_size, layer_size = lax.axis_size("dp"), lax.axis_size("layer")
    block = query_grads.reshape(query_grads.shape[0], -1)
    one_each = pair_count == layer_count == 1 and side_count == 2
    form = pair_gradient if one_each else pair_gradients
    grad_rows = form(acts_in, grads_out, proj_in, proj_out, lengths)
    scale = rank * math.sqrt(layer_count * layer_size) * math.sqrt(acts_in.shape[2])
    if one_each and dp_size == layer_size == len(FIRST):
        return shared_scores(grad_rows, block, margin, labels, scale)
    factor = jax.nn.sigmoid(-margin) * jnp.where(labels == 0, 1.0, -1.0) / scale
    rows = lax.all_gather(grad_rows, "dp", axis=0, tiled=True)
    scores = jnp.einsum("pk,qk->pq", rows, block, preferred_element_type=jnp.float32)
    scores = lax.all_to_all(scores, "dp", split_axis=0, concat_axis=1, tiled=True)
    summed = lax.psum_scatter(scores, "layer", scatter_dimension=1, tiled=True)
    return summed * factor[:, None]


def solution(mesh):
    placed = (
        P(("groups", "dp"), None, None, "layer", None),
        P(("groups", "dp"), None, None, "layer", None),
        P("layer", None, None),
        P("layer", None, None),
        P("dp", "layer", None),
        P(("groups", "dp")),
        P(("groups", "dp")),
        P(("groups", "dp"), None),
    )
    return jax.shard_map(
        local, mesh=mesh, in_specs=placed, out_specs=P(("groups", "dp"), "layer"), check_vma=False
    )
```

```python
import functools
import math

import jax
import jax.numpy as jnp
from jax import lax
from jax.experimental import pallas as pl
from jax.experimental.pallas import tpu as pltpu
from jax.sharding import PartitionSpec as P

FIRST = ((2, 0, 1, 3), (0, 3, 2, 1), (1, 2, 3, 0), (3, 1, 0, 2))
SECOND = ((3, 1, 2, 0), (1, 2, 0, 3), (0, 3, 1, 2), (2, 0, 3, 1))
PARTS = 4


def pair_kernel(seq_len, acts, grads, proj_in, proj_out, lengths, out, *scratch):
    tokens_v, proj_v, turned_v, kron_v, lengths_s, sems = scratch
    tokens = acts.shape[0]
    rank, model_width = proj_in.shape
    limits = pltpu.make_async_copy(lengths, lengths_s, sems.at[4])
    loads = [
        pltpu.make_async_copy(src, dst.at[pl.ds(half * src.shape[0], src.shape[0])], sems.at[2 * i + half])
        for i, (pair, dst) in enumerate((((proj_in, proj_out), proj_v), ((acts, grads), tokens_v)))
        for half, src in enumerate(pair)
    ]
    limits.start()
    for i, copy in enumerate(loads):
        copy.start(priority=i % 2)
    limits.wait()
    token = lax.broadcasted_iota(jnp.int32, (tokens, 1), 0)
    side = token // seq_len
    live = token - side * seq_len < jnp.where(side == 0, lengths_s[0, 0], lengths_s[0, 1])
    weight = jnp.where(live, jnp.where(side == 0, 1.0, -1.0), 0.0)
    for copy in loads[:2]:
        copy.wait()
    width = model_width // PARTS
    for c in range(PARTS):
        turned_v[pl.ds(c * width, width), :] = proj_v[:, pl.ds(c * width, width)].T
    for copy in loads[2:]:
        copy.wait()
    coords = jnp.dot(tokens_v[...], turned_v[...], preferred_element_type=jnp.float32)
    in_coords = (coords[:tokens, :rank] * weight).astype(jnp.bfloat16)
    out_coords = coords[tokens:, rank:].astype(jnp.bfloat16)
    kron_v[...] = lax.dot_general(
        out_coords, in_coords, (((0,), (0,)), ((), ())), preferred_element_type=jnp.float32
    )
    half = rank // 2
    out[...] = jnp.concatenate([kron_v[pl.ds(i, half, stride=2), :] for i in range(2)], axis=1)


def pair_gradient(acts_in, grads_out, proj_in, proj_out, lengths):
    _, sides, seq_len, _, model_width = acts_in.shape
    rank = proj_in.shape[2]
    tokens = sides * seq_len
    rows = pl.pallas_call(
        functools.partial(pair_kernel, seq_len),
        out_shape=jax.ShapeDtypeStruct((rank // 2, 2 * rank), jnp.float32),
        in_specs=[pl.BlockSpec(memory_space=pl.ANY)] * 5,
        out_specs=pl.BlockSpec(memory_space=pltpu.VMEM),
        scratch_shapes=[
            pltpu.VMEM((2 * tokens, model_width), jnp.bfloat16),
            pltpu.VMEM((2 * rank, model_width), jnp.bfloat16),
            pltpu.VMEM((model_width, 2 * rank), jnp.bfloat16),
            pltpu.VMEM((rank, rank), jnp.float32),
            pltpu.SMEM((1, 2), jnp.int32),
            pltpu.SemaphoreType.DMA((5,)),
        ],
        compiler_params=pltpu.CompilerParams(vmem_limit_bytes=32 * 1024 * 1024),
        cost_estimate=pl.CostEstimate(
            flops=4 * tokens * model_width * rank,
            bytes_accessed=4 * (tokens + rank) * model_width,
            transcendentals=0,
        ),
    )(
        *(
            pltpu.with_memory_space_constraint(x, pltpu.HBM)
            for x in (
                acts_in.reshape(tokens, model_width),
                grads_out.reshape(tokens, model_width),
                jnp.swapaxes(proj_in, 1, 2).reshape(rank, model_width),
                jnp.swapaxes(proj_out, 1, 2).reshape(rank, model_width),
                lengths,
            )
        )
    )
    return lax.optimization_barrier(rows.reshape(1, rank * rank))


def swap(x):
    return lax.ppermute(x, "layer", [(i, i ^ 1) for i in range(lax.axis_size("layer"))])


def own_places(slot):
    return [(d, i) for d, row in enumerate(slot) for i, pair in enumerate(row) if pair == d]


def fetch_pair(x, slot):
    count = len(slot)
    moves = [
        (slot[d][i] * count + i, d * count + i) for d in range(count) for i in range(count) if slot[d][i] != d
    ]
    own = [d * count + i for d, i in own_places(slot)]
    fill = zip(own, own[1::-1] + own[:1:-1])
    return lax.ppermute(x, ("dp", "layer"), moves + list(fill))


def to_owner(x, slot):
    count = len(slot)
    moves = [(d * count + i, slot[d][i] * count + d) for d in range(count) for i in range(count)]
    return lax.ppermute(x, ("dp", "layer"), moves)


def factor_kernel(scale, margin, label, rows, factor):
    sign = jnp.where(label[0] == 0, 1.0, -1.0)
    factor[...] = sign / ((1.0 + jnp.exp(jnp.full(factor.shape, margin[0], jnp.float32))) * scale)


def shared_scores(own_row, own_block, margin, labels, scale):
    blocks = own_block, swap(own_block)
    rows = jnp.concatenate([own_row, swap(own_row)], axis=0).astype(jnp.bfloat16)
    first, second = fetch_pair(rows, FIRST), fetch_pair(rows, SECOND)
    factor = pl.pallas_call(
        functools.partial(factor_kernel, scale),
        out_shape=jax.ShapeDtypeStruct(own_block.shape[:1], jnp.float32),
        in_specs=[pl.BlockSpec(memory_space=pltpu.SMEM)] * 2 + [pl.BlockSpec(memory_space=pl.ANY)],
        out_specs=pl.BlockSpec(memory_space=pltpu.VMEM),
        compiler_params=pltpu.CompilerParams(vmem_limit_bytes=1024 * 1024),
        cost_estimate=pl.CostEstimate(flops=0, bytes_accessed=4 * own_block.shape[0], transcendentals=0),
    )(margin, labels, rows)
    here = lax.axis_index("dp") * len(FIRST) + lax.axis_index("layer")

    def score(got, slot):
        is_own = functools.reduce(jnp.logical_or, [here == d * len(slot) + i for d, i in own_places(slot)])
        return sum(
            jnp.einsum("k,qk->q", jnp.where(is_own, mine, row), block, preferred_element_type=jnp.float32)
            for mine, row, block in zip(rows, got, blocks)
        )

    first, second = to_owner(score(first, FIRST), FIRST), to_owner(score(second, SECOND), SECOND)
    return ((first + second) * factor)[None]


def pair_gradients(acts_in, grads_out, proj_in, proj_out, lengths):
    pair_count, side_count, seq_len, layer_count, _ = acts_in.shape
    in_coords = jnp.einsum("pstld,ldr->pstlr", acts_in, proj_in, preferred_element_type=jnp.float32)
    out_coords = jnp.einsum(
        "pstld,ldr->pstlr", grads_out, proj_out, preferred_element_type=jnp.float32
    )
    position = jnp.arange(seq_len, dtype=jnp.int32)
    live = (position[None, None, :] < lengths[:, :, None]).astype(jnp.float32)
    signs = 1.0 - 2.0 * jnp.arange(side_count, dtype=jnp.float32)
    kron_grads = jnp.einsum("pst,pstlr,pstlk->plrk", live * signs[:, None], out_coords, in_coords)
    return kron_grads.reshape(pair_count, -1).astype(jnp.bfloat16)


def local(acts_in, grads_out, proj_in, proj_out, query_grads, margin, labels, lengths):
    pair_count, side_count, _, layer_count, _ = acts_in.shape
    rank = proj_in.shape[2]
    dp_size, layer_size = lax.axis_size("dp"), lax.axis_size("layer")
    block = query_grads.reshape(query_grads.shape[0], -1)
    one_each = pair_count == layer_count == 1 and side_count == 2
    form = pair_gradient if one_each else pair_gradients
    grad_rows = form(acts_in, grads_out, proj_in, proj_out, lengths)
    scale = rank * math.sqrt(layer_count * layer_size) * math.sqrt(acts_in.shape[2])
    if one_each and dp_size == layer_size == len(FIRST):
        return shared_scores(grad_rows, block, margin, labels, scale)
    factor = jax.nn.sigmoid(-margin) * jnp.where(labels == 0, 1.0, -1.0) / scale
    rows = lax.all_gather(grad_rows.astype(jnp.bfloat16), "dp", axis=0, tiled=True)
    scores = jnp.einsum("pk,qk->pq", rows, block, preferred_element_type=jnp.float32)
    scores = lax.all_to_all(scores, "dp", split_axis=0, concat_axis=1, tiled=True)
    summed = lax.psum_scatter(scores, "layer", scatter_dimension=1, tiled=True)
    return summed * factor[:, None]


def solution(mesh):
    placed = (
        P(("groups", "dp"), None, None, "layer", None),
        P(("groups", "dp"), None, None, "layer", None),
        P("layer", None, None),
        P("layer", None, None),
        P("dp", "layer", None),
        P(("groups", "dp")),
        P(("groups", "dp")),
        P(("groups", "dp"), None),
    )
    return jax.shard_map(
        local, mesh=mesh, in_specs=placed, out_specs=P(("groups", "dp"), "layer"), check_vma=False
    )
```

```python
import functools
import math

import jax
import jax.numpy as jnp
from jax import lax
from jax.experimental import pallas as pl
from jax.experimental.pallas import tpu as pltpu
from jax.sharding import PartitionSpec as P

FIRST = ((1, 0, 2, 3), (0, 3, 2, 1), (3, 2, 0, 1), (2, 1, 3, 0))
FIRST_FROM = ((0, 0, 3, 2), (1, 1, 2, 2), (0, 0, 2, 3), (1, 1, 3, 3))
SECOND = ((2, 3, 0, 1), (1, 2, 3, 0), (0, 1, 3, 2), (3, 0, 1, 2))
SECOND_FROM = ((0, 0, 3, 2), (1, 1, 3, 2), (0, 0, 2, 2), (1, 1, 3, 3))


PARTS = 4


def pair_kernel(seq_len, acts, grads, proj_in, proj_out, lengths, out, *scratch):
    tokens_v, proj_v, turned_v, kron_v, lengths_s, sems = scratch
    tokens = acts.shape[0]
    rank, model_width = proj_in.shape
    limits = pltpu.make_async_copy(lengths, lengths_s, sems.at[4])
    loads = [
        pltpu.make_async_copy(src, dst.at[pl.ds(half * src.shape[0], src.shape[0])], sems.at[2 * i + half])
        for i, (pair, dst) in enumerate((((proj_in, proj_out), proj_v), ((acts, grads), tokens_v)))
        for half, src in enumerate(pair)
    ]
    limits.start()
    for i, copy in enumerate(loads):
        copy.start(priority=i % 2)
    limits.wait()
    token = lax.broadcasted_iota(jnp.int32, (tokens, 1), 0)
    side = token // seq_len
    live = token - side * seq_len < jnp.where(side == 0, lengths_s[0, 0], lengths_s[0, 1])
    weight = jnp.where(live, jnp.where(side == 0, 1.0, -1.0), 0.0)
    for copy in loads[:2]:
        copy.wait()
    width = model_width // PARTS
    for c in range(PARTS):
        turned_v[pl.ds(c * width, width), :] = proj_v[:, pl.ds(c * width, width)].T
    for copy in loads[2:]:
        copy.wait()
    coords = jnp.dot(tokens_v[...], turned_v[...], preferred_element_type=jnp.float32)
    in_coords = (coords[:tokens, :rank] * weight).astype(jnp.bfloat16)
    out_coords = coords[tokens:, rank:].astype(jnp.bfloat16)
    kron_v[...] = lax.dot_general(
        out_coords, in_coords, (((0,), (0,)), ((), ())), preferred_element_type=jnp.float32
    )
    half = rank // 2
    out[...] = jnp.concatenate([kron_v[pl.ds(i, half, stride=2), :] for i in range(2)], axis=1)


def pair_gradient(acts_in, grads_out, proj_in, proj_out, lengths):
    _, sides, seq_len, _, model_width = acts_in.shape
    rank = proj_in.shape[2]
    tokens = sides * seq_len
    rows = pl.pallas_call(
        functools.partial(pair_kernel, seq_len),
        out_shape=jax.ShapeDtypeStruct((rank // 2, 2 * rank), jnp.float32),
        in_specs=[pl.BlockSpec(memory_space=pl.ANY)] * 5,
        out_specs=pl.BlockSpec(memory_space=pltpu.VMEM),
        scratch_shapes=[
            pltpu.VMEM((2 * tokens, model_width), jnp.bfloat16),
            pltpu.VMEM((2 * rank, model_width), jnp.bfloat16),
            pltpu.VMEM((model_width, 2 * rank), jnp.bfloat16),
            pltpu.VMEM((rank, rank), jnp.float32),
            pltpu.SMEM((1, 2), jnp.int32),
            pltpu.SemaphoreType.DMA((5,)),
        ],
        compiler_params=pltpu.CompilerParams(vmem_limit_bytes=32 * 1024 * 1024),
        cost_estimate=pl.CostEstimate(
            flops=4 * tokens * model_width * rank,
            bytes_accessed=4 * (tokens + rank) * model_width,
            transcendentals=0,
        ),
    )(
        *(
            pltpu.with_memory_space_constraint(x, pltpu.HBM)
            for x in (
                acts_in.reshape(tokens, model_width),
                grads_out.reshape(tokens, model_width),
                jnp.swapaxes(proj_in, 1, 2).reshape(rank, model_width),
                jnp.swapaxes(proj_out, 1, 2).reshape(rank, model_width),
                lengths,
            )
        )
    )
    return lax.optimization_barrier(rows.reshape(1, rank * rank))


def swap(x):
    return lax.ppermute(x, "layer", [(i, i ^ 1) for i in range(lax.axis_size("layer"))])


def fetch_pair(x, pairs, senders):
    count = len(pairs)
    places = [(d, i) for d in range(count) for i in range(count)]
    moves = [(pairs[d][i] * count + senders[d][i], d * count + i) for d, i in places]
    return lax.ppermute(x, ("dp", "layer"), moves)


def to_owner(x, slot):
    count = len(slot)
    moves = [(d * count + i, slot[d][i] * count + d) for d in range(count) for i in range(count)]
    return lax.ppermute(x, ("dp", "layer"), moves)


def factor_kernel(scale, margin, label, rows, factor):
    sign = jnp.where(label[0] == 0, 1.0, -1.0)
    factor[...] = sign / ((1.0 + jnp.exp(jnp.full(factor.shape, margin[0], jnp.float32))) * scale)


def shared_scores(own_row, own_block, margin, labels, scale):
    blocks = own_block, swap(own_block)
    rows = jnp.concatenate([own_row, swap(own_row)], axis=0).astype(jnp.bfloat16)
    first, second = fetch_pair(rows, FIRST, FIRST_FROM), fetch_pair(rows, SECOND, SECOND_FROM)
    factor = pl.pallas_call(
        functools.partial(factor_kernel, scale),
        out_shape=jax.ShapeDtypeStruct(own_block.shape[:1], jnp.float32),
        in_specs=[pl.BlockSpec(memory_space=pltpu.SMEM)] * 2 + [pl.BlockSpec(memory_space=pl.ANY)],
        out_specs=pl.BlockSpec(memory_space=pltpu.VMEM),
        compiler_params=pltpu.CompilerParams(vmem_limit_bytes=1024 * 1024),
        cost_estimate=pl.CostEstimate(flops=0, bytes_accessed=4 * own_block.shape[0], transcendentals=0),
    )(margin, labels, rows)
    here = lax.axis_index("dp") * len(FIRST) + lax.axis_index("layer")

    def score(got, senders):
        crossed = [d * len(row) + i for d, row in enumerate(senders) for i, sender in enumerate(row) if sender != i]
        is_crossed = functools.reduce(jnp.logical_or, [here == i for i in crossed])
        return sum(
            jnp.einsum("k,qk->q", jnp.where(is_crossed, got[1 - i], got[i]), block, preferred_element_type=jnp.float32)
            for i, block in enumerate(blocks)
        )

    first, second = score(first, FIRST_FROM), score(second, SECOND_FROM)
    return ((to_owner(first, FIRST) + to_owner(second, SECOND)) * factor)[None]


def pair_gradients(acts_in, grads_out, proj_in, proj_out, lengths):
    pair_count, side_count, seq_len, layer_count, _ = acts_in.shape
    in_coords = jnp.einsum("pstld,ldr->pstlr", acts_in, proj_in, preferred_element_type=jnp.float32)
    out_coords = jnp.einsum(
        "pstld,ldr->pstlr", grads_out, proj_out, preferred_element_type=jnp.float32
    )
    position = jnp.arange(seq_len, dtype=jnp.int32)
    live = (position[None, None, :] < lengths[:, :, None]).astype(jnp.float32)
    signs = 1.0 - 2.0 * jnp.arange(side_count, dtype=jnp.float32)
    kron_grads = jnp.einsum("pst,pstlr,pstlk->plrk", live * signs[:, None], out_coords, in_coords)
    return kron_grads.reshape(pair_count, -1).astype(jnp.bfloat16)


def local(acts_in, grads_out, proj_in, proj_out, query_grads, margin, labels, lengths):
    pair_count, side_count, _, layer_count, _ = acts_in.shape
    rank = proj_in.shape[2]
    dp_size, layer_size = lax.axis_size("dp"), lax.axis_size("layer")
    block = query_grads.reshape(query_grads.shape[0], -1)
    one_each = pair_count == layer_count == 1 and side_count == 2
    form = pair_gradient if one_each else pair_gradients
    grad_rows = form(acts_in, grads_out, proj_in, proj_out, lengths)
    scale = rank * math.sqrt(layer_count * layer_size) * math.sqrt(acts_in.shape[2])
    if one_each and dp_size == layer_size == len(FIRST):
        return shared_scores(grad_rows, block, margin, labels, scale)
    factor = jax.nn.sigmoid(-margin) * jnp.where(labels == 0, 1.0, -1.0) / scale
    rows = lax.all_gather(grad_rows.astype(jnp.bfloat16), "dp", axis=0, tiled=True)
    scores = jnp.einsum("pk,qk->pq", rows, block, preferred_element_type=jnp.float32)
    scores = lax.all_to_all(scores, "dp", split_axis=0, concat_axis=1, tiled=True)
    summed = lax.psum_scatter(scores, "layer", scatter_dimension=1, tiled=True)
    return summed * factor[:, None]


def solution(mesh):
    placed = (
        P(("groups", "dp"), None, None, "layer", None),
        P(("groups", "dp"), None, None, "layer", None),
        P("layer", None, None),
        P("layer", None, None),
        P("dp", "layer", None),
        P(("groups", "dp")),
        P(("groups", "dp")),
        P(("groups", "dp"), None),
    )
    return jax.shard_map(
        local, mesh=mesh, in_specs=placed, out_specs=P(("groups", "dp"), "layer"), check_vma=False
    )
```

```python
import functools
import math

import jax
import jax.numpy as jnp
from jax import lax
from jax.experimental import pallas as pl
from jax.experimental.pallas import tpu as pltpu
from jax.sharding import PartitionSpec as P

FIRST = ((3, 0, 1, 2), (0, 2, 3, 1), (3, 1, 0, 2), (2, 1, 3, 0))
FIRST_FROM = ((1, 0, 3, 3), (1, 0, 2, 2), (0, 0, 2, 2), (1, 1, 3, 3))
SECOND = ((1, 2, 3, 0), (1, 3, 2, 0), (2, 0, 3, 1), (3, 0, 1, 2))
SECOND_FROM = ((0, 0, 2, 2), (1, 0, 2, 3), (1, 0, 3, 2), (1, 1, 3, 3))


PARTS = 4


def pair_kernel(seq_len, acts, grads, proj_in, proj_out, lengths, out, *scratch):
    tokens_v, proj_v, turned_v, kron_v, lengths_s, sems = scratch
    tokens = acts.shape[0]
    rank, model_width = proj_in.shape
    limits = pltpu.make_async_copy(lengths, lengths_s, sems.at[4])
    loads = [
        pltpu.make_async_copy(src, dst.at[pl.ds(half * src.shape[0], src.shape[0])], sems.at[2 * i + half])
        for i, (pair, dst) in enumerate((((proj_in, proj_out), proj_v), ((acts, grads), tokens_v)))
        for half, src in enumerate(pair)
    ]
    limits.start()
    for i, copy in enumerate(loads):
        copy.start(priority=i % 2)
    limits.wait()
    token = lax.broadcasted_iota(jnp.int32, (tokens, 1), 0)
    side = token // seq_len
    live = token - side * seq_len < jnp.where(side == 0, lengths_s[0, 0], lengths_s[0, 1])
    weight = jnp.where(live, jnp.where(side == 0, 1.0, -1.0), 0.0)
    for copy in loads[:2]:
        copy.wait()
    width = model_width // PARTS
    for c in range(PARTS):
        turned_v[pl.ds(c * width, width), :] = proj_v[:, pl.ds(c * width, width)].T
    coords = []
    for half, copy in enumerate(loads[2:]):
        copy.wait()
        part = tokens_v[pl.ds(half * tokens, tokens), :]
        coords.append(jnp.dot(part, turned_v[...], preferred_element_type=jnp.float32))
    in_coords = (coords[0][:, :rank] * weight).astype(jnp.bfloat16)
    out_coords = coords[1][:, rank:].astype(jnp.bfloat16)
    kron_v[...] = lax.dot_general(
        out_coords, in_coords, (((0,), (0,)), ((), ())), preferred_element_type=jnp.float32
    )
    half = rank // 2
    out[...] = jnp.concatenate([kron_v[pl.ds(i, half, stride=2), :] for i in range(2)], axis=1)


def pair_gradient(acts_in, grads_out, proj_in, proj_out, lengths):
    _, sides, seq_len, _, model_width = acts_in.shape
    rank = proj_in.shape[2]
    tokens = sides * seq_len
    rows = pl.pallas_call(
        functools.partial(pair_kernel, seq_len),
        out_shape=jax.ShapeDtypeStruct((rank // 2, 2 * rank), jnp.float32),
        in_specs=[pl.BlockSpec(memory_space=pl.ANY)] * 5,
        out_specs=pl.BlockSpec(memory_space=pltpu.VMEM),
        scratch_shapes=[
            pltpu.VMEM((2 * tokens, model_width), jnp.bfloat16),
            pltpu.VMEM((2 * rank, model_width), jnp.bfloat16),
            pltpu.VMEM((model_width, 2 * rank), jnp.bfloat16),
            pltpu.VMEM((rank, rank), jnp.float32),
            pltpu.SMEM((1, 2), jnp.int32),
            pltpu.SemaphoreType.DMA((5,)),
        ],
        compiler_params=pltpu.CompilerParams(vmem_limit_bytes=32 * 1024 * 1024),
        cost_estimate=pl.CostEstimate(
            flops=4 * tokens * model_width * rank,
            bytes_accessed=4 * (tokens + rank) * model_width,
            transcendentals=0,
        ),
    )(
        *(
            pltpu.with_memory_space_constraint(x, pltpu.HBM)
            for x in (
                acts_in.reshape(tokens, model_width),
                grads_out.reshape(tokens, model_width),
                jnp.swapaxes(proj_in, 1, 2).reshape(rank, model_width),
                jnp.swapaxes(proj_out, 1, 2).reshape(rank, model_width),
                lengths,
            )
        )
    )
    return lax.optimization_barrier(rows.reshape(1, rank * rank))


def swap(x):
    return lax.ppermute(x, "layer", [(i, i ^ 1) for i in range(lax.axis_size("layer"))])


def fetch_pair(x, pairs, senders):
    count = len(pairs)
    places = [(d, i) for d in range(count) for i in range(count)]
    moves = [(pairs[d][i] * count + senders[d][i], d * count + i) for d, i in places]
    return lax.ppermute(x, ("dp", "layer"), moves)


def to_owner(x, slot):
    count = len(slot)
    moves = [(d * count + i, slot[d][i] * count + d) for d in range(count) for i in range(count)]
    return lax.ppermute(x, ("dp", "layer"), moves)


def sign_kernel(scale, label, rows, factor):
    factor[...] = jnp.full(factor.shape, jnp.where(label[0] == 0, 1.0, -1.0) / scale, jnp.float32)


def shared_scores(own_row, own_block, margin, labels, scale):
    blocks = own_block, swap(own_block)
    rows = jnp.concatenate([own_row, swap(own_row)], axis=0) * jax.nn.sigmoid(-margin)[:, None]
    rows = rows.astype(jnp.bfloat16)
    first, second = fetch_pair(rows, FIRST, FIRST_FROM), fetch_pair(rows, SECOND, SECOND_FROM)
    factor = pl.pallas_call(
        functools.partial(sign_kernel, scale),
        out_shape=jax.ShapeDtypeStruct(own_block.shape[:1], jnp.float32),
        in_specs=[pl.BlockSpec(memory_space=pltpu.SMEM), pl.BlockSpec(memory_space=pl.ANY)],
        out_specs=pl.BlockSpec(memory_space=pltpu.VMEM),
        compiler_params=pltpu.CompilerParams(vmem_limit_bytes=1024 * 1024),
        cost_estimate=pl.CostEstimate(flops=0, bytes_accessed=4 * own_block.shape[0], transcendentals=0),
    )(labels, rows)
    here = lax.axis_index("dp") * len(FIRST) + lax.axis_index("layer")

    def score(got, senders):
        crossed = [d * len(row) + i for d, row in enumerate(senders) for i, sender in enumerate(row) if sender != i]
        is_crossed = functools.reduce(jnp.logical_or, [here == i for i in crossed])
        return sum(
            jnp.einsum("k,qk->q", jnp.where(is_crossed, got[1 - i], got[i]), block, preferred_element_type=jnp.float32)
            for i, block in enumerate(blocks)
        )

    first, second = score(first, FIRST_FROM), score(second, SECOND_FROM)
    return ((to_owner(first, FIRST) + to_owner(second, SECOND)) * factor)[None]


def pair_gradients(acts_in, grads_out, proj_in, proj_out, lengths):
    pair_count, side_count, seq_len, layer_count, _ = acts_in.shape
    in_coords = jnp.einsum("pstld,ldr->pstlr", acts_in, proj_in, preferred_element_type=jnp.float32)
    out_coords = jnp.einsum(
        "pstld,ldr->pstlr", grads_out, proj_out, preferred_element_type=jnp.float32
    )
    position = jnp.arange(seq_len, dtype=jnp.int32)
    live = (position[None, None, :] < lengths[:, :, None]).astype(jnp.float32)
    signs = 1.0 - 2.0 * jnp.arange(side_count, dtype=jnp.float32)
    kron_grads = jnp.einsum("pst,pstlr,pstlk->plrk", live * signs[:, None], out_coords, in_coords)
    return kron_grads.reshape(pair_count, -1).astype(jnp.bfloat16)


def local(acts_in, grads_out, proj_in, proj_out, query_grads, margin, labels, lengths):
    pair_count, side_count, _, layer_count, _ = acts_in.shape
    rank = proj_in.shape[2]
    dp_size, layer_size = lax.axis_size("dp"), lax.axis_size("layer")
    block = query_grads.reshape(query_grads.shape[0], -1)
    one_each = pair_count == layer_count == 1 and side_count == 2
    form = pair_gradient if one_each else pair_gradients
    grad_rows = form(acts_in, grads_out, proj_in, proj_out, lengths)
    scale = rank * math.sqrt(layer_count * layer_size) * math.sqrt(acts_in.shape[2])
    if one_each and dp_size == layer_size == len(FIRST):
        return shared_scores(grad_rows, block, margin, labels, scale)
    factor = jax.nn.sigmoid(-margin) * jnp.where(labels == 0, 1.0, -1.0) / scale
    rows = lax.all_gather(grad_rows.astype(jnp.bfloat16), "dp", axis=0, tiled=True)
    scores = jnp.einsum("pk,qk->pq", rows, block, preferred_element_type=jnp.float32)
    scores = lax.all_to_all(scores, "dp", split_axis=0, concat_axis=1, tiled=True)
    summed = lax.psum_scatter(scores, "layer", scatter_dimension=1, tiled=True)
    return summed * factor[:, None]


def solution(mesh):
    placed = (
        P(("groups", "dp"), None, None, "layer", None),
        P(("groups", "dp"), None, None, "layer", None),
        P("layer", None, None),
        P("layer", None, None),
        P("dp", "layer", None),
        P(("groups", "dp")),
        P(("groups", "dp")),
        P(("groups", "dp"), None),
    )
    return jax.shard_map(
        local, mesh=mesh, in_specs=placed, out_specs=P(("groups", "dp"), "layer"), check_vma=False
    )
```

```python
import functools
import math

import jax
import jax.numpy as jnp
from jax import lax
from jax.experimental import pallas as pl
from jax.experimental.pallas import tpu as pltpu
from jax.sharding import PartitionSpec as P

FIRST = ((2, 3, 0, 1), (1, 2, 3, 0), (0, 1, 3, 2), (3, 0, 1, 2))
FIRST_FROM = ((0, 0, 3, 2), (1, 1, 3, 2), (0, 0, 2, 2), (1, 1, 3, 3))
SECOND = ((1, 0, 2, 3), (0, 3, 2, 1), (3, 2, 0, 1), (2, 1, 3, 0))
SECOND_FROM = ((0, 0, 3, 2), (1, 1, 2, 2), (0, 0, 2, 3), (1, 1, 3, 3))


PARTS = 4


def pair_kernel(seq_len, acts, grads, proj_in, proj_out, lengths, out, *scratch):
    tokens_v, proj_v, turned_v, kron_v, lengths_s, sems = scratch
    tokens = acts.shape[0]
    rank, model_width = proj_in.shape
    limits = pltpu.make_async_copy(lengths, lengths_s, sems.at[4])
    loads = [
        pltpu.make_async_copy(src, dst.at[pl.ds(half * src.shape[0], src.shape[0])], sems.at[2 * i + half])
        for i, (pair, dst) in enumerate((((proj_in, proj_out), proj_v), ((acts, grads), tokens_v)))
        for half, src in enumerate(pair)
    ]
    limits.start()
    for i, copy in enumerate(loads):
        copy.start(priority=i % 2)
    limits.wait()
    token = lax.broadcasted_iota(jnp.int32, (tokens, 1), 0)
    side = token // seq_len
    live = token - side * seq_len < jnp.where(side == 0, lengths_s[0, 0], lengths_s[0, 1])
    weight = jnp.where(live, jnp.where(side == 0, 1.0, -1.0), 0.0)
    for copy in loads[:2]:
        copy.wait()
    width = model_width // PARTS
    for c in range(PARTS):
        turned_v[pl.ds(c * width, width), :] = proj_v[:, pl.ds(c * width, width)].T
    for copy in loads[2:]:
        copy.wait()
    coords = jnp.dot(tokens_v[...], turned_v[...], preferred_element_type=jnp.float32)
    in_coords = (coords[:tokens, :rank] * weight).astype(jnp.bfloat16)
    out_coords = coords[tokens:, rank:].astype(jnp.bfloat16)
    kron_v[...] = lax.dot_general(
        out_coords, in_coords, (((0,), (0,)), ((), ())), preferred_element_type=jnp.float32
    )
    half = rank // 2
    out[...] = jnp.concatenate([kron_v[pl.ds(i, half, stride=2), :] for i in range(2)], axis=1)


def pair_gradient(acts_in, grads_out, proj_in, proj_out, lengths):
    _, sides, seq_len, _, model_width = acts_in.shape
    rank = proj_in.shape[2]
    tokens = sides * seq_len
    rows = pl.pallas_call(
        functools.partial(pair_kernel, seq_len),
        out_shape=jax.ShapeDtypeStruct((rank // 2, 2 * rank), jnp.float32),
        in_specs=[pl.BlockSpec(memory_space=pl.ANY)] * 5,
        out_specs=pl.BlockSpec(memory_space=pltpu.VMEM),
        scratch_shapes=[
            pltpu.VMEM((2 * tokens, model_width), jnp.bfloat16),
            pltpu.VMEM((2 * rank, model_width), jnp.bfloat16),
            pltpu.VMEM((model_width, 2 * rank), jnp.bfloat16),
            pltpu.VMEM((rank, rank), jnp.float32),
            pltpu.SMEM((1, 2), jnp.int32),
            pltpu.SemaphoreType.DMA((5,)),
        ],
        compiler_params=pltpu.CompilerParams(vmem_limit_bytes=32 * 1024 * 1024),
        cost_estimate=pl.CostEstimate(
            flops=4 * tokens * model_width * rank,
            bytes_accessed=4 * (tokens + rank) * model_width,
            transcendentals=0,
        ),
    )(
        *(
            pltpu.with_memory_space_constraint(x, pltpu.HBM)
            for x in (
                acts_in.reshape(tokens, model_width),
                grads_out.reshape(tokens, model_width),
                jnp.swapaxes(proj_in, 1, 2).reshape(rank, model_width),
                jnp.swapaxes(proj_out, 1, 2).reshape(rank, model_width),
                lengths,
            )
        )
    )
    return lax.optimization_barrier(rows.reshape(1, rank * rank))


def swap(x):
    return lax.ppermute(x, "layer", [(i, i ^ 1) for i in range(lax.axis_size("layer"))])


def fetch_pair(x, pairs, senders):
    count = len(pairs)
    places = [(d, i) for d in range(count) for i in range(count)]
    moves = [(pairs[d][i] * count + senders[d][i], d * count + i) for d, i in places]
    return lax.ppermute(x, ("dp", "layer"), moves)


def to_owner(x, slot):
    count = len(slot)
    moves = [(d * count + i, slot[d][i] * count + d) for d in range(count) for i in range(count)]
    return lax.ppermute(x, ("dp", "layer"), moves)


def slot_kernel(senders, rows, own_block, other_block, out):
    here = lax.axis_index("dp") * len(senders) + lax.axis_index("layer")
    crossed = [d * len(row) + i for d, row in enumerate(senders) for i, sender in enumerate(row) if sender != i]
    is_crossed = functools.reduce(jnp.logical_or, [here == i for i in crossed])
    one, two = (
        lax.dot_general(rows[...], block[...], (((1,), (1,)), ((), ())), preferred_element_type=jnp.float32)
        for block in (own_block, other_block)
    )
    out[...] = jnp.where(is_crossed, one[1:] + two[:1], one[:1] + two[1:])


def factor_kernel(scale, margin, label, rows, factor):
    sign = jnp.where(label[0] == 0, 1.0, -1.0)
    factor[...] = sign / ((1.0 + jnp.exp(jnp.full(factor.shape, margin[0], jnp.float32))) * scale)


def shared_scores(own_row, own_block, margin, labels, scale):
    blocks = own_block, swap(own_block)
    rows = jnp.concatenate([own_row, swap(own_row)], axis=0).astype(jnp.bfloat16)
    first, second = fetch_pair(rows, FIRST, FIRST_FROM), fetch_pair(rows, SECOND, SECOND_FROM)
    factor = pl.pallas_call(
        functools.partial(factor_kernel, scale),
        out_shape=jax.ShapeDtypeStruct(own_block.shape[:1], jnp.float32),
        in_specs=[pl.BlockSpec(memory_space=pltpu.SMEM)] * 2 + [pl.BlockSpec(memory_space=pl.ANY)],
        out_specs=pl.BlockSpec(memory_space=pltpu.VMEM),
        compiler_params=pltpu.CompilerParams(vmem_limit_bytes=1024 * 1024),
        cost_estimate=pl.CostEstimate(flops=0, bytes_accessed=4 * own_block.shape[0], transcendentals=0),
    )(margin, labels, rows)

    def score(got, senders):
        return pl.pallas_call(
            functools.partial(slot_kernel, senders),
            out_shape=jax.ShapeDtypeStruct((1, own_block.shape[0]), jnp.float32),
            in_specs=[pl.BlockSpec(memory_space=pltpu.VMEM)] * 3,
            out_specs=pl.BlockSpec(memory_space=pltpu.VMEM),
            compiler_params=pltpu.CompilerParams(vmem_limit_bytes=1024 * 1024),
            cost_estimate=pl.CostEstimate(flops=8 * own_block.size, bytes_accessed=4 * own_block.size, transcendentals=0),
        )(*(pltpu.with_memory_space_constraint(x, pltpu.VMEM) for x in (got, *blocks)))

    first, second = score(first, FIRST_FROM), score(second, SECOND_FROM)
    return (to_owner(first, FIRST) + to_owner(second, SECOND)) * factor[None]


def pair_gradients(acts_in, grads_out, proj_in, proj_out, lengths):
    pair_count, side_count, seq_len, layer_count, _ = acts_in.shape
    in_coords = jnp.einsum("pstld,ldr->pstlr", acts_in, proj_in, preferred_element_type=jnp.float32)
    out_coords = jnp.einsum(
        "pstld,ldr->pstlr", grads_out, proj_out, preferred_element_type=jnp.float32
    )
    position = jnp.arange(seq_len, dtype=jnp.int32)
    live = (position[None, None, :] < lengths[:, :, None]).astype(jnp.float32)
    signs = 1.0 - 2.0 * jnp.arange(side_count, dtype=jnp.float32)
    kron_grads = jnp.einsum("pst,pstlr,pstlk->plrk", live * signs[:, None], out_coords, in_coords)
    return kron_grads.reshape(pair_count, -1).astype(jnp.bfloat16)


def local(acts_in, grads_out, proj_in, proj_out, query_grads, margin, labels, lengths):
    pair_count, side_count, _, layer_count, _ = acts_in.shape
    rank = proj_in.shape[2]
    dp_size, layer_size = lax.axis_size("dp"), lax.axis_size("layer")
    block = query_grads.reshape(query_grads.shape[0], -1)
    one_each = pair_count == layer_count == 1 and side_count == 2
    form = pair_gradient if one_each else pair_gradients
    grad_rows = form(acts_in, grads_out, proj_in, proj_out, lengths)
    scale = rank * math.sqrt(layer_count * layer_size) * math.sqrt(acts_in.shape[2])
    if one_each and dp_size == layer_size == len(FIRST):
        return shared_scores(grad_rows, block, margin, labels, scale)
    factor = jax.nn.sigmoid(-margin) * jnp.where(labels == 0, 1.0, -1.0) / scale
    rows = lax.all_gather(grad_rows.astype(jnp.bfloat16), "dp", axis=0, tiled=True)
    scores = jnp.einsum("pk,qk->pq", rows, block, preferred_element_type=jnp.float32)
    scores = lax.all_to_all(scores, "dp", split_axis=0, concat_axis=1, tiled=True)
    summed = lax.psum_scatter(scores, "layer", scatter_dimension=1, tiled=True)
    return summed * factor[:, None]


def solution(mesh):
    placed = (
        P(("groups", "dp"), None, None, "layer", None),
        P(("groups", "dp"), None, None, "layer", None),
        P("layer", None, None),
        P("layer", None, None),
        P("dp", "layer", None),
        P(("groups", "dp")),
        P(("groups", "dp")),
        P(("groups", "dp"), None),
    )
    return jax.shard_map(
        local, mesh=mesh, in_specs=placed, out_specs=P(("groups", "dp"), "layer"), check_vma=False
    )
```

```python
import functools
import math

import jax
import jax.numpy as jnp
from jax import lax
from jax.experimental import pallas as pl
from jax.experimental.pallas import tpu as pltpu
from jax.sharding import PartitionSpec as P

FIRST = ((2, 3, 0, 1), (1, 2, 3, 0), (0, 1, 3, 2), (3, 0, 1, 2))
FIRST_FROM = ((0, 0, 3, 2), (1, 1, 3, 2), (0, 0, 2, 2), (1, 1, 3, 3))
SECOND = ((1, 0, 2, 3), (0, 3, 2, 1), (3, 2, 0, 1), (2, 1, 3, 0))
SECOND_FROM = ((0, 0, 3, 2), (1, 1, 2, 2), (0, 0, 2, 3), (1, 1, 3, 3))


PARTS = 4


def pair_kernel(seq_len, acts, grads, proj_in, proj_out, lengths, out, *scratch):
    tokens_v, proj_v, turned_v, square_v, lengths_s, sems = scratch
    tokens = acts.shape[0]
    rank, model_width = proj_in.shape
    limits = pltpu.make_async_copy(lengths, lengths_s, sems.at[4])
    loads = [
        pltpu.make_async_copy(src, dst.at[pl.ds(half * src.shape[0], src.shape[0])], sems.at[2 * i + half])
        for i, (pair, dst) in enumerate((((proj_in, proj_out), proj_v), ((acts, grads), tokens_v)))
        for half, src in enumerate(pair)
    ]
    limits.start()
    for i, copy in enumerate(loads):
        copy.start(priority=i % 2)
    limits.wait()
    token = lax.broadcasted_iota(jnp.int32, (tokens, 1), 0)
    side = token // seq_len
    live = token - side * seq_len < jnp.where(side == 0, lengths_s[0, 0], lengths_s[0, 1])
    weight = jnp.where(live, jnp.where(side == 0, 1.0, -1.0), 0.0)
    for copy in loads[:2]:
        copy.wait()
    width = model_width // PARTS
    for c in range(PARTS):
        turned_v[pl.ds(c * width, width), :] = proj_v[:, pl.ds(c * width, width)].T
    for copy in loads[2:]:
        copy.wait()
    coords = jnp.dot(tokens_v[...], turned_v[...], preferred_element_type=jnp.float32)
    square_v[...] = lax.dot_general(
        coords[tokens:].astype(jnp.bfloat16),
        (coords[:tokens] * weight).astype(jnp.bfloat16),
        (((0,), (0,)), ((), ())),
        preferred_element_type=jnp.float32,
    )
    rows = [square_v[pl.ds(rank + i, rank // 2, stride=2), :] for i in range(2)]
    out[...] = jnp.concatenate([x[:, :rank] for x in rows], axis=1)


def pair_gradient(acts_in, grads_out, proj_in, proj_out, lengths):
    _, sides, seq_len, _, model_width = acts_in.shape
    rank = proj_in.shape[2]
    tokens = sides * seq_len
    rows = pl.pallas_call(
        functools.partial(pair_kernel, seq_len),
        out_shape=jax.ShapeDtypeStruct((rank // 2, 2 * rank), jnp.float32),
        in_specs=[pl.BlockSpec(memory_space=pl.ANY)] * 5,
        out_specs=pl.BlockSpec(memory_space=pltpu.VMEM),
        scratch_shapes=[
            pltpu.VMEM((2 * tokens, model_width), jnp.bfloat16),
            pltpu.VMEM((2 * rank, model_width), jnp.bfloat16),
            pltpu.VMEM((model_width, 2 * rank), jnp.bfloat16),
            pltpu.VMEM((2 * rank, 2 * rank), jnp.float32),
            pltpu.SMEM((1, 2), jnp.int32),
            pltpu.SemaphoreType.DMA((5,)),
        ],
        compiler_params=pltpu.CompilerParams(vmem_limit_bytes=32 * 1024 * 1024),
        cost_estimate=pl.CostEstimate(
            flops=4 * tokens * model_width * rank,
            bytes_accessed=4 * (tokens + rank) * model_width,
            transcendentals=0,
        ),
    )(
        *(
            pltpu.with_memory_space_constraint(x, pltpu.HBM)
            for x in (
                acts_in.reshape(tokens, model_width),
                grads_out.reshape(tokens, model_width),
                jnp.swapaxes(proj_in, 1, 2).reshape(rank, model_width),
                jnp.swapaxes(proj_out, 1, 2).reshape(rank, model_width),
                lengths,
            )
        )
    )
    return lax.optimization_barrier(rows.reshape(1, rank * rank))


def swap(x):
    return lax.ppermute(x, "layer", [(i, i ^ 1) for i in range(lax.axis_size("layer"))])


def fetch_pair(x, pairs, senders):
    count = len(pairs)
    places = [(d, i) for d in range(count) for i in range(count)]
    moves = [(pairs[d][i] * count + senders[d][i], d * count + i) for d, i in places]
    return lax.ppermute(x, ("dp", "layer"), moves)


def to_owner(x, slot):
    count = len(slot)
    moves = [(d * count + i, slot[d][i] * count + d) for d in range(count) for i in range(count)]
    return lax.ppermute(x, ("dp", "layer"), moves)


def slot_kernel(senders, rows, own_block, other_block, out):
    here = lax.axis_index("dp") * len(senders) + lax.axis_index("layer")
    crossed = [d * len(row) + i for d, row in enumerate(senders) for i, sender in enumerate(row) if sender != i]
    is_crossed = functools.reduce(jnp.logical_or, [here == i for i in crossed])
    one, two = (
        lax.dot_general(rows[...], block[...], (((1,), (1,)), ((), ())), preferred_element_type=jnp.float32)
        for block in (own_block, other_block)
    )
    out[...] = jnp.where(is_crossed, one[1:] + two[:1], one[:1] + two[1:])


def factor_kernel(scale, margin, label, rows, factor):
    sign = jnp.where(label[0] == 0, 1.0, -1.0)
    factor[...] = sign / ((1.0 + jnp.exp(jnp.full(factor.shape, margin[0], jnp.float32))) * scale)


def shared_scores(own_row, own_block, margin, labels, scale):
    blocks = own_block, swap(own_block)
    rows = jnp.concatenate([own_row, swap(own_row)], axis=0).astype(jnp.bfloat16)
    first, second = fetch_pair(rows, FIRST, FIRST_FROM), fetch_pair(rows, SECOND, SECOND_FROM)
    factor = pl.pallas_call(
        functools.partial(factor_kernel, scale),
        out_shape=jax.ShapeDtypeStruct(own_block.shape[:1], jnp.float32),
        in_specs=[pl.BlockSpec(memory_space=pltpu.SMEM)] * 2 + [pl.BlockSpec(memory_space=pl.ANY)],
        out_specs=pl.BlockSpec(memory_space=pltpu.VMEM),
        compiler_params=pltpu.CompilerParams(vmem_limit_bytes=1024 * 1024),
        cost_estimate=pl.CostEstimate(flops=0, bytes_accessed=4 * own_block.shape[0], transcendentals=0),
    )(margin, labels, rows)

    def score(got, senders):
        return pl.pallas_call(
            functools.partial(slot_kernel, senders),
            out_shape=jax.ShapeDtypeStruct((1, own_block.shape[0]), jnp.float32),
            in_specs=[pl.BlockSpec(memory_space=pltpu.VMEM)] * 3,
            out_specs=pl.BlockSpec(memory_space=pltpu.VMEM),
            compiler_params=pltpu.CompilerParams(vmem_limit_bytes=1024 * 1024),
            cost_estimate=pl.CostEstimate(flops=8 * own_block.size, bytes_accessed=4 * own_block.size, transcendentals=0),
        )(*(pltpu.with_memory_space_constraint(x, pltpu.VMEM) for x in (got, *blocks)))

    first, second = score(first, FIRST_FROM), score(second, SECOND_FROM)
    return (to_owner(first, FIRST) + to_owner(second, SECOND)) * factor[None]


def pair_gradients(acts_in, grads_out, proj_in, proj_out, lengths):
    pair_count, side_count, seq_len, layer_count, _ = acts_in.shape
    in_coords = jnp.einsum("pstld,ldr->pstlr", acts_in, proj_in, preferred_element_type=jnp.float32)
    out_coords = jnp.einsum(
        "pstld,ldr->pstlr", grads_out, proj_out, preferred_element_type=jnp.float32
    )
    position = jnp.arange(seq_len, dtype=jnp.int32)
    live = (position[None, None, :] < lengths[:, :, None]).astype(jnp.float32)
    signs = 1.0 - 2.0 * jnp.arange(side_count, dtype=jnp.float32)
    kron_grads = jnp.einsum("pst,pstlr,pstlk->plrk", live * signs[:, None], out_coords, in_coords)
    return kron_grads.reshape(pair_count, -1).astype(jnp.bfloat16)


def local(acts_in, grads_out, proj_in, proj_out, query_grads, margin, labels, lengths):
    pair_count, side_count, _, layer_count, _ = acts_in.shape
    rank = proj_in.shape[2]
    dp_size, layer_size = lax.axis_size("dp"), lax.axis_size("layer")
    block = query_grads.reshape(query_grads.shape[0], -1)
    one_each = pair_count == layer_count == 1 and side_count == 2
    form = pair_gradient if one_each else pair_gradients
    grad_rows = form(acts_in, grads_out, proj_in, proj_out, lengths)
    scale = rank * math.sqrt(layer_count * layer_size) * math.sqrt(acts_in.shape[2])
    if one_each and dp_size == layer_size == len(FIRST):
        return shared_scores(grad_rows, block, margin, labels, scale)
    factor = jax.nn.sigmoid(-margin) * jnp.where(labels == 0, 1.0, -1.0) / scale
    rows = lax.all_gather(grad_rows.astype(jnp.bfloat16), "dp", axis=0, tiled=True)
    scores = jnp.einsum("pk,qk->pq", rows, block, preferred_element_type=jnp.float32)
    scores = lax.all_to_all(scores, "dp", split_axis=0, concat_axis=1, tiled=True)
    summed = lax.psum_scatter(scores, "layer", scatter_dimension=1, tiled=True)
    return summed * factor[:, None]


def solution(mesh):
    placed = (
        P(("groups", "dp"), None, None, "layer", None),
        P(("groups", "dp"), None, None, "layer", None),
        P("layer", None, None),
        P("layer", None, None),
        P("dp", "layer", None),
        P(("groups", "dp")),
        P(("groups", "dp")),
        P(("groups", "dp"), None),
    )
    return jax.shard_map(
        local, mesh=mesh, in_specs=placed, out_specs=P(("groups", "dp"), "layer"), check_vma=False
    )
```

```python
import functools
import math

import jax
import jax.numpy as jnp
from jax import lax
from jax.experimental import pallas as pl
from jax.experimental.pallas import tpu as pltpu
from jax.sharding import PartitionSpec as P

FIRST = ((2, 3, 0, 1), (1, 2, 3, 0), (0, 1, 3, 2), (3, 0, 1, 2))
FIRST_FROM = ((0, 0, 3, 2), (1, 1, 3, 2), (0, 0, 2, 2), (1, 1, 3, 3))
SECOND = ((1, 0, 2, 3), (0, 3, 2, 1), (3, 2, 0, 1), (2, 1, 3, 0))
SECOND_FROM = ((0, 0, 3, 2), (1, 1, 2, 2), (0, 0, 2, 3), (1, 1, 3, 3))


PARTS = 4


def pair_kernel(seq_len, acts, grads, proj_in, proj_out, queries, lengths, out, queries_out, *scratch):
    tokens_v, proj_v, turned_v, square_v, lengths_s, sems = scratch
    tokens = acts.shape[0]
    rank, model_width = proj_in.shape
    limits = pltpu.make_async_copy(lengths, lengths_s, sems.at[4])
    loads = [
        pltpu.make_async_copy(src, dst.at[pl.ds(half * src.shape[0], src.shape[0])], sems.at[2 * i + half])
        for i, (pair, dst) in enumerate((((proj_in, proj_out), proj_v), ((acts, grads), tokens_v)))
        for half, src in enumerate(pair)
    ]
    limits.start()
    for i, copy in enumerate(loads):
        copy.start(priority=i % 2)
    load_queries = pltpu.make_async_copy(queries, queries_out, sems.at[5])
    load_queries.start(priority=1)
    limits.wait()
    token = lax.broadcasted_iota(jnp.int32, (tokens, 1), 0)
    side = token // seq_len
    live = token - side * seq_len < jnp.where(side == 0, lengths_s[0, 0], lengths_s[0, 1])
    weight = jnp.where(live, jnp.where(side == 0, 1.0, -1.0), 0.0)
    for copy in loads[:2]:
        copy.wait()
    width = model_width // PARTS
    for c in range(PARTS):
        turned_v[pl.ds(c * width, width), :] = proj_v[:, pl.ds(c * width, width)].T
    for copy in loads[2:]:
        copy.wait()
    coords = jnp.dot(tokens_v[...], turned_v[...], preferred_element_type=jnp.float32)
    square_v[...] = lax.dot_general(
        coords[tokens:].astype(jnp.bfloat16),
        (coords[:tokens] * weight).astype(jnp.bfloat16),
        (((0,), (0,)), ((), ())),
        preferred_element_type=jnp.float32,
    )
    rows = [square_v[pl.ds(rank + i, rank // 2, stride=2), :] for i in range(2)]
    out[...] = jnp.concatenate([x[:, :rank] for x in rows], axis=1)
    load_queries.wait()


def pair_gradient(acts_in, grads_out, proj_in, proj_out, block, lengths):
    _, sides, seq_len, _, model_width = acts_in.shape
    rank = proj_in.shape[2]
    tokens = sides * seq_len
    rows, block = pl.pallas_call(
        functools.partial(pair_kernel, seq_len),
        out_shape=(
            jax.ShapeDtypeStruct((rank // 2, 2 * rank), jnp.float32),
            jax.ShapeDtypeStruct(block.shape, block.dtype),
        ),
        in_specs=[pl.BlockSpec(memory_space=pl.ANY)] * 6,
        out_specs=(pl.BlockSpec(memory_space=pltpu.VMEM),) * 2,
        scratch_shapes=[
            pltpu.VMEM((2 * tokens, model_width), jnp.bfloat16),
            pltpu.VMEM((2 * rank, model_width), jnp.bfloat16),
            pltpu.VMEM((model_width, 2 * rank), jnp.bfloat16),
            pltpu.VMEM((2 * rank, 2 * rank), jnp.float32),
            pltpu.SMEM((1, 2), jnp.int32),
            pltpu.SemaphoreType.DMA((6,)),
        ],
        compiler_params=pltpu.CompilerParams(vmem_limit_bytes=32 * 1024 * 1024),
        cost_estimate=pl.CostEstimate(
            flops=4 * tokens * model_width * rank,
            bytes_accessed=4 * (tokens + rank) * model_width,
            transcendentals=0,
        ),
    )(
        *(
            pltpu.with_memory_space_constraint(x, pltpu.HBM)
            for x in (
                acts_in.reshape(tokens, model_width),
                grads_out.reshape(tokens, model_width),
                jnp.swapaxes(proj_in, 1, 2).reshape(rank, model_width),
                jnp.swapaxes(proj_out, 1, 2).reshape(rank, model_width),
                block,
                lengths,
            )
        )
    )
    return lax.optimization_barrier(rows.reshape(1, rank * rank)), block


def swap(x):
    return lax.ppermute(x, "layer", [(i, i ^ 1) for i in range(lax.axis_size("layer"))])


def fetch_pair(x, pairs, senders):
    count = len(pairs)
    places = [(d, i) for d in range(count) for i in range(count)]
    moves = [(pairs[d][i] * count + senders[d][i], d * count + i) for d, i in places]
    return lax.ppermute(x, ("dp", "layer"), moves)


def to_owner(x, slot):
    count = len(slot)
    moves = [(d * count + i, slot[d][i] * count + d) for d in range(count) for i in range(count)]
    return lax.ppermute(x, ("dp", "layer"), moves)


def slot_kernel(senders, rows, own_block, other_block, out):
    here = lax.axis_index("dp") * len(senders) + lax.axis_index("layer")
    crossed = [d * len(row) + i for d, row in enumerate(senders) for i, sender in enumerate(row) if sender != i]
    is_crossed = functools.reduce(jnp.logical_or, [here == i for i in crossed])
    one, two = (
        lax.dot_general(rows[...], block[...], (((1,), (1,)), ((), ())), preferred_element_type=jnp.float32)
        for block in (own_block, other_block)
    )
    out[...] = jnp.where(is_crossed, one[1:] + two[:1], one[:1] + two[1:])


def factor_kernel(scale, margin, label, rows, factor):
    sign = jnp.where(label[0] == 0, 1.0, -1.0)
    factor[...] = sign / ((1.0 + jnp.exp(jnp.full(factor.shape, margin[0], jnp.float32))) * scale)


def shared_scores(own_row, own_block, margin, labels, scale):
    blocks = own_block, swap(own_block)
    rows = jnp.concatenate([own_row, swap(own_row)], axis=0).astype(jnp.bfloat16)
    first, second = fetch_pair(rows, FIRST, FIRST_FROM), fetch_pair(rows, SECOND, SECOND_FROM)
    factor = pl.pallas_call(
        functools.partial(factor_kernel, scale),
        out_shape=jax.ShapeDtypeStruct(own_block.shape[:1], jnp.float32),
        in_specs=[pl.BlockSpec(memory_space=pltpu.SMEM)] * 2 + [pl.BlockSpec(memory_space=pl.ANY)],
        out_specs=pl.BlockSpec(memory_space=pltpu.VMEM),
        compiler_params=pltpu.CompilerParams(vmem_limit_bytes=1024 * 1024),
        cost_estimate=pl.CostEstimate(flops=0, bytes_accessed=4 * own_block.shape[0], transcendentals=0),
    )(margin, labels, rows)


    def score(got, senders):
        return pl.pallas_call(
            functools.partial(slot_kernel, senders),
            out_shape=jax.ShapeDtypeStruct((1, own_block.shape[0]), jnp.float32),
            in_specs=[pl.BlockSpec(memory_space=pltpu.VMEM)] * 3,
            out_specs=pl.BlockSpec(memory_space=pltpu.VMEM),
            compiler_params=pltpu.CompilerParams(vmem_limit_bytes=1024 * 1024),
            cost_estimate=pl.CostEstimate(flops=8 * own_block.size, bytes_accessed=4 * own_block.size, transcendentals=0),
        )(*(pltpu.with_memory_space_constraint(x, pltpu.VMEM) for x in (got, *blocks)))

    first, second = score(first, FIRST_FROM), score(second, SECOND_FROM)
    return (to_owner(first, FIRST) + to_owner(second, SECOND)) * factor[None]


def pair_gradients(acts_in, grads_out, proj_in, proj_out, lengths):
    pair_count, side_count, seq_len, layer_count, _ = acts_in.shape
    in_coords = jnp.einsum("pstld,ldr->pstlr", acts_in, proj_in, preferred_element_type=jnp.float32)
    out_coords = jnp.einsum(
        "pstld,ldr->pstlr", grads_out, proj_out, preferred_element_type=jnp.float32
    )
    position = jnp.arange(seq_len, dtype=jnp.int32)
    live = (position[None, None, :] < lengths[:, :, None]).astype(jnp.float32)
    signs = 1.0 - 2.0 * jnp.arange(side_count, dtype=jnp.float32)
    kron_grads = jnp.einsum("pst,pstlr,pstlk->plrk", live * signs[:, None], out_coords, in_coords)
    return kron_grads.reshape(pair_count, -1).astype(jnp.bfloat16)


def local(acts_in, grads_out, proj_in, proj_out, query_grads, margin, labels, lengths):
    pair_count, side_count, _, layer_count, _ = acts_in.shape
    rank = proj_in.shape[2]
    dp_size, layer_size = lax.axis_size("dp"), lax.axis_size("layer")
    block = query_grads.reshape(query_grads.shape[0], -1)
    one_each = pair_count == layer_count == 1 and side_count == 2
    if one_each:
        grad_rows, block = pair_gradient(acts_in, grads_out, proj_in, proj_out, block, lengths)
    else:
        grad_rows = pair_gradients(acts_in, grads_out, proj_in, proj_out, lengths)
    scale = rank * math.sqrt(layer_count * layer_size) * math.sqrt(acts_in.shape[2])
    if one_each and dp_size == layer_size == len(FIRST):
        return shared_scores(grad_rows, block, margin, labels, scale)
    factor = jax.nn.sigmoid(-margin) * jnp.where(labels == 0, 1.0, -1.0) / scale
    rows = lax.all_gather(grad_rows.astype(jnp.bfloat16), "dp", axis=0, tiled=True)
    scores = jnp.einsum("pk,qk->pq", rows, block, preferred_element_type=jnp.float32)
    scores = lax.all_to_all(scores, "dp", split_axis=0, concat_axis=1, tiled=True)
    summed = lax.psum_scatter(scores, "layer", scatter_dimension=1, tiled=True)
    return summed * factor[:, None]


def solution(mesh):
    placed = (
        P(("groups", "dp"), None, None, "layer", None),
        P(("groups", "dp"), None, None, "layer", None),
        P("layer", None, None),
        P("layer", None, None),
        P("dp", "layer", None),
        P(("groups", "dp")),
        P(("groups", "dp")),
        P(("groups", "dp"), None),
    )
    return jax.shard_map(
        local, mesh=mesh, in_specs=placed, out_specs=P(("groups", "dp"), "layer"), check_vma=False
    )
```

```python
import functools
import math

import jax
import jax.numpy as jnp
from jax import lax
from jax.experimental import pallas as pl
from jax.experimental.pallas import tpu as pltpu
from jax.sharding import PartitionSpec as P

FIRST = ((2, 3, 0, 1), (1, 2, 3, 0), (0, 1, 3, 2), (3, 0, 1, 2))
FIRST_FROM = ((0, 0, 3, 2), (1, 1, 3, 2), (0, 0, 2, 2), (1, 1, 3, 3))
SECOND = ((1, 0, 2, 3), (0, 3, 2, 1), (3, 2, 0, 1), (2, 1, 3, 0))
SECOND_FROM = ((0, 0, 3, 2), (1, 1, 2, 2), (0, 0, 2, 3), (1, 1, 3, 3))


def pair_kernel(seq_len, acts, grads, proj_in, proj_out, lengths, out, *scratch):
    *held, square_v, lengths_s, sems = scratch
    limits = pltpu.make_async_copy(lengths, lengths_s, sems.at[len(held)])
    limits.start()
    loads = []
    for src, dst, queue in zip((acts, proj_in, grads, proj_out), held, (0, 1, 1, 0)):
        loads.append(pltpu.make_async_copy(src, dst, sems.at[len(loads)]))
        loads[-1].start(priority=queue)

    def project(first):
        for copy in loads[first : first + 2]:
            copy.wait()
        tokens, proj = held[first : first + 2]
        return lax.dot_general(
            tokens[...], proj[...], (((1,), (1,)), ((), ())), preferred_element_type=jnp.float32
        )

    coords = project(0)
    limits.wait()
    token = lax.broadcasted_iota(jnp.int32, (coords.shape[0], 1), 0)
    side = token // seq_len
    live = token - side * seq_len < jnp.where(side == 0, lengths_s[0, 0], lengths_s[0, 1])
    weight = jnp.where(live, jnp.where(side == 0, 1.0, -1.0), 0.0)
    in_coords = (coords * weight).astype(jnp.bfloat16)
    out_coords = project(2).astype(jnp.bfloat16)
    square_v[...] = lax.dot_general(
        out_coords, in_coords, (((0,), (0,)), ((), ())), preferred_element_type=jnp.float32
    )
    half = square_v.shape[0] // 2
    out[...] = jnp.concatenate([square_v[pl.ds(i, half, stride=2), :] for i in range(2)], axis=1)


def pair_gradient(acts_in, grads_out, proj_in, proj_out, lengths):
    _, sides, seq_len, _, model_width = acts_in.shape
    rank = proj_in.shape[2]
    tokens = sides * seq_len
    rows = pl.pallas_call(
        functools.partial(pair_kernel, seq_len),
        out_shape=jax.ShapeDtypeStruct((rank // 2, 2 * rank), jnp.float32),
        in_specs=[pl.BlockSpec(memory_space=pl.ANY)] * 5,
        out_specs=pl.BlockSpec(memory_space=pltpu.VMEM),
        scratch_shapes=[
            *(pltpu.VMEM((rows, model_width), jnp.bfloat16) for rows in (tokens, rank, tokens, rank)),
            pltpu.VMEM((rank, rank), jnp.float32),
            pltpu.SMEM((1, 2), jnp.int32),
            pltpu.SemaphoreType.DMA((5,)),
        ],
        compiler_params=pltpu.CompilerParams(vmem_limit_bytes=32 * 1024 * 1024),
        cost_estimate=pl.CostEstimate(
            flops=4 * tokens * model_width * rank,
            bytes_accessed=4 * (tokens + rank) * model_width,
            transcendentals=0,
        ),
    )(
        *(
            pltpu.with_memory_space_constraint(x, pltpu.HBM)
            for x in (
                acts_in.reshape(tokens, model_width),
                grads_out.reshape(tokens, model_width),
                jnp.swapaxes(proj_in, 1, 2).reshape(rank, model_width),
                jnp.swapaxes(proj_out, 1, 2).reshape(rank, model_width),
                lengths,
            )
        )
    )
    return lax.optimization_barrier(rows.reshape(1, rank * rank))


def swap(x):
    return lax.ppermute(x, "layer", [(i, i ^ 1) for i in range(lax.axis_size("layer"))])


def fetch_pair(x, pairs, senders):
    count = len(pairs)
    places = [(d, i) for d in range(count) for i in range(count)]
    moves = [(pairs[d][i] * count + senders[d][i], d * count + i) for d, i in places]
    return lax.ppermute(x, ("dp", "layer"), moves)


def to_owner(x, slot):
    count = len(slot)
    moves = [(d * count + i, slot[d][i] * count + d) for d in range(count) for i in range(count)]
    return lax.ppermute(x, ("dp", "layer"), moves)


def slot_kernel(senders, rows, own_block, other_block, out):
    here = lax.axis_index("dp") * len(senders) + lax.axis_index("layer")
    crossed = [d * len(row) + i for d, row in enumerate(senders) for i, sender in enumerate(row) if sender != i]
    is_crossed = functools.reduce(jnp.logical_or, [here == i for i in crossed])
    one, two = (
        lax.dot_general(rows[...], block[...], (((1,), (1,)), ((), ())), preferred_element_type=jnp.float32)
        for block in (own_block, other_block)
    )
    out[...] = jnp.where(is_crossed, one[1:] + two[:1], one[:1] + two[1:])


def factor_kernel(scale, margin, label, rows, factor):
    sign = jnp.where(label[0] == 0, 1.0, -1.0)
    factor[...] = sign / ((1.0 + jnp.exp(jnp.full(factor.shape, margin[0], jnp.float32))) * scale)


def shared_scores(own_row, own_block, margin, labels, scale):
    blocks = own_block, swap(own_block)
    rows = jnp.concatenate([own_row, swap(own_row)], axis=0).astype(jnp.bfloat16)
    first, second = fetch_pair(rows, FIRST, FIRST_FROM), fetch_pair(rows, SECOND, SECOND_FROM)
    factor = pl.pallas_call(
        functools.partial(factor_kernel, scale),
        out_shape=jax.ShapeDtypeStruct(own_block.shape[:1], jnp.float32),
        in_specs=[pl.BlockSpec(memory_space=pltpu.SMEM)] * 2 + [pl.BlockSpec(memory_space=pl.ANY)],
        out_specs=pl.BlockSpec(memory_space=pltpu.VMEM),
        compiler_params=pltpu.CompilerParams(vmem_limit_bytes=1024 * 1024),
        cost_estimate=pl.CostEstimate(flops=0, bytes_accessed=4 * own_block.shape[0], transcendentals=0),
    )(margin, labels, rows)

    def score(got, senders):
        return pl.pallas_call(
            functools.partial(slot_kernel, senders),
            out_shape=jax.ShapeDtypeStruct((1, own_block.shape[0]), jnp.float32),
            in_specs=[pl.BlockSpec(memory_space=pltpu.VMEM)] * 3,
            out_specs=pl.BlockSpec(memory_space=pltpu.VMEM),
            compiler_params=pltpu.CompilerParams(vmem_limit_bytes=1024 * 1024),
            cost_estimate=pl.CostEstimate(flops=8 * own_block.size, bytes_accessed=4 * own_block.size, transcendentals=0),
        )(*(pltpu.with_memory_space_constraint(x, pltpu.VMEM) for x in (got, *blocks)))

    first, second = score(first, FIRST_FROM), score(second, SECOND_FROM)
    return (to_owner(first, FIRST) + to_owner(second, SECOND)) * factor[None]


def pair_gradients(acts_in, grads_out, proj_in, proj_out, lengths):
    pair_count, side_count, seq_len, layer_count, _ = acts_in.shape
    in_coords = jnp.einsum("pstld,ldr->pstlr", acts_in, proj_in, preferred_element_type=jnp.float32)
    out_coords = jnp.einsum(
        "pstld,ldr->pstlr", grads_out, proj_out, preferred_element_type=jnp.float32
    )
    position = jnp.arange(seq_len, dtype=jnp.int32)
    live = (position[None, None, :] < lengths[:, :, None]).astype(jnp.float32)
    signs = 1.0 - 2.0 * jnp.arange(side_count, dtype=jnp.float32)
    kron_grads = jnp.einsum("pst,pstlr,pstlk->plrk", live * signs[:, None], out_coords, in_coords)
    return kron_grads.reshape(pair_count, -1).astype(jnp.bfloat16)


def local(acts_in, grads_out, proj_in, proj_out, query_grads, margin, labels, lengths):
    pair_count, side_count, _, layer_count, _ = acts_in.shape
    rank = proj_in.shape[2]
    dp_size, layer_size = lax.axis_size("dp"), lax.axis_size("layer")
    block = query_grads.reshape(query_grads.shape[0], -1)
    one_each = pair_count == layer_count == 1 and side_count == 2
    form = pair_gradient if one_each else pair_gradients
    grad_rows = form(acts_in, grads_out, proj_in, proj_out, lengths)
    scale = rank * math.sqrt(layer_count * layer_size) * math.sqrt(acts_in.shape[2])
    if one_each and dp_size == layer_size == len(FIRST):
        return shared_scores(grad_rows, block, margin, labels, scale)
    factor = jax.nn.sigmoid(-margin) * jnp.where(labels == 0, 1.0, -1.0) / scale
    rows = lax.all_gather(grad_rows.astype(jnp.bfloat16), "dp", axis=0, tiled=True)
    scores = jnp.einsum("pk,qk->pq", rows, block, preferred_element_type=jnp.float32)
    scores = lax.all_to_all(scores, "dp", split_axis=0, concat_axis=1, tiled=True)
    summed = lax.psum_scatter(scores, "layer", scatter_dimension=1, tiled=True)
    return summed * factor[:, None]


def solution(mesh):
    placed = (
        P(("groups", "dp"), None, None, "layer", None),
        P(("groups", "dp"), None, None, "layer", None),
        P("layer", None, None),
        P("layer", None, None),
        P("dp", "layer", None),
        P(("groups", "dp")),
        P(("groups", "dp")),
        P(("groups", "dp"), None),
    )
    return jax.shard_map(
        local, mesh=mesh, in_specs=placed, out_specs=P(("groups", "dp"), "layer"), check_vma=False
    )
```

```python
import functools
import math

import jax
import jax.numpy as jnp
from jax import lax
from jax.experimental import pallas as pl
from jax.experimental.pallas import tpu as pltpu
from jax.sharding import PartitionSpec as P

FIRST = ((2, 3, 0, 1), (1, 2, 3, 0), (0, 1, 3, 2), (3, 0, 1, 2))
FIRST_FROM = ((0, 0, 3, 2), (1, 1, 3, 2), (0, 0, 2, 2), (1, 1, 3, 3))
SECOND = ((1, 0, 2, 3), (0, 3, 2, 1), (3, 2, 0, 1), (2, 1, 3, 0))
SECOND_FROM = ((0, 0, 3, 2), (1, 1, 2, 2), (0, 0, 2, 3), (1, 1, 3, 3))


CHUNKS = 2


def pair_kernel(seq_len, acts, grads, proj_in, proj_out, lengths, out, *scratch):
    tokens_v, proj_v, square_v, lengths_s, sems, lengths_sem = scratch
    tokens = acts.shape[0]
    rank, model_width = proj_in.shape
    width = model_width // CHUNKS
    limits = pltpu.make_async_copy(lengths, lengths_s, lengths_sem)
    limits.start()
    loads = []
    for c in range(CHUNKS):
        part = pl.ds(c * width, width)
        loads.append([])
        for pair, dst in (((proj_in, proj_out), proj_v), ((acts, grads), tokens_v)):
            for half, src in enumerate(pair):
                to = dst.at[pl.ds(half * src.shape[0], src.shape[0]), part]
                loads[c].append(pltpu.make_async_copy(src.at[:, part], to, sems.at[c, len(loads[c])]))
                loads[c][-1].start(priority=CHUNKS - 1 - c)
    limits.wait()
    token = lax.broadcasted_iota(jnp.int32, (tokens, 1), 0)
    side = token // seq_len
    live = token - side * seq_len < jnp.where(side == 0, lengths_s[0, 0], lengths_s[0, 1])
    weight = jnp.where(live, jnp.where(side == 0, 1.0, -1.0), 0.0)
    coords = None
    for c, copies in enumerate(loads):
        for copy in copies:
            copy.wait()
        part = pl.ds(c * width, width)
        term = lax.dot_general(
            tokens_v[:, part], proj_v[:, part], (((1,), (1,)), ((), ())), preferred_element_type=jnp.float32
        )
        coords = term if coords is None else coords + term
    square_v[...] = lax.dot_general(
        coords[tokens:].astype(jnp.bfloat16),
        (coords[:tokens] * weight).astype(jnp.bfloat16),
        (((0,), (0,)), ((), ())),
        preferred_element_type=jnp.float32,
    )
    rows = [square_v[pl.ds(rank + i, rank // 2, stride=2), :] for i in range(2)]
    out[...] = jnp.concatenate([x[:, :rank] for x in rows], axis=1)


def pair_gradient(acts_in, grads_out, proj_in, proj_out, lengths):
    _, sides, seq_len, _, model_width = acts_in.shape
    rank = proj_in.shape[2]
    tokens = sides * seq_len
    rows = pl.pallas_call(
        functools.partial(pair_kernel, seq_len),
        out_shape=jax.ShapeDtypeStruct((rank // 2, 2 * rank), jnp.float32),
        in_specs=[pl.BlockSpec(memory_space=pl.ANY)] * 5,
        out_specs=pl.BlockSpec(memory_space=pltpu.VMEM),
        scratch_shapes=[
            pltpu.VMEM((2 * tokens, model_width), jnp.bfloat16),
            pltpu.VMEM((2 * rank, model_width), jnp.bfloat16),
            pltpu.VMEM((2 * rank, 2 * rank), jnp.float32),
            pltpu.SMEM((1, 2), jnp.int32),
            pltpu.SemaphoreType.DMA((CHUNKS, 4)),
            pltpu.SemaphoreType.DMA,
        ],
        compiler_params=pltpu.CompilerParams(vmem_limit_bytes=32 * 1024 * 1024),
        cost_estimate=pl.CostEstimate(
            flops=4 * tokens * model_width * rank,
            bytes_accessed=4 * (tokens + rank) * model_width,
            transcendentals=0,
        ),
    )(
        *(
            pltpu.with_memory_space_constraint(x, pltpu.HBM)
            for x in (
                acts_in.reshape(tokens, model_width),
                grads_out.reshape(tokens, model_width),
                jnp.swapaxes(proj_in, 1, 2).reshape(rank, model_width),
                jnp.swapaxes(proj_out, 1, 2).reshape(rank, model_width),
                lengths,
            )
        )
    )
    return lax.optimization_barrier(rows.reshape(1, rank * rank))


def swap(x):
    return lax.ppermute(x, "layer", [(i, i ^ 1) for i in range(lax.axis_size("layer"))])


def fetch_pair(x, pairs, senders):
    count = len(pairs)
    places = [(d, i) for d in range(count) for i in range(count)]
    moves = [(pairs[d][i] * count + senders[d][i], d * count + i) for d, i in places]
    return lax.ppermute(x, ("dp", "layer"), moves)


def to_owner(x, slot):
    count = len(slot)
    moves = [(d * count + i, slot[d][i] * count + d) for d in range(count) for i in range(count)]
    return lax.ppermute(x, ("dp", "layer"), moves)


def slot_kernel(senders, rows, own_block, other_block, out):
    here = lax.axis_index("dp") * len(senders) + lax.axis_index("layer")
    crossed = [d * len(row) + i for d, row in enumerate(senders) for i, sender in enumerate(row) if sender != i]
    is_crossed = functools.reduce(jnp.logical_or, [here == i for i in crossed])
    one, two = (
        lax.dot_general(rows[...], block[...], (((1,), (1,)), ((), ())), preferred_element_type=jnp.float32)
        for block in (own_block, other_block)
    )
    out[...] = jnp.where(is_crossed, one[1:] + two[:1], one[:1] + two[1:])


def factor_kernel(scale, margin, label, rows, factor):
    sign = jnp.where(label[0] == 0, 1.0, -1.0)
    factor[...] = sign / ((1.0 + jnp.exp(jnp.full(factor.shape, margin[0], jnp.float32))) * scale)


def shared_scores(own_row, own_block, margin, labels, scale):
    blocks = own_block, swap(own_block)
    rows = jnp.concatenate([own_row, swap(own_row)], axis=0).astype(jnp.bfloat16)
    first, second = fetch_pair(rows, FIRST, FIRST_FROM), fetch_pair(rows, SECOND, SECOND_FROM)
    factor = pl.pallas_call(
        functools.partial(factor_kernel, scale),
        out_shape=jax.ShapeDtypeStruct(own_block.shape[:1], jnp.float32),
        in_specs=[pl.BlockSpec(memory_space=pltpu.SMEM)] * 2 + [pl.BlockSpec(memory_space=pl.ANY)],
        out_specs=pl.BlockSpec(memory_space=pltpu.VMEM),
        compiler_params=pltpu.CompilerParams(vmem_limit_bytes=1024 * 1024),
        cost_estimate=pl.CostEstimate(flops=0, bytes_accessed=4 * own_block.shape[0], transcendentals=0),
    )(margin, labels, rows)

    def score(got, senders):
        return pl.pallas_call(
            functools.partial(slot_kernel, senders),
            out_shape=jax.ShapeDtypeStruct((1, own_block.shape[0]), jnp.float32),
            in_specs=[pl.BlockSpec(memory_space=pltpu.VMEM)] * 3,
            out_specs=pl.BlockSpec(memory_space=pltpu.VMEM),
            compiler_params=pltpu.CompilerParams(vmem_limit_bytes=1024 * 1024),
            cost_estimate=pl.CostEstimate(flops=8 * own_block.size, bytes_accessed=4 * own_block.size, transcendentals=0),
        )(*(pltpu.with_memory_space_constraint(x, pltpu.VMEM) for x in (got, *blocks)))

    first, second = score(first, FIRST_FROM), score(second, SECOND_FROM)
    return (to_owner(first, FIRST) + to_owner(second, SECOND)) * factor[None]


def pair_gradients(acts_in, grads_out, proj_in, proj_out, lengths):
    pair_count, side_count, seq_len, layer_count, _ = acts_in.shape
    in_coords = jnp.einsum("pstld,ldr->pstlr", acts_in, proj_in, preferred_element_type=jnp.float32)
    out_coords = jnp.einsum(
        "pstld,ldr->pstlr", grads_out, proj_out, preferred_element_type=jnp.float32
    )
    position = jnp.arange(seq_len, dtype=jnp.int32)
    live = (position[None, None, :] < lengths[:, :, None]).astype(jnp.float32)
    signs = 1.0 - 2.0 * jnp.arange(side_count, dtype=jnp.float32)
    kron_grads = jnp.einsum("pst,pstlr,pstlk->plrk", live * signs[:, None], out_coords, in_coords)
    return kron_grads.reshape(pair_count, -1).astype(jnp.bfloat16)


def local(acts_in, grads_out, proj_in, proj_out, query_grads, margin, labels, lengths):
    pair_count, side_count, _, layer_count, _ = acts_in.shape
    rank = proj_in.shape[2]
    dp_size, layer_size = lax.axis_size("dp"), lax.axis_size("layer")
    block = query_grads.reshape(query_grads.shape[0], -1)
    one_each = pair_count == layer_count == 1 and side_count == 2
    form = pair_gradient if one_each else pair_gradients
    grad_rows = form(acts_in, grads_out, proj_in, proj_out, lengths)
    scale = rank * math.sqrt(layer_count * layer_size) * math.sqrt(acts_in.shape[2])
    if one_each and dp_size == layer_size == len(FIRST):
        return shared_scores(grad_rows, block, margin, labels, scale)
    factor = jax.nn.sigmoid(-margin) * jnp.where(labels == 0, 1.0, -1.0) / scale
    rows = lax.all_gather(grad_rows.astype(jnp.bfloat16), "dp", axis=0, tiled=True)
    scores = jnp.einsum("pk,qk->pq", rows, block, preferred_element_type=jnp.float32)
    scores = lax.all_to_all(scores, "dp", split_axis=0, concat_axis=1, tiled=True)
    summed = lax.psum_scatter(scores, "layer", scatter_dimension=1, tiled=True)
    return summed * factor[:, None]


def solution(mesh):
    placed = (
        P(("groups", "dp"), None, None, "layer", None),
        P(("groups", "dp"), None, None, "layer", None),
        P("layer", None, None),
        P("layer", None, None),
        P("dp", "layer", None),
        P(("groups", "dp")),
        P(("groups", "dp")),
        P(("groups", "dp"), None),
    )
    return jax.shard_map(
        local, mesh=mesh, in_specs=placed, out_specs=P(("groups", "dp"), "layer"), check_vma=False
    )
```

```python
import functools
import math

import jax
import jax.numpy as jnp
from jax import lax
from jax.experimental import pallas as pl
from jax.experimental.pallas import tpu as pltpu
from jax.sharding import PartitionSpec as P

FIRST = ((2, 3, 0, 1), (1, 2, 3, 0), (0, 1, 3, 2), (3, 0, 1, 2))
FIRST_FROM = ((0, 0, 3, 2), (1, 1, 3, 2), (0, 0, 2, 2), (1, 1, 3, 3))
SECOND = ((1, 0, 2, 3), (0, 3, 2, 1), (3, 2, 0, 1), (2, 1, 3, 0))
SECOND_FROM = ((0, 0, 3, 2), (1, 1, 2, 2), (0, 0, 2, 3), (1, 1, 3, 3))


PROJECT_STEP = 1024
SCORE_STEP = 1024


def stepped(left, right, step):
    def add(i, total):
        part = pl.ds(pl.multiple_of(i * step, step), step)
        return total + lax.dot_general(
            left[:, part], right[:, part], (((1,), (1,)), ((), ())), preferred_element_type=jnp.float32
        )

    zero = jnp.zeros((left.shape[0], right.shape[0]), jnp.float32)
    return lax.fori_loop(0, left.shape[1] // step, add, zero)


def pair_kernel(seq_len, acts, grads, proj_in, proj_out, lengths, out, *scratch):
    tokens_v, proj_v, square_v, lengths_s, sems = scratch
    tokens = acts.shape[0]
    rank = proj_in.shape[0]
    limits = pltpu.make_async_copy(lengths, lengths_s, sems.at[4])
    loads = [
        pltpu.make_async_copy(src, dst.at[pl.ds(half * src.shape[0], src.shape[0])], sems.at[2 * i + half])
        for i, (pair, dst) in enumerate((((proj_in, proj_out), proj_v), ((acts, grads), tokens_v)))
        for half, src in enumerate(pair)
    ]
    limits.start()
    for i, copy in enumerate(loads):
        copy.start(priority=i % 2)
    limits.wait()
    token = lax.broadcasted_iota(jnp.int32, (tokens, 1), 0)
    side = token // seq_len
    live = token - side * seq_len < jnp.where(side == 0, lengths_s[0, 0], lengths_s[0, 1])
    weight = jnp.where(live, jnp.where(side == 0, 1.0, -1.0), 0.0)
    for copy in loads:
        copy.wait()
    coords = stepped(tokens_v, proj_v, PROJECT_STEP)
    square_v[...] = lax.dot_general(
        coords[tokens:].astype(jnp.bfloat16),
        (coords[:tokens] * weight).astype(jnp.bfloat16),
        (((0,), (0,)), ((), ())),
        preferred_element_type=jnp.float32,
    )
    rows = [square_v[pl.ds(rank + i, rank // 2, stride=2), :] for i in range(2)]
    out[...] = jnp.concatenate([x[:, :rank] for x in rows], axis=1)


def pair_gradient(acts_in, grads_out, proj_in, proj_out, lengths):
    _, sides, seq_len, _, model_width = acts_in.shape
    rank = proj_in.shape[2]
    tokens = sides * seq_len
    rows = pl.pallas_call(
        functools.partial(pair_kernel, seq_len),
        out_shape=jax.ShapeDtypeStruct((rank // 2, 2 * rank), jnp.float32),
        in_specs=[pl.BlockSpec(memory_space=pl.ANY)] * 5,
        out_specs=pl.BlockSpec(memory_space=pltpu.VMEM),
        scratch_shapes=[
            pltpu.VMEM((2 * tokens, model_width), jnp.bfloat16),
            pltpu.VMEM((2 * rank, model_width), jnp.bfloat16),
            pltpu.VMEM((2 * rank, 2 * rank), jnp.float32),
            pltpu.SMEM((1, 2), jnp.int32),
            pltpu.SemaphoreType.DMA((5,)),
        ],
        compiler_params=pltpu.CompilerParams(vmem_limit_bytes=32 * 1024 * 1024),
        cost_estimate=pl.CostEstimate(
            flops=4 * tokens * model_width * rank,
            bytes_accessed=4 * (tokens + rank) * model_width,
            transcendentals=0,
        ),
    )(
        *(
            pltpu.with_memory_space_constraint(x, pltpu.HBM)
            for x in (
                acts_in.reshape(tokens, model_width),
                grads_out.reshape(tokens, model_width),
                jnp.swapaxes(proj_in, 1, 2).reshape(rank, model_width),
                jnp.swapaxes(proj_out, 1, 2).reshape(rank, model_width),
                lengths,
            )
        )
    )
    return lax.optimization_barrier(rows.reshape(1, rank * rank))


def swap(x):
    return lax.ppermute(x, "layer", [(i, i ^ 1) for i in range(lax.axis_size("layer"))])


def fetch_pair(x, pairs, senders):
    count = len(pairs)
    places = [(d, i) for d in range(count) for i in range(count)]
    moves = [(pairs[d][i] * count + senders[d][i], d * count + i) for d, i in places]
    return lax.ppermute(x, ("dp", "layer"), moves)


def to_owner(x, slot):
    count = len(slot)
    moves = [(d * count + i, slot[d][i] * count + d) for d in range(count) for i in range(count)]
    return lax.ppermute(x, ("dp", "layer"), moves)


def slot_kernel(senders, rows, own_block, other_block, out):
    here = lax.axis_index("dp") * len(senders) + lax.axis_index("layer")
    crossed = [d * len(row) + i for d, row in enumerate(senders) for i, sender in enumerate(row) if sender != i]
    is_crossed = functools.reduce(jnp.logical_or, [here == i for i in crossed])
    one, two = (stepped(rows, block, SCORE_STEP) for block in (own_block, other_block))
    out[...] = jnp.where(is_crossed, one[1:] + two[:1], one[:1] + two[1:])


def factor_kernel(scale, margin, label, rows, factor):
    sign = jnp.where(label[0] == 0, 1.0, -1.0)
    factor[...] = sign / ((1.0 + jnp.exp(jnp.full(factor.shape, margin[0], jnp.float32))) * scale)


def shared_scores(own_row, own_block, margin, labels, scale):
    blocks = own_block, swap(own_block)
    rows = jnp.concatenate([own_row, swap(own_row)], axis=0).astype(jnp.bfloat16)
    first, second = fetch_pair(rows, FIRST, FIRST_FROM), fetch_pair(rows, SECOND, SECOND_FROM)
    factor = pl.pallas_call(
        functools.partial(factor_kernel, scale),
        out_shape=jax.ShapeDtypeStruct(own_block.shape[:1], jnp.float32),
        in_specs=[pl.BlockSpec(memory_space=pltpu.SMEM)] * 2 + [pl.BlockSpec(memory_space=pl.ANY)],
        out_specs=pl.BlockSpec(memory_space=pltpu.VMEM),
        compiler_params=pltpu.CompilerParams(vmem_limit_bytes=1024 * 1024),
        cost_estimate=pl.CostEstimate(flops=0, bytes_accessed=4 * own_block.shape[0], transcendentals=0),
    )(margin, labels, rows)

    def score(got, senders):
        return pl.pallas_call(
            functools.partial(slot_kernel, senders),
            out_shape=jax.ShapeDtypeStruct((1, own_block.shape[0]), jnp.float32),
            in_specs=[pl.BlockSpec(memory_space=pltpu.VMEM)] * 3,
            out_specs=pl.BlockSpec(memory_space=pltpu.VMEM),
            compiler_params=pltpu.CompilerParams(vmem_limit_bytes=1024 * 1024),
            cost_estimate=pl.CostEstimate(flops=8 * own_block.size, bytes_accessed=4 * own_block.size, transcendentals=0),
        )(*(pltpu.with_memory_space_constraint(x, pltpu.VMEM) for x in (got, *blocks)))

    first, second = score(first, FIRST_FROM), score(second, SECOND_FROM)
    return (to_owner(first, FIRST) + to_owner(second, SECOND)) * factor[None]


def pair_gradients(acts_in, grads_out, proj_in, proj_out, lengths):
    pair_count, side_count, seq_len, layer_count, _ = acts_in.shape
    in_coords = jnp.einsum("pstld,ldr->pstlr", acts_in, proj_in, preferred_element_type=jnp.float32)
    out_coords = jnp.einsum(
        "pstld,ldr->pstlr", grads_out, proj_out, preferred_element_type=jnp.float32
    )
    position = jnp.arange(seq_len, dtype=jnp.int32)
    live = (position[None, None, :] < lengths[:, :, None]).astype(jnp.float32)
    signs = 1.0 - 2.0 * jnp.arange(side_count, dtype=jnp.float32)
    kron_grads = jnp.einsum("pst,pstlr,pstlk->plrk", live * signs[:, None], out_coords, in_coords)
    return kron_grads.reshape(pair_count, -1).astype(jnp.bfloat16)


def local(acts_in, grads_out, proj_in, proj_out, query_grads, margin, labels, lengths):
    pair_count, side_count, _, layer_count, _ = acts_in.shape
    rank = proj_in.shape[2]
    dp_size, layer_size = lax.axis_size("dp"), lax.axis_size("layer")
    block = query_grads.reshape(query_grads.shape[0], -1)
    one_each = pair_count == layer_count == 1 and side_count == 2
    form = pair_gradient if one_each else pair_gradients
    grad_rows = form(acts_in, grads_out, proj_in, proj_out, lengths)
    scale = rank * math.sqrt(layer_count * layer_size) * math.sqrt(acts_in.shape[2])
    if one_each and dp_size == layer_size == len(FIRST):
        return shared_scores(grad_rows, block, margin, labels, scale)
    factor = jax.nn.sigmoid(-margin) * jnp.where(labels == 0, 1.0, -1.0) / scale
    rows = lax.all_gather(grad_rows.astype(jnp.bfloat16), "dp", axis=0, tiled=True)
    scores = jnp.einsum("pk,qk->pq", rows, block, preferred_element_type=jnp.float32)
    scores = lax.all_to_all(scores, "dp", split_axis=0, concat_axis=1, tiled=True)
    summed = lax.psum_scatter(scores, "layer", scatter_dimension=1, tiled=True)
    return summed * factor[:, None]


def solution(mesh):
    placed = (
        P(("groups", "dp"), None, None, "layer", None),
        P(("groups", "dp"), None, None, "layer", None),
        P("layer", None, None),
        P("layer", None, None),
        P("dp", "layer", None),
        P(("groups", "dp")),
        P(("groups", "dp")),
        P(("groups", "dp"), None),
    )
    return jax.shard_map(
        local, mesh=mesh, in_specs=placed, out_specs=P(("groups", "dp"), "layer"), check_vma=False
    )
```

```python
import functools
import math

import jax
import jax.numpy as jnp
from jax import lax
from jax.experimental import pallas as pl
from jax.experimental.pallas import tpu as pltpu
from jax.sharding import PartitionSpec as P

FIRST = ((2, 3, 0, 1), (1, 2, 3, 0), (0, 1, 3, 2), (3, 0, 1, 2))
FIRST_FROM = ((0, 0, 3, 2), (1, 1, 3, 2), (0, 0, 2, 2), (1, 1, 3, 3))
SECOND = ((1, 0, 2, 3), (0, 3, 2, 1), (3, 2, 0, 1), (2, 1, 3, 0))
SECOND_FROM = ((0, 0, 3, 2), (1, 1, 2, 2), (0, 0, 2, 3), (1, 1, 3, 3))


PARTS = 4


def pair_kernel(seq_len, acts, grads, proj_in, proj_out, lengths, out, *scratch):
    tokens_v, proj_v, turned_v, square_v, lengths_s, sems = scratch
    tokens = acts.shape[0]
    rank, model_width = proj_in.shape
    limits = pltpu.make_async_copy(lengths, lengths_s, sems.at[4])
    loads = [
        pltpu.make_async_copy(src, dst.at[pl.ds(half * src.shape[0], src.shape[0])], sems.at[2 * i + half])
        for i, (pair, dst) in enumerate((((proj_in, proj_out), proj_v), ((acts, grads), tokens_v)))
        for half, src in enumerate(pair)
    ]
    limits.start()
    for i, copy in enumerate(loads):
        copy.start(priority=i % 2)
    limits.wait()
    token = lax.broadcasted_iota(jnp.int32, (tokens, 1), 0)
    side = token // seq_len
    live = token - side * seq_len < jnp.where(side == 0, lengths_s[0, 0], lengths_s[0, 1])
    weight = jnp.where(live, jnp.where(side == 0, 1.0, -1.0), 0.0)
    for copy in loads[:2]:
        copy.wait()
    width = model_width // PARTS
    for c in range(PARTS):
        turned_v[pl.ds(c * width, width), :] = proj_v[:, pl.ds(c * width, width)].T
    for copy in loads[2:]:
        copy.wait()
    coords = jnp.dot(tokens_v[...], turned_v[...], preferred_element_type=jnp.float32)
    square_v[...] = lax.dot_general(
        coords[tokens:].astype(jnp.bfloat16),
        (coords[:tokens] * weight).astype(jnp.bfloat16),
        (((0,), (0,)), ((), ())),
        preferred_element_type=jnp.float32,
    )
    rows = [square_v[pl.ds(rank + i, rank // 2, stride=2), :] for i in range(2)]
    out[...] = jnp.concatenate([x[:, :rank] for x in rows], axis=1)


def pair_gradient(acts_in, grads_out, proj_in, proj_out, lengths):
    _, sides, seq_len, _, model_width = acts_in.shape
    rank = proj_in.shape[2]
    tokens = sides * seq_len
    rows = pl.pallas_call(
        functools.partial(pair_kernel, seq_len),
        out_shape=jax.ShapeDtypeStruct((rank // 2, 2 * rank), jnp.float32),
        in_specs=[pl.BlockSpec(memory_space=pl.ANY)] * 5,
        out_specs=pl.BlockSpec(memory_space=pltpu.VMEM),
        scratch_shapes=[
            pltpu.VMEM((2 * tokens, model_width), jnp.bfloat16),
            pltpu.VMEM((2 * rank, model_width), jnp.bfloat16),
            pltpu.VMEM((model_width, 2 * rank), jnp.bfloat16),
            pltpu.VMEM((2 * rank, 2 * rank), jnp.float32),
            pltpu.SMEM((1, 2), jnp.int32),
            pltpu.SemaphoreType.DMA((5,)),
        ],
        compiler_params=pltpu.CompilerParams(vmem_limit_bytes=32 * 1024 * 1024),
        cost_estimate=pl.CostEstimate(
            flops=4 * tokens * model_width * rank,
            bytes_accessed=4 * (tokens + rank) * model_width,
            transcendentals=0,
        ),
    )(
        *(
            pltpu.with_memory_space_constraint(x, pltpu.HBM)
            for x in (
                acts_in.reshape(tokens, model_width),
                grads_out.reshape(tokens, model_width),
                jnp.swapaxes(proj_in, 1, 2).reshape(rank, model_width),
                jnp.swapaxes(proj_out, 1, 2).reshape(rank, model_width),
                lengths,
            )
        )
    )
    return lax.optimization_barrier(rows.reshape(1, rank * rank))


def swap(x):
    return lax.ppermute(x, "layer", [(i, i ^ 1) for i in range(lax.axis_size("layer"))])


def fetch_pair(x, pairs, senders):
    count = len(pairs)
    places = [(d, i) for d in range(count) for i in range(count)]
    moves = [(pairs[d][i] * count + senders[d][i], d * count + i) for d, i in places]
    return lax.ppermute(x, ("dp", "layer"), moves)


def to_owner(x, slot):
    count = len(slot)
    moves = [(d * count + i, slot[d][i] * count + d) for d in range(count) for i in range(count)]
    return lax.ppermute(x, ("dp", "layer"), moves)


def slot_kernel(senders, rows, own_block, other_block, out):
    here = lax.axis_index("dp") * len(senders) + lax.axis_index("layer")
    crossed = [d * len(row) + i for d, row in enumerate(senders) for i, sender in enumerate(row) if sender != i]
    is_crossed = functools.reduce(jnp.logical_or, [here == i for i in crossed])
    both = rows[...].astype(jnp.float32)
    lanes = 128
    total = jnp.zeros((own_block.shape[0], lanes), jnp.float32)
    for block, row in ((own_block, jnp.where(is_crossed, both[1:], both[:1])), (other_block, jnp.where(is_crossed, both[:1], both[1:]))):
        for at in range(0, block.shape[1], lanes):
            total += block[:, pl.ds(at, lanes)].astype(jnp.float32) * row[:, at : at + lanes]
    out[...] = jnp.sum(total.T, axis=0, keepdims=True)


def factor_kernel(scale, margin, label, rows, factor):
    sign = jnp.where(label[0] == 0, 1.0, -1.0)
    factor[...] = sign / ((1.0 + jnp.exp(jnp.full(factor.shape, margin[0], jnp.float32))) * scale)


def shared_scores(own_row, own_block, margin, labels, scale):
    blocks = own_block, swap(own_block)
    rows = jnp.concatenate([own_row, swap(own_row)], axis=0).astype(jnp.bfloat16)
    first, second = fetch_pair(rows, FIRST, FIRST_FROM), fetch_pair(rows, SECOND, SECOND_FROM)
    factor = pl.pallas_call(
        functools.partial(factor_kernel, scale),
        out_shape=jax.ShapeDtypeStruct(own_block.shape[:1], jnp.float32),
        in_specs=[pl.BlockSpec(memory_space=pltpu.SMEM)] * 2 + [pl.BlockSpec(memory_space=pl.ANY)],
        out_specs=pl.BlockSpec(memory_space=pltpu.VMEM),
        compiler_params=pltpu.CompilerParams(vmem_limit_bytes=1024 * 1024),
        cost_estimate=pl.CostEstimate(flops=0, bytes_accessed=4 * own_block.shape[0], transcendentals=0),
    )(margin, labels, rows)

    def score(got, senders):
        return pl.pallas_call(
            functools.partial(slot_kernel, senders),
            out_shape=jax.ShapeDtypeStruct((1, own_block.shape[0]), jnp.float32),
            in_specs=[pl.BlockSpec(memory_space=pltpu.VMEM)] * 3,
            out_specs=pl.BlockSpec(memory_space=pltpu.VMEM),
            compiler_params=pltpu.CompilerParams(vmem_limit_bytes=1024 * 1024),
            cost_estimate=pl.CostEstimate(flops=8 * own_block.size, bytes_accessed=4 * own_block.size, transcendentals=0),
        )(*(pltpu.with_memory_space_constraint(x, pltpu.VMEM) for x in (got, *blocks)))

    first, second = score(first, FIRST_FROM), score(second, SECOND_FROM)
    return (to_owner(first, FIRST) + to_owner(second, SECOND)) * factor[None]


def pair_gradients(acts_in, grads_out, proj_in, proj_out, lengths):
    pair_count, side_count, seq_len, layer_count, _ = acts_in.shape
    in_coords = jnp.einsum("pstld,ldr->pstlr", acts_in, proj_in, preferred_element_type=jnp.float32)
    out_coords = jnp.einsum(
        "pstld,ldr->pstlr", grads_out, proj_out, preferred_element_type=jnp.float32
    )
    position = jnp.arange(seq_len, dtype=jnp.int32)
    live = (position[None, None, :] < lengths[:, :, None]).astype(jnp.float32)
    signs = 1.0 - 2.0 * jnp.arange(side_count, dtype=jnp.float32)
    kron_grads = jnp.einsum("pst,pstlr,pstlk->plrk", live * signs[:, None], out_coords, in_coords)
    return kron_grads.reshape(pair_count, -1).astype(jnp.bfloat16)


def local(acts_in, grads_out, proj_in, proj_out, query_grads, margin, labels, lengths):
    pair_count, side_count, _, layer_count, _ = acts_in.shape
    rank = proj_in.shape[2]
    dp_size, layer_size = lax.axis_size("dp"), lax.axis_size("layer")
    block = query_grads.reshape(query_grads.shape[0], -1)
    one_each = pair_count == layer_count == 1 and side_count == 2
    form = pair_gradient if one_each else pair_gradients
    grad_rows = form(acts_in, grads_out, proj_in, proj_out, lengths)
    scale = rank * math.sqrt(layer_count * layer_size) * math.sqrt(acts_in.shape[2])
    if one_each and dp_size == layer_size == len(FIRST):
        return shared_scores(grad_rows, block, margin, labels, scale)
    factor = jax.nn.sigmoid(-margin) * jnp.where(labels == 0, 1.0, -1.0) / scale
    rows = lax.all_gather(grad_rows.astype(jnp.bfloat16), "dp", axis=0, tiled=True)
    scores = jnp.einsum("pk,qk->pq", rows, block, preferred_element_type=jnp.float32)
    scores = lax.all_to_all(scores, "dp", split_axis=0, concat_axis=1, tiled=True)
    summed = lax.psum_scatter(scores, "layer", scatter_dimension=1, tiled=True)
    return summed * factor[:, None]


def solution(mesh):
    placed = (
        P(("groups", "dp"), None, None, "layer", None),
        P(("groups", "dp"), None, None, "layer", None),
        P("layer", None, None),
        P("layer", None, None),
        P("dp", "layer", None),
        P(("groups", "dp")),
        P(("groups", "dp")),
        P(("groups", "dp"), None),
    )
    return jax.shard_map(
        local, mesh=mesh, in_specs=placed, out_specs=P(("groups", "dp"), "layer"), check_vma=False
    )
```

```python
import functools
import math

import jax
import jax.numpy as jnp
from jax import lax
from jax.experimental import pallas as pl
from jax.experimental.pallas import tpu as pltpu
from jax.sharding import PartitionSpec as P

FIRST = ((2, 3, 0, 1), (1, 2, 3, 0), (0, 1, 3, 2), (3, 0, 1, 2))
FIRST_FROM = ((0, 0, 3, 2), (1, 1, 3, 2), (0, 0, 2, 2), (1, 1, 3, 3))
SECOND = ((1, 0, 2, 3), (0, 3, 2, 1), (3, 2, 0, 1), (2, 1, 3, 0))
SECOND_FROM = ((0, 0, 3, 2), (1, 1, 2, 2), (0, 0, 2, 3), (1, 1, 3, 3))


PARTS = 4


def pair_kernel(seq_len, acts, grads, proj_in, proj_out, lengths, out, *scratch):
    tokens_v, proj_v, turned_v, square_v, lengths_s, sems = scratch
    tokens = acts.shape[0]
    rank, model_width = proj_in.shape
    limits = pltpu.make_async_copy(lengths, lengths_s, sems.at[4])
    loads = [
        pltpu.make_async_copy(src, dst.at[pl.ds(half * src.shape[0], src.shape[0])], sems.at[2 * i + half])
        for i, (pair, dst) in enumerate((((proj_in, proj_out), proj_v), ((acts, grads), tokens_v)))
        for half, src in enumerate(pair)
    ]
    limits.start()
    for i, copy in enumerate(loads):
        copy.start(priority=i % 2)
    limits.wait()
    token = lax.broadcasted_iota(jnp.int32, (tokens, 1), 0)
    side = token // seq_len
    live = token - side * seq_len < jnp.where(side == 0, lengths_s[0, 0], lengths_s[0, 1])
    weight = jnp.where(live, jnp.where(side == 0, 1.0, -1.0), 0.0)
    for copy in loads[:2]:
        copy.wait()
    width = model_width // PARTS
    for c in range(PARTS):
        turned_v[pl.ds(c * width, width), :] = proj_v[:, pl.ds(c * width, width)].T
    for copy in loads[2:]:
        copy.wait()
    coords = jnp.dot(tokens_v[...], turned_v[...], preferred_element_type=jnp.float32)
    square_v[...] = lax.dot_general(
        coords[tokens:].astype(jnp.bfloat16),
        (coords[:tokens] * weight).astype(jnp.bfloat16),
        (((0,), (0,)), ((), ())),
        preferred_element_type=jnp.float32,
    )
    rows = [square_v[pl.ds(rank + i, rank // 2, stride=2), :] for i in range(2)]
    out[...] = jnp.concatenate([x[:, :rank] for x in rows], axis=1)


def pair_gradient(acts_in, grads_out, proj_in, proj_out, lengths):
    _, sides, seq_len, _, model_width = acts_in.shape
    rank = proj_in.shape[2]
    tokens = sides * seq_len
    rows = pl.pallas_call(
        functools.partial(pair_kernel, seq_len),
        out_shape=jax.ShapeDtypeStruct((rank // 2, 2 * rank), jnp.float32),
        in_specs=[pl.BlockSpec(memory_space=pl.ANY)] * 5,
        out_specs=pl.BlockSpec(memory_space=pltpu.VMEM),
        scratch_shapes=[
            pltpu.VMEM((2 * tokens, model_width), jnp.bfloat16),
            pltpu.VMEM((2 * rank, model_width), jnp.bfloat16),
            pltpu.VMEM((model_width, 2 * rank), jnp.bfloat16),
            pltpu.VMEM((2 * rank, 2 * rank), jnp.float32),
            pltpu.SMEM((1, 2), jnp.int32),
            pltpu.SemaphoreType.DMA((5,)),
        ],
        compiler_params=pltpu.CompilerParams(vmem_limit_bytes=32 * 1024 * 1024),
        cost_estimate=pl.CostEstimate(
            flops=4 * tokens * model_width * rank,
            bytes_accessed=4 * (tokens + rank) * model_width,
            transcendentals=0,
        ),
    )(
        *(
            pltpu.with_memory_space_constraint(x, pltpu.HBM)
            for x in (
                acts_in.reshape(tokens, model_width),
                grads_out.reshape(tokens, model_width),
                jnp.swapaxes(proj_in, 1, 2).reshape(rank, model_width),
                jnp.swapaxes(proj_out, 1, 2).reshape(rank, model_width),
                lengths,
            )
        )
    )
    return lax.optimization_barrier(rows.reshape(1, rank * rank))


def swap(x):
    return lax.ppermute(x, "layer", [(i, i ^ 1) for i in range(lax.axis_size("layer"))])


def fetch_pair(x, pairs, senders):
    count = len(pairs)
    places = [(d, i) for d in range(count) for i in range(count)]
    moves = [(pairs[d][i] * count + senders[d][i], d * count + i) for d, i in places]
    return lax.ppermute(x, ("dp", "layer"), moves)


def to_owner(x, slot):
    count = len(slot)
    moves = [(d * count + i, slot[d][i] * count + d) for d in range(count) for i in range(count)]
    return lax.ppermute(x, ("dp", "layer"), moves)


def slot_kernel(senders, rows, own_block, other_block, out):
    here = lax.axis_index("dp") * len(senders) + lax.axis_index("layer")
    crossed = [d * len(row) + i for d, row in enumerate(senders) for i, sender in enumerate(row) if sender != i]
    is_crossed = functools.reduce(jnp.logical_or, [here == i for i in crossed])
    two = lax.dot_general(
        rows[...], other_block[...], (((1,), (1,)), ((), ())), preferred_element_type=jnp.float32
    )
    both = rows[...].astype(jnp.float32)
    row = jnp.where(is_crossed, both[1:], both[:1])
    lanes = 128
    one = jnp.zeros((own_block.shape[0], lanes), jnp.float32)
    for at in range(0, own_block.shape[1], lanes):
        one += own_block[:, pl.ds(at, lanes)].astype(jnp.float32) * row[:, at : at + lanes]
    out[...] = jnp.sum(one.T, axis=0, keepdims=True) + jnp.where(is_crossed, two[:1], two[1:])


def factor_kernel(scale, margin, label, rows, factor):
    sign = jnp.where(label[0] == 0, 1.0, -1.0)
    factor[...] = sign / ((1.0 + jnp.exp(jnp.full(factor.shape, margin[0], jnp.float32))) * scale)


def shared_scores(own_row, own_block, margin, labels, scale):
    blocks = own_block, swap(own_block)
    rows = jnp.concatenate([own_row, swap(own_row)], axis=0).astype(jnp.bfloat16)
    first, second = fetch_pair(rows, FIRST, FIRST_FROM), fetch_pair(rows, SECOND, SECOND_FROM)
    factor = pl.pallas_call(
        functools.partial(factor_kernel, scale),
        out_shape=jax.ShapeDtypeStruct(own_block.shape[:1], jnp.float32),
        in_specs=[pl.BlockSpec(memory_space=pltpu.SMEM)] * 2 + [pl.BlockSpec(memory_space=pl.ANY)],
        out_specs=pl.BlockSpec(memory_space=pltpu.VMEM),
        compiler_params=pltpu.CompilerParams(vmem_limit_bytes=1024 * 1024),
        cost_estimate=pl.CostEstimate(flops=0, bytes_accessed=4 * own_block.shape[0], transcendentals=0),
    )(margin, labels, rows)

    def score(got, senders):
        return pl.pallas_call(
            functools.partial(slot_kernel, senders),
            out_shape=jax.ShapeDtypeStruct((1, own_block.shape[0]), jnp.float32),
            in_specs=[pl.BlockSpec(memory_space=pltpu.VMEM)] * 3,
            out_specs=pl.BlockSpec(memory_space=pltpu.VMEM),
            compiler_params=pltpu.CompilerParams(vmem_limit_bytes=1024 * 1024),
            cost_estimate=pl.CostEstimate(flops=8 * own_block.size, bytes_accessed=4 * own_block.size, transcendentals=0),
        )(*(pltpu.with_memory_space_constraint(x, pltpu.VMEM) for x in (got, *blocks)))

    first, second = score(first, FIRST_FROM), score(second, SECOND_FROM)
    return (to_owner(first, FIRST) + to_owner(second, SECOND)) * factor[None]


def pair_gradients(acts_in, grads_out, proj_in, proj_out, lengths):
    pair_count, side_count, seq_len, layer_count, _ = acts_in.shape
    in_coords = jnp.einsum("pstld,ldr->pstlr", acts_in, proj_in, preferred_element_type=jnp.float32)
    out_coords = jnp.einsum(
        "pstld,ldr->pstlr", grads_out, proj_out, preferred_element_type=jnp.float32
    )
    position = jnp.arange(seq_len, dtype=jnp.int32)
    live = (position[None, None, :] < lengths[:, :, None]).astype(jnp.float32)
    signs = 1.0 - 2.0 * jnp.arange(side_count, dtype=jnp.float32)
    kron_grads = jnp.einsum("pst,pstlr,pstlk->plrk", live * signs[:, None], out_coords, in_coords)
    return kron_grads.reshape(pair_count, -1).astype(jnp.bfloat16)


def local(acts_in, grads_out, proj_in, proj_out, query_grads, margin, labels, lengths):
    pair_count, side_count, _, layer_count, _ = acts_in.shape
    rank = proj_in.shape[2]
    dp_size, layer_size = lax.axis_size("dp"), lax.axis_size("layer")
    block = query_grads.reshape(query_grads.shape[0], -1)
    one_each = pair_count == layer_count == 1 and side_count == 2
    form = pair_gradient if one_each else pair_gradients
    grad_rows = form(acts_in, grads_out, proj_in, proj_out, lengths)
    scale = rank * math.sqrt(layer_count * layer_size) * math.sqrt(acts_in.shape[2])
    if one_each and dp_size == layer_size == len(FIRST):
        return shared_scores(grad_rows, block, margin, labels, scale)
    factor = jax.nn.sigmoid(-margin) * jnp.where(labels == 0, 1.0, -1.0) / scale
    rows = lax.all_gather(grad_rows.astype(jnp.bfloat16), "dp", axis=0, tiled=True)
    scores = jnp.einsum("pk,qk->pq", rows, block, preferred_element_type=jnp.float32)
    scores = lax.all_to_all(scores, "dp", split_axis=0, concat_axis=1, tiled=True)
    summed = lax.psum_scatter(scores, "layer", scatter_dimension=1, tiled=True)
    return summed * factor[:, None]


def solution(mesh):
    placed = (
        P(("groups", "dp"), None, None, "layer", None),
        P(("groups", "dp"), None, None, "layer", None),
        P("layer", None, None),
        P("layer", None, None),
        P("dp", "layer", None),
        P(("groups", "dp")),
        P(("groups", "dp")),
        P(("groups", "dp"), None),
    )
    return jax.shard_map(
        local, mesh=mesh, in_specs=placed, out_specs=P(("groups", "dp"), "layer"), check_vma=False
    )
```

```python
import functools
import math

import jax
import jax.numpy as jnp
from jax import lax
from jax.experimental import pallas as pl
from jax.experimental.pallas import tpu as pltpu
from jax.sharding import PartitionSpec as P

FIRST = ((2, 3, 0, 1), (1, 2, 3, 0), (0, 1, 3, 2), (3, 0, 1, 2))
FIRST_FROM = ((0, 0, 3, 2), (1, 1, 3, 2), (0, 0, 2, 2), (1, 1, 3, 3))
SECOND = ((1, 0, 2, 3), (0, 3, 2, 1), (3, 2, 0, 1), (2, 1, 3, 0))
SECOND_FROM = ((0, 0, 3, 2), (1, 1, 2, 2), (0, 0, 2, 3), (1, 1, 3, 3))


PARTS = 4


def pair_kernel(seq_len, acts, grads, proj_in, proj_out, lengths, out, *scratch):
    tokens_v, proj_v, turned_v, square_v, lengths_s, sems = scratch
    tokens = acts.shape[0]
    rank, model_width = proj_in.shape
    limits = pltpu.make_async_copy(lengths, lengths_s, sems.at[4])
    loads = [
        pltpu.make_async_copy(src, dst.at[pl.ds(half * src.shape[0], src.shape[0])], sems.at[2 * i + half])
        for i, (pair, dst) in enumerate((((proj_in, proj_out), proj_v), ((acts, grads), tokens_v)))
        for half, src in enumerate(pair)
    ]
    limits.start()
    for i, copy in enumerate(loads):
        copy.start(priority=i % 2)
    limits.wait()
    token = lax.broadcasted_iota(jnp.int32, (tokens, 1), 0)
    side = token // seq_len
    live = token - side * seq_len < jnp.where(side == 0, lengths_s[0, 0], lengths_s[0, 1])
    weight = jnp.where(live, jnp.where(side == 0, 1.0, -1.0), 0.0)
    for copy in loads[:2]:
        copy.wait()
    width = model_width // PARTS
    for c in range(PARTS):
        turned_v[pl.ds(c * width, width), :] = proj_v[:, pl.ds(c * width, width)].T
    for copy in loads[2:]:
        copy.wait()
    halves = [pl.ds(at, model_width // 2) for at in (0, model_width // 2)]
    low, high = (jnp.dot(tokens_v[:, part], turned_v[part, :], preferred_element_type=jnp.float32) for part in halves)
    coords = low + high
    square_v[...] = lax.dot_general(
        coords[tokens:].astype(jnp.bfloat16),
        (coords[:tokens] * weight).astype(jnp.bfloat16),
        (((0,), (0,)), ((), ())),
        preferred_element_type=jnp.float32,
    )
    rows = [square_v[pl.ds(rank + i, rank // 2, stride=2), :] for i in range(2)]
    out[...] = jnp.concatenate([x[:, :rank] for x in rows], axis=1)


def pair_gradient(acts_in, grads_out, proj_in, proj_out, lengths):
    _, sides, seq_len, _, model_width = acts_in.shape
    rank = proj_in.shape[2]
    tokens = sides * seq_len
    rows = pl.pallas_call(
        functools.partial(pair_kernel, seq_len),
        out_shape=jax.ShapeDtypeStruct((rank // 2, 2 * rank), jnp.float32),
        in_specs=[pl.BlockSpec(memory_space=pl.ANY)] * 5,
        out_specs=pl.BlockSpec(memory_space=pltpu.VMEM),
        scratch_shapes=[
            pltpu.VMEM((2 * tokens, model_width), jnp.bfloat16),
            pltpu.VMEM((2 * rank, model_width), jnp.bfloat16),
            pltpu.VMEM((model_width, 2 * rank), jnp.bfloat16),
            pltpu.VMEM((2 * rank, 2 * rank), jnp.float32),
            pltpu.SMEM((1, 2), jnp.int32),
            pltpu.SemaphoreType.DMA((5,)),
        ],
        compiler_params=pltpu.CompilerParams(vmem_limit_bytes=32 * 1024 * 1024),
        cost_estimate=pl.CostEstimate(
            flops=4 * tokens * model_width * rank,
            bytes_accessed=4 * (tokens + rank) * model_width,
            transcendentals=0,
        ),
    )(
        *(
            pltpu.with_memory_space_constraint(x, pltpu.HBM)
            for x in (
                acts_in.reshape(tokens, model_width),
                grads_out.reshape(tokens, model_width),
                jnp.swapaxes(proj_in, 1, 2).reshape(rank, model_width),
                jnp.swapaxes(proj_out, 1, 2).reshape(rank, model_width),
                lengths,
            )
        )
    )
    return lax.optimization_barrier(rows.reshape(1, rank * rank))


def swap(x):
    return lax.ppermute(x, "layer", [(i, i ^ 1) for i in range(lax.axis_size("layer"))])


def fetch_pair(x, pairs, senders):
    count = len(pairs)
    places = [(d, i) for d in range(count) for i in range(count)]
    moves = [(pairs[d][i] * count + senders[d][i], d * count + i) for d, i in places]
    return lax.ppermute(x, ("dp", "layer"), moves)


def to_owner(x, slot):
    count = len(slot)
    moves = [(d * count + i, slot[d][i] * count + d) for d in range(count) for i in range(count)]
    return lax.ppermute(x, ("dp", "layer"), moves)


def slot_kernel(senders, rows, own_block, other_block, out):
    here = lax.axis_index("dp") * len(senders) + lax.axis_index("layer")
    crossed = [d * len(row) + i for d, row in enumerate(senders) for i, sender in enumerate(row) if sender != i]
    is_crossed = functools.reduce(jnp.logical_or, [here == i for i in crossed])
    two = lax.dot_general(
        rows[...], other_block[...], (((1,), (1,)), ((), ())), preferred_element_type=jnp.float32
    )
    both = rows[...].astype(jnp.float32)
    row = jnp.where(is_crossed, both[1:], both[:1])
    lanes = 128
    one = jnp.zeros((own_block.shape[0], lanes), jnp.float32)
    for at in range(0, own_block.shape[1], lanes):
        one += own_block[:, pl.ds(at, lanes)].astype(jnp.float32) * row[:, at : at + lanes]
    out[...] = jnp.sum(one.T, axis=0, keepdims=True) + jnp.where(is_crossed, two[:1], two[1:])


def factor_kernel(scale, margin, label, rows, factor):
    sign = jnp.where(label[0] == 0, 1.0, -1.0)
    factor[...] = sign / ((1.0 + jnp.exp(jnp.full(factor.shape, margin[0], jnp.float32))) * scale)


def shared_scores(own_row, own_block, margin, labels, scale):
    blocks = own_block, swap(own_block)
    rows = jnp.concatenate([own_row, swap(own_row)], axis=0).astype(jnp.bfloat16)
    first, second = fetch_pair(rows, FIRST, FIRST_FROM), fetch_pair(rows, SECOND, SECOND_FROM)
    factor = pl.pallas_call(
        functools.partial(factor_kernel, scale),
        out_shape=jax.ShapeDtypeStruct(own_block.shape[:1], jnp.float32),
        in_specs=[pl.BlockSpec(memory_space=pltpu.SMEM)] * 2 + [pl.BlockSpec(memory_space=pl.ANY)],
        out_specs=pl.BlockSpec(memory_space=pltpu.VMEM),
        compiler_params=pltpu.CompilerParams(vmem_limit_bytes=1024 * 1024),
        cost_estimate=pl.CostEstimate(flops=0, bytes_accessed=4 * own_block.shape[0], transcendentals=0),
    )(margin, labels, rows)

    def score(got, senders):
        return pl.pallas_call(
            functools.partial(slot_kernel, senders),
            out_shape=jax.ShapeDtypeStruct((1, own_block.shape[0]), jnp.float32),
            in_specs=[pl.BlockSpec(memory_space=pltpu.VMEM)] * 3,
            out_specs=pl.BlockSpec(memory_space=pltpu.VMEM),
            compiler_params=pltpu.CompilerParams(vmem_limit_bytes=1024 * 1024),
            cost_estimate=pl.CostEstimate(flops=8 * own_block.size, bytes_accessed=4 * own_block.size, transcendentals=0),
        )(*(pltpu.with_memory_space_constraint(x, pltpu.VMEM) for x in (got, *blocks)))

    first, second = score(first, FIRST_FROM), score(second, SECOND_FROM)
    return (to_owner(first, FIRST) + to_owner(second, SECOND)) * factor[None]


def pair_gradients(acts_in, grads_out, proj_in, proj_out, lengths):
    pair_count, side_count, seq_len, layer_count, _ = acts_in.shape
    in_coords = jnp.einsum("pstld,ldr->pstlr", acts_in, proj_in, preferred_element_type=jnp.float32)
    out_coords = jnp.einsum(
        "pstld,ldr->pstlr", grads_out, proj_out, preferred_element_type=jnp.float32
    )
    position = jnp.arange(seq_len, dtype=jnp.int32)
    live = (position[None, None, :] < lengths[:, :, None]).astype(jnp.float32)
    signs = 1.0 - 2.0 * jnp.arange(side_count, dtype=jnp.float32)
    kron_grads = jnp.einsum("pst,pstlr,pstlk->plrk", live * signs[:, None], out_coords, in_coords)
    return kron_grads.reshape(pair_count, -1).astype(jnp.bfloat16)


def local(acts_in, grads_out, proj_in, proj_out, query_grads, margin, labels, lengths):
    pair_count, side_count, _, layer_count, _ = acts_in.shape
    rank = proj_in.shape[2]
    dp_size, layer_size = lax.axis_size("dp"), lax.axis_size("layer")
    block = query_grads.reshape(query_grads.shape[0], -1)
    one_each = pair_count == layer_count == 1 and side_count == 2
    form = pair_gradient if one_each else pair_gradients
    grad_rows = form(acts_in, grads_out, proj_in, proj_out, lengths)
    scale = rank * math.sqrt(layer_count * layer_size) * math.sqrt(acts_in.shape[2])
    if one_each and dp_size == layer_size == len(FIRST):
        return shared_scores(grad_rows, block, margin, labels, scale)
    factor = jax.nn.sigmoid(-margin) * jnp.where(labels == 0, 1.0, -1.0) / scale
    rows = lax.all_gather(grad_rows.astype(jnp.bfloat16), "dp", axis=0, tiled=True)
    scores = jnp.einsum("pk,qk->pq", rows, block, preferred_element_type=jnp.float32)
    scores = lax.all_to_all(scores, "dp", split_axis=0, concat_axis=1, tiled=True)
    summed = lax.psum_scatter(scores, "layer", scatter_dimension=1, tiled=True)
    return summed * factor[:, None]


def solution(mesh):
    placed = (
        P(("groups", "dp"), None, None, "layer", None),
        P(("groups", "dp"), None, None, "layer", None),
        P("layer", None, None),
        P("layer", None, None),
        P("dp", "layer", None),
        P(("groups", "dp")),
        P(("groups", "dp")),
        P(("groups", "dp"), None),
    )
    return jax.shard_map(
        local, mesh=mesh, in_specs=placed, out_specs=P(("groups", "dp"), "layer"), check_vma=False
    )
```

```python
import functools
import math

import jax
import jax.numpy as jnp
from jax import lax
from jax.experimental import pallas as pl
from jax.experimental.pallas import tpu as pltpu
from jax.sharding import PartitionSpec as P

FIRST = ((2, 3, 0, 1), (1, 2, 3, 0), (0, 1, 3, 2), (3, 0, 1, 2))
FIRST_FROM = ((0, 0, 3, 2), (1, 1, 3, 2), (0, 0, 2, 2), (1, 1, 3, 3))
SECOND = ((1, 0, 2, 3), (0, 3, 2, 1), (3, 2, 0, 1), (2, 1, 3, 0))
SECOND_FROM = ((0, 0, 3, 2), (1, 1, 2, 2), (0, 0, 2, 3), (1, 1, 3, 3))


PARTS = 4


def pair_kernel(seq_len, acts, grads, proj_in, proj_out, lengths, out, *scratch):
    tokens_v, proj_v, turned_v, square_v, lengths_s, sems = scratch
    tokens = acts.shape[0]
    rank, model_width = proj_in.shape
    limits = pltpu.make_async_copy(lengths, lengths_s, sems.at[4])
    loads = [
        pltpu.make_async_copy(src, dst.at[pl.ds(half * src.shape[0], src.shape[0])], sems.at[2 * i + half])
        for i, (pair, dst) in enumerate((((proj_in, proj_out), proj_v), ((acts, grads), tokens_v)))
        for half, src in enumerate(pair)
    ]
    limits.start()
    for i, copy in enumerate(loads):
        copy.start(priority=i % 2)
    limits.wait()
    token = lax.broadcasted_iota(jnp.int32, (tokens, 1), 0)
    side = token // seq_len
    live = token - side * seq_len < jnp.where(side == 0, lengths_s[0, 0], lengths_s[0, 1])
    weight = jnp.where(live, jnp.where(side == 0, 1.0, -1.0), 0.0)
    for copy in loads[:2]:
        copy.wait()
    width = model_width // PARTS
    for c in range(PARTS):
        turned_v[pl.ds(c * width, width), :] = proj_v[:, pl.ds(c * width, width)].T
    for copy in loads[2:]:
        copy.wait()
    coords = jnp.dot(tokens_v[...], turned_v[...], preferred_element_type=jnp.float32)
    square_v[...] = lax.dot_general(
        coords[tokens:].astype(jnp.bfloat16),
        (coords[:tokens] * weight).astype(jnp.bfloat16),
        (((0,), (0,)), ((), ())),
        preferred_element_type=jnp.float32,
    )
    rows = [square_v[pl.ds(rank + i, rank // 2, stride=2), :] for i in range(2)]
    out[...] = jnp.concatenate([x[:, :rank] for x in rows], axis=1)


def pair_gradient(acts_in, grads_out, proj_in, proj_out, lengths):
    _, sides, seq_len, _, model_width = acts_in.shape
    rank = proj_in.shape[2]
    tokens = sides * seq_len
    rows = pl.pallas_call(
        functools.partial(pair_kernel, seq_len),
        out_shape=jax.ShapeDtypeStruct((rank // 2, 2 * rank), jnp.float32),
        in_specs=[pl.BlockSpec(memory_space=pl.ANY)] * 5,
        out_specs=pl.BlockSpec(memory_space=pltpu.VMEM),
        scratch_shapes=[
            pltpu.VMEM((2 * tokens, model_width), jnp.bfloat16),
            pltpu.VMEM((2 * rank, model_width), jnp.bfloat16),
            pltpu.VMEM((model_width, 2 * rank), jnp.bfloat16),
            pltpu.VMEM((2 * rank, 2 * rank), jnp.float32),
            pltpu.SMEM((1, 2), jnp.int32),
            pltpu.SemaphoreType.DMA((5,)),
        ],
        compiler_params=pltpu.CompilerParams(vmem_limit_bytes=32 * 1024 * 1024),
        cost_estimate=pl.CostEstimate(
            flops=4 * tokens * model_width * rank,
            bytes_accessed=4 * (tokens + rank) * model_width,
            transcendentals=0,
        ),
    )(
        *(
            pltpu.with_memory_space_constraint(x, pltpu.HBM)
            for x in (
                acts_in.reshape(tokens, model_width),
                grads_out.reshape(tokens, model_width),
                jnp.swapaxes(proj_in, 1, 2).reshape(rank, model_width),
                jnp.swapaxes(proj_out, 1, 2).reshape(rank, model_width),
                lengths,
            )
        )
    )
    return lax.optimization_barrier(rows.reshape(1, rank * rank))


def swap(x):
    return lax.ppermute(x, "layer", [(i, i ^ 1) for i in range(lax.axis_size("layer"))])


def fetch_pair(x, pairs, senders):
    count = len(pairs)
    places = [(d, i) for d in range(count) for i in range(count)]
    moves = [(pairs[d][i] * count + senders[d][i], d * count + i) for d, i in places]
    return lax.ppermute(x, ("dp", "layer"), moves)


def to_owner(x, slot):
    count = len(slot)
    moves = [(d * count + i, slot[d][i] * count + d) for d in range(count) for i in range(count)]
    return lax.ppermute(x, ("dp", "layer"), moves)


def slot_kernel(senders, rows, own_block, other_block, out):
    here = lax.axis_index("dp") * len(senders) + lax.axis_index("layer")
    crossed = [d * len(row) + i for d, row in enumerate(senders) for i, sender in enumerate(row) if sender != i]
    is_crossed = functools.reduce(jnp.logical_or, [here == i for i in crossed])
    width = own_block.shape[1]
    quarter = width // 4
    rest = pl.ds(quarter, width - quarter)
    two = lax.dot_general(
        rows[:, rest], other_block[:, rest], (((1,), (1,)), ((), ())), preferred_element_type=jnp.float32
    )
    both = rows[...].astype(jnp.float32)
    own_row, other_row = jnp.where(is_crossed, both[1:], both[:1]), jnp.where(is_crossed, both[:1], both[1:])
    lanes = 128
    one = jnp.zeros((own_block.shape[0], lanes), jnp.float32)
    for block, row, end in ((own_block, own_row, width), (other_block, other_row, quarter)):
        for at in range(0, end, lanes):
            one += block[:, pl.ds(at, lanes)].astype(jnp.float32) * row[:, at : at + lanes]
    out[...] = jnp.sum(one.T, axis=0, keepdims=True) + jnp.where(is_crossed, two[:1], two[1:])


def factor_kernel(scale, margin, label, rows, factor):
    sign = jnp.where(label[0] == 0, 1.0, -1.0)
    factor[...] = sign / ((1.0 + jnp.exp(jnp.full(factor.shape, margin[0], jnp.float32))) * scale)


def shared_scores(own_row, own_block, margin, labels, scale):
    blocks = own_block, swap(own_block)
    rows = jnp.concatenate([own_row, swap(own_row)], axis=0).astype(jnp.bfloat16)
    first, second = fetch_pair(rows, FIRST, FIRST_FROM), fetch_pair(rows, SECOND, SECOND_FROM)
    factor = pl.pallas_call(
        functools.partial(factor_kernel, scale),
        out_shape=jax.ShapeDtypeStruct(own_block.shape[:1], jnp.float32),
        in_specs=[pl.BlockSpec(memory_space=pltpu.SMEM)] * 2 + [pl.BlockSpec(memory_space=pl.ANY)],
        out_specs=pl.BlockSpec(memory_space=pltpu.VMEM),
        compiler_params=pltpu.CompilerParams(vmem_limit_bytes=1024 * 1024),
        cost_estimate=pl.CostEstimate(flops=0, bytes_accessed=4 * own_block.shape[0], transcendentals=0),
    )(margin, labels, rows)

    def score(got, senders):
        return pl.pallas_call(
            functools.partial(slot_kernel, senders),
            out_shape=jax.ShapeDtypeStruct((1, own_block.shape[0]), jnp.float32),
            in_specs=[pl.BlockSpec(memory_space=pltpu.VMEM)] * 3,
            out_specs=pl.BlockSpec(memory_space=pltpu.VMEM),
            compiler_params=pltpu.CompilerParams(vmem_limit_bytes=1024 * 1024),
            cost_estimate=pl.CostEstimate(flops=8 * own_block.size, bytes_accessed=4 * own_block.size, transcendentals=0),
        )(*(pltpu.with_memory_space_constraint(x, pltpu.VMEM) for x in (got, *blocks)))

    first, second = score(first, FIRST_FROM), score(second, SECOND_FROM)
    return (to_owner(first, FIRST) + to_owner(second, SECOND)) * factor[None]


def pair_gradients(acts_in, grads_out, proj_in, proj_out, lengths):
    pair_count, side_count, seq_len, layer_count, _ = acts_in.shape
    in_coords = jnp.einsum("pstld,ldr->pstlr", acts_in, proj_in, preferred_element_type=jnp.float32)
    out_coords = jnp.einsum(
        "pstld,ldr->pstlr", grads_out, proj_out, preferred_element_type=jnp.float32
    )
    position = jnp.arange(seq_len, dtype=jnp.int32)
    live = (position[None, None, :] < lengths[:, :, None]).astype(jnp.float32)
    signs = 1.0 - 2.0 * jnp.arange(side_count, dtype=jnp.float32)
    kron_grads = jnp.einsum("pst,pstlr,pstlk->plrk", live * signs[:, None], out_coords, in_coords)
    return kron_grads.reshape(pair_count, -1).astype(jnp.bfloat16)


def local(acts_in, grads_out, proj_in, proj_out, query_grads, margin, labels, lengths):
    pair_count, side_count, _, layer_count, _ = acts_in.shape
    rank = proj_in.shape[2]
    dp_size, layer_size = lax.axis_size("dp"), lax.axis_size("layer")
    block = query_grads.reshape(query_grads.shape[0], -1)
    one_each = pair_count == layer_count == 1 and side_count == 2
    form = pair_gradient if one_each else pair_gradients
    grad_rows = form(acts_in, grads_out, proj_in, proj_out, lengths)
    scale = rank * math.sqrt(layer_count * layer_size) * math.sqrt(acts_in.shape[2])
    if one_each and dp_size == layer_size == len(FIRST):
        return shared_scores(grad_rows, block, margin, labels, scale)
    factor = jax.nn.sigmoid(-margin) * jnp.where(labels == 0, 1.0, -1.0) / scale
    rows = lax.all_gather(grad_rows.astype(jnp.bfloat16), "dp", axis=0, tiled=True)
    scores = jnp.einsum("pk,qk->pq", rows, block, preferred_element_type=jnp.float32)
    scores = lax.all_to_all(scores, "dp", split_axis=0, concat_axis=1, tiled=True)
    summed = lax.psum_scatter(scores, "layer", scatter_dimension=1, tiled=True)
    return summed * factor[:, None]


def solution(mesh):
    placed = (
        P(("groups", "dp"), None, None, "layer", None),
        P(("groups", "dp"), None, None, "layer", None),
        P("layer", None, None),
        P("layer", None, None),
        P("dp", "layer", None),
        P(("groups", "dp")),
        P(("groups", "dp")),
        P(("groups", "dp"), None),
    )
    return jax.shard_map(
        local, mesh=mesh, in_specs=placed, out_specs=P(("groups", "dp"), "layer"), check_vma=False
    )
```

```python
import functools
import math

import jax
import jax.numpy as jnp
from jax import lax
from jax.experimental import pallas as pl
from jax.experimental.pallas import tpu as pltpu
from jax.sharding import PartitionSpec as P

FIRST = ((2, 3, 0, 1), (1, 2, 3, 0), (0, 1, 3, 2), (3, 0, 1, 2))
FIRST_FROM = ((0, 0, 3, 2), (1, 1, 3, 2), (0, 0, 2, 2), (1, 1, 3, 3))
SECOND = ((1, 0, 2, 3), (0, 3, 2, 1), (3, 2, 0, 1), (2, 1, 3, 0))
SECOND_FROM = ((0, 0, 3, 2), (1, 1, 2, 2), (0, 0, 2, 3), (1, 1, 3, 3))


PARTS = 4


def pair_kernel(seq_len, acts, grads, proj_in, proj_out, lengths, out, *scratch):
    tokens_v, proj_v, turned_v, square_v, lengths_s, sems = scratch
    tokens = acts.shape[0]
    rank, model_width = proj_in.shape
    limits = pltpu.make_async_copy(lengths, lengths_s, sems.at[4])
    loads = [
        pltpu.make_async_copy(src, dst.at[pl.ds(half * src.shape[0], src.shape[0])], sems.at[2 * i + half])
        for i, (pair, dst) in enumerate((((proj_in, proj_out), proj_v), ((acts, grads), tokens_v)))
        for half, src in enumerate(pair)
    ]
    limits.start()
    for i, copy in enumerate(loads):
        copy.start(priority=i % 2)
    limits.wait()
    token = lax.broadcasted_iota(jnp.int32, (tokens, 1), 0)
    side = token // seq_len
    live = token - side * seq_len < jnp.where(side == 0, lengths_s[0, 0], lengths_s[0, 1])
    weight = jnp.where(live, jnp.where(side == 0, 1.0, -1.0), 0.0)
    for copy in loads[:2]:
        copy.wait()
    width = model_width // PARTS
    for c in range(PARTS):
        turned_v[pl.ds(c * width, width), :] = proj_v[:, pl.ds(c * width, width)].T
    for copy in loads[2:]:
        copy.wait()
    coords = jnp.dot(tokens_v[...], turned_v[...], preferred_element_type=jnp.float32)
    square_v[...] = lax.dot_general(
        coords[tokens:].astype(jnp.bfloat16),
        (coords[:tokens] * weight).astype(jnp.bfloat16),
        (((0,), (0,)), ((), ())),
        preferred_element_type=jnp.float32,
    )
    rows = [square_v[pl.ds(rank + i, rank // 2, stride=2), :] for i in range(2)]
    out[...] = jnp.concatenate([x[:, :rank] for x in rows], axis=1)


def pair_gradient(acts_in, grads_out, proj_in, proj_out, lengths):
    _, sides, seq_len, _, model_width = acts_in.shape
    rank = proj_in.shape[2]
    tokens = sides * seq_len
    rows = pl.pallas_call(
        functools.partial(pair_kernel, seq_len),
        out_shape=jax.ShapeDtypeStruct((rank // 2, 2 * rank), jnp.float32),
        in_specs=[pl.BlockSpec(memory_space=pl.ANY)] * 5,
        out_specs=pl.BlockSpec(memory_space=pltpu.VMEM),
        scratch_shapes=[
            pltpu.VMEM((2 * tokens, model_width), jnp.bfloat16),
            pltpu.VMEM((2 * rank, model_width), jnp.bfloat16),
            pltpu.VMEM((model_width, 2 * rank), jnp.bfloat16),
            pltpu.VMEM((2 * rank, 2 * rank), jnp.float32),
            pltpu.SMEM((1, 2), jnp.int32),
            pltpu.SemaphoreType.DMA((5,)),
        ],
        compiler_params=pltpu.CompilerParams(vmem_limit_bytes=32 * 1024 * 1024),
        cost_estimate=pl.CostEstimate(
            flops=4 * tokens * model_width * rank,
            bytes_accessed=4 * (tokens + rank) * model_width,
            transcendentals=0,
        ),
    )(
        *(
            pltpu.with_memory_space_constraint(x, pltpu.HBM)
            for x in (
                acts_in.reshape(tokens, model_width),
                grads_out.reshape(tokens, model_width),
                jnp.swapaxes(proj_in, 1, 2).reshape(rank, model_width),
                jnp.swapaxes(proj_out, 1, 2).reshape(rank, model_width),
                lengths,
            )
        )
    )
    return lax.optimization_barrier(rows.reshape(1, rank * rank))


def swap(x):
    return lax.ppermute(x, "layer", [(i, i ^ 1) for i in range(lax.axis_size("layer"))])


def fetch_pair(x, pairs, senders):
    count = len(pairs)
    places = [(d, i) for d in range(count) for i in range(count)]
    moves = [(pairs[d][i] * count + senders[d][i], d * count + i) for d, i in places]
    return lax.ppermute(x, ("dp", "layer"), moves)


def to_owner(x, slot):
    count = len(slot)
    moves = [(d * count + i, slot[d][i] * count + d) for d in range(count) for i in range(count)]
    return lax.ppermute(x, ("dp", "layer"), moves)


def slot_kernel(senders, rows, own_block, other_block, out):
    here = lax.axis_index("dp") * len(senders) + lax.axis_index("layer")
    crossed = [d * len(row) + i for d, row in enumerate(senders) for i, sender in enumerate(row) if sender != i]
    is_crossed = functools.reduce(jnp.logical_or, [here == i for i in crossed])
    width = own_block.shape[1]
    kept = width - width // 4
    rest = pl.ds(kept, width - kept)
    end, two = (
        lax.dot_general(left, right, (((1,), (1,)), ((), ())), preferred_element_type=jnp.float32)
        for left, right in ((rows[:, rest], own_block[:, rest]), (rows[...], other_block[...]))
    )
    both = rows[...].astype(jnp.float32)
    row = jnp.where(is_crossed, both[1:], both[:1])
    lanes = 128
    one = jnp.zeros((own_block.shape[0], lanes), jnp.float32)
    for at in range(0, kept, lanes):
        one += own_block[:, pl.ds(at, lanes)].astype(jnp.float32) * row[:, at : at + lanes]
    dots = jnp.where(is_crossed, end[1:] + two[:1], end[:1] + two[1:])
    out[...] = jnp.sum(one.T, axis=0, keepdims=True) + dots


def factor_kernel(scale, margin, label, rows, factor):
    sign = jnp.where(label[0] == 0, 1.0, -1.0)
    factor[...] = sign / ((1.0 + jnp.exp(jnp.full(factor.shape, margin[0], jnp.float32))) * scale)


def shared_scores(own_row, own_block, margin, labels, scale):
    blocks = own_block, swap(own_block)
    rows = jnp.concatenate([own_row, swap(own_row)], axis=0).astype(jnp.bfloat16)
    first, second = fetch_pair(rows, FIRST, FIRST_FROM), fetch_pair(rows, SECOND, SECOND_FROM)
    factor = pl.pallas_call(
        functools.partial(factor_kernel, scale),
        out_shape=jax.ShapeDtypeStruct(own_block.shape[:1], jnp.float32),
        in_specs=[pl.BlockSpec(memory_space=pltpu.SMEM)] * 2 + [pl.BlockSpec(memory_space=pl.ANY)],
        out_specs=pl.BlockSpec(memory_space=pltpu.VMEM),
        compiler_params=pltpu.CompilerParams(vmem_limit_bytes=1024 * 1024),
        cost_estimate=pl.CostEstimate(flops=0, bytes_accessed=4 * own_block.shape[0], transcendentals=0),
    )(margin, labels, rows)

    def score(got, senders):
        return pl.pallas_call(
            functools.partial(slot_kernel, senders),
            out_shape=jax.ShapeDtypeStruct((1, own_block.shape[0]), jnp.float32),
            in_specs=[pl.BlockSpec(memory_space=pltpu.VMEM)] * 3,
            out_specs=pl.BlockSpec(memory_space=pltpu.VMEM),
            compiler_params=pltpu.CompilerParams(vmem_limit_bytes=1024 * 1024),
            cost_estimate=pl.CostEstimate(flops=8 * own_block.size, bytes_accessed=4 * own_block.size, transcendentals=0),
        )(*(pltpu.with_memory_space_constraint(x, pltpu.VMEM) for x in (got, *blocks)))

    first, second = score(first, FIRST_FROM), score(second, SECOND_FROM)
    return (to_owner(first, FIRST) + to_owner(second, SECOND)) * factor[None]


def pair_gradients(acts_in, grads_out, proj_in, proj_out, lengths):
    pair_count, side_count, seq_len, layer_count, _ = acts_in.shape
    in_coords = jnp.einsum("pstld,ldr->pstlr", acts_in, proj_in, preferred_element_type=jnp.float32)
    out_coords = jnp.einsum(
        "pstld,ldr->pstlr", grads_out, proj_out, preferred_element_type=jnp.float32
    )
    position = jnp.arange(seq_len, dtype=jnp.int32)
    live = (position[None, None, :] < lengths[:, :, None]).astype(jnp.float32)
    signs = 1.0 - 2.0 * jnp.arange(side_count, dtype=jnp.float32)
    kron_grads = jnp.einsum("pst,pstlr,pstlk->plrk", live * signs[:, None], out_coords, in_coords)
    return kron_grads.reshape(pair_count, -1).astype(jnp.bfloat16)


def local(acts_in, grads_out, proj_in, proj_out, query_grads, margin, labels, lengths):
    pair_count, side_count, _, layer_count, _ = acts_in.shape
    rank = proj_in.shape[2]
    dp_size, layer_size = lax.axis_size("dp"), lax.axis_size("layer")
    block = query_grads.reshape(query_grads.shape[0], -1)
    one_each = pair_count == layer_count == 1 and side_count == 2
    form = pair_gradient if one_each else pair_gradients
    grad_rows = form(acts_in, grads_out, proj_in, proj_out, lengths)
    scale = rank * math.sqrt(layer_count * layer_size) * math.sqrt(acts_in.shape[2])
    if one_each and dp_size == layer_size == len(FIRST):
        return shared_scores(grad_rows, block, margin, labels, scale)
    factor = jax.nn.sigmoid(-margin) * jnp.where(labels == 0, 1.0, -1.0) / scale
    rows = lax.all_gather(grad_rows.astype(jnp.bfloat16), "dp", axis=0, tiled=True)
    scores = jnp.einsum("pk,qk->pq", rows, block, preferred_element_type=jnp.float32)
    scores = lax.all_to_all(scores, "dp", split_axis=0, concat_axis=1, tiled=True)
    summed = lax.psum_scatter(scores, "layer", scatter_dimension=1, tiled=True)
    return summed * factor[:, None]


def solution(mesh):
    placed = (
        P(("groups", "dp"), None, None, "layer", None),
        P(("groups", "dp"), None, None, "layer", None),
        P("layer", None, None),
        P("layer", None, None),
        P("dp", "layer", None),
        P(("groups", "dp")),
        P(("groups", "dp")),
        P(("groups", "dp"), None),
    )
    return jax.shard_map(
        local, mesh=mesh, in_specs=placed, out_specs=P(("groups", "dp"), "layer"), check_vma=False
    )
```
